32 devices in a mesh: grp: 2 (over y), wide: 4 (over z), red: 2 (over x), tok: 2 (over core).
Axes of the slice: x: 2, y: 2, z: 4, core: 2. Of those that a mesh axis runs over, the one named last changes fastest.
Arguments:
- tokens: bfloat16 [1024, 6144], P(('grp', 'tok'), ('red', 'wide')), parts along dimension 0, may hold values from -6 to 6
- ln_gain: bfloat16 [6144], P(('red', 'wide')), may hold values from 0.099609375 to 1.8984375
- q_gain: float32 [4, 128], P('wide'), may hold values from 0.6 to 3
- k_gain: float32 [4, 128], P('wide'), may hold values from 0.6 to 3
- w_qkv: bfloat16 [6144, 4, 384], P(('red', 'tok'), 'wide'), may hold values from -0.078125 to 0.078125
- w_up: bfloat16 [6144, 24576], P(('red', 'tok'), 'wide'), may hold values from -0.078125 to 0.078125
- w_attn: bfloat16 [4, 128, 6144], P('wide', None, ('red', 'tok')), may hold values from -0.25 to 0.25
- w_down: bfloat16 [24576, 6144], P('wide', ('red', 'tok')), may hold values from -0.0546875 to 0.0546875
Outputs:
- block_out: float32 [1024, 6144], P(('grp', 'tok'), ('red', 'wide')), parts along dimension 0
The draws below stay inside these ranges and needn't reach their ends.
There are 2 independent parts, one for each index of `grp`. The reference program is written for one: setup_inputs(seed, part) draws one part's arguments, and reference() takes and returns one part's arrays. A program takes and returns all parts, laid end to end along the dimension named above; an argument that names none is the same for every part. Nothing has to cross between parts.
All inputs are finite; a program needn't handle non-finite values.
Results may differ from the reference program's by a relative error of at most 0.018.
Values may be sent and summed in bfloat16 or wider, within the bound.
No kernel may reach another device: no remote copies, remote signals or barrier semaphores. Data moves between devices by JAX's collectives and lax.ppermute only.
A program may use at most 192 MiB of HBM per device.

```python
import jax
import jax.numpy as jnp
from jax import lax

D = 6144
FF = 24576
HD = 128
PATCHES = 256
HEADS = 4
IMAGES = 2
TOKENS = 512
N_RED = 2


def draw_q_gain(key, part):
    key = jax.random.fold_in(key, 11)
    return jax.random.uniform(key, (HEADS, HD), jnp.float32, 0.6, 3.0)


def draw_k_gain(key, part):
    key = jax.random.fold_in(key, 23)
    return jax.random.uniform(key, (HEADS, HD), jnp.float32, 0.6, 3.0)


def raised(result, own_key, source, target, parts, factor):
    owner, partner = [(jnp.arange(result.shape[position]) // (result.shape[position] // parts)).reshape([-1 if axis == position else 1 for axis in range(result.ndim)]) for position in (source, target)]
    chosen = jax.random.permutation(own_key, parts)[partner]
    strong = (owner == chosen) | (owner == (partner + parts // 2) % parts)
    return jnp.where(strong, factor * result, result)


def level_of(own_key, extent, split, smallest, top_value):
    loudness = 1.0
    for axis_at, blocks in split:
        steps = jax.random.uniform(jax.random.fold_in(jax.random.fold_in(own_key, 6), axis_at), (blocks,), jnp.float32, smallest / len(split), top_value / len(split))
        loudness = loudness * jnp.repeat(jnp.exp(steps), extent[axis_at] // blocks).reshape((-1,) + (1,) * (len(extent) - 1 - axis_at))
    return loudness


def bell_draw(rng, extent, scale, reach, cuts=(), held_as=jnp.bfloat16):
    entries = jax.random.normal(rng, extent, jnp.float32) * scale
    if len(cuts) > 0:
        entries = level_of(rng, extent, cuts, -0.22, 0.18) * entries
    return jnp.clip(entries, min=-reach, max=reach).astype(held_as)


def gaussian_with(own_key, dims, spread, bound, split, heavy, kind=jnp.bfloat16):
    array = spread * jax.random.normal(own_key, dims, jnp.float32)
    if split:
        array = array * level_of(own_key, dims, split, -0.22, 0.18)
    return jnp.clip(raised(array, jax.random.fold_in(own_key, 3), *heavy), -bound, bound).astype(kind)


def setup_inputs(seed: int = 0, part: int = 0) -> dict:
    seeds = jax.random.split(jax.random.key(seed), 9)
    own_keys = jax.random.split(jax.random.fold_in(seeds[8], part), 9)
    tokens = bell_draw(own_keys[0], (TOKENS, D), 1.0, 6.0, ((0, 2), (1, 8)))
    ln_gain = jnp.clip(1.0 + 0.18 * jax.random.normal(seeds[1], (D,), jnp.float32), 0.099609375, 1.8984375).astype(jnp.bfloat16)
    q_gain = draw_q_gain(jax.random.fold_in(seeds[8], 71), part)
    k_gain = draw_k_gain(jax.random.fold_in(seeds[8], 71), part)
    w_qkv = bell_draw(seeds[4], (D, HEADS, 3 * HD), D ** -0.5, 0.078125, ((0, 4), (1, 4)))
    w_up = bell_draw(seeds[5], (D, FF), D ** -0.5, 0.078125, ((0, 4), (1, 4)))
    w_attn = bell_draw(seeds[6], (HEADS, HD, D), (HEADS * HD) ** -0.5, 0.25, ((0, 4), (2, 4)))
    w_down = gaussian_with(seeds[7], (FF, D), FF ** -0.5, 0.0546875, ((0, 4), (1, 4)), (0, 1, 4, 2.0))
    return dict(tokens=tokens, ln_gain=ln_gain, q_gain=q_gain, k_gain=k_gain, w_qkv=w_qkv, w_up=w_up, w_attn=w_attn, w_down=w_down)


EPS = 1e-06

def layer_norm(values, gain):
    mean = lax.optimization_barrier(jnp.mean(values, axis=-1, keepdims=True))
    meansq = lax.optimization_barrier(jnp.mean(values * values, axis=-1, keepdims=True))
    return (values - mean) * lax.rsqrt(meansq - mean * mean + EPS) * gain.astype(jnp.float32)

def block_sum(normed, weight):
    width = D // N_RED
    total = jnp.zeros((normed.shape[0], weight.shape[1]), jnp.float32)
    for index in range(N_RED):
        partial_sum = jnp.dot(normed[:, index * width:(index + 1) * width], weight[index * width:(index + 1) * width], preferred_element_type=jnp.float32)
        rounded = lax.optimization_barrier(partial_sum.astype(jnp.bfloat16))
        total = total + rounded.astype(jnp.float32)
    return total

def reference(tokens, ln_gain, q_gain, k_gain, w_qkv, w_up, w_attn, w_down):
    floats = tokens.astype(jnp.float32)
    normed = layer_norm(floats, ln_gain).astype(jnp.bfloat16)
    qkv = block_sum(normed, w_qkv.reshape(D, HEADS * 3 * HD))
    qkv = qkv.reshape(TOKENS, HEADS, 3 * HD)
    query = layer_norm(qkv[:, :, :HD], q_gain).astype(jnp.bfloat16)
    key = layer_norm(qkv[:, :, HD:2 * HD], k_gain).astype(jnp.bfloat16)
    value = qkv[:, :, 2 * HD:].astype(jnp.bfloat16)
    up = block_sum(normed, w_up)
    hidden = jax.nn.gelu(up, approximate=False).astype(jnp.bfloat16)
    qf = query.astype(jnp.float32).reshape(IMAGES, PATCHES, HEADS, HD)
    kf = key.astype(jnp.float32).reshape(IMAGES, PATCHES, HEADS, HD)
    vf = value.astype(jnp.float32).reshape(IMAGES, PATCHES, HEADS, HD)
    scores = jnp.einsum('iphd,iqhd->ihpq', qf, kf, precision=lax.Precision.HIGHEST) * HD ** (-0.5)
    peak = lax.optimization_barrier(jnp.max(scores, axis=-1, keepdims=True))
    weights = jnp.exp(scores - peak)
    numer = jnp.einsum('ihpq,iqhd->iphd', weights, vf, precision=lax.Precision.HIGHEST)
    denom = lax.optimization_barrier(jnp.sum(weights, axis=-1))
    attended = (numer / jnp.transpose(denom, (0, 2, 1))[..., None]).astype(jnp.bfloat16)
    attended = attended.reshape(TOKENS, HEADS, HD)
    block = FF // HEADS
    total = floats
    for head in range(HEADS):
        term = jnp.dot(attended[:, head, :], w_attn[head], preferred_element_type=jnp.float32)
        term = term + jnp.dot(hidden[:, head * block:(head + 1) * block], w_down[head * block:(head + 1) * block], preferred_element_type=jnp.float32)
        total = total + term.astype(jnp.bfloat16).astype(jnp.float32)
    return total
```

```python
import jax
import jax.numpy as jnp
from jax import lax
from jax.sharding import PartitionSpec as P

D = 6144
PATCHES = 256
EPS = 1e-06
CHUNKS = 2
PIECES = 2


def normalize(values, mean, meansq, gain):
    return (values - mean) * lax.rsqrt(meansq - mean * mean + EPS) * gain.astype(jnp.float32)


def head_norm(values, gain):
    mean = jnp.mean(values, axis=-1, keepdims=True)
    meansq = jnp.mean(values * values, axis=-1, keepdims=True)
    return normalize(values, mean, meansq, gain)


def attend(qkv, q_gain, k_gain):
    width = q_gain.shape[1]
    query = head_norm(qkv[:, :width], q_gain[0]).astype(jnp.bfloat16)
    key = head_norm(qkv[:, width : 2 * width], k_gain[0]).astype(jnp.bfloat16)
    value = qkv[:, 2 * width :].astype(jnp.bfloat16)
    query, key, value = (a.reshape(-1, PATCHES, width) for a in (query, key, value))
    scores = jnp.einsum("ipd,iqd->ipq", query, key, preferred_element_type=jnp.float32)
    scores = scores * width ** (-0.5)
    weights = jnp.exp(scores - jnp.max(scores, axis=-1, keepdims=True))
    total = jnp.sum(weights, axis=-1, keepdims=True)
    acc = jnp.einsum(
        "ipq,iqd->ipd", weights, value.astype(jnp.float32), precision=lax.Precision.HIGHEST
    )
    return (acc / total).astype(jnp.bfloat16).reshape(-1, width)


def make_body(mesh):
    n_red = mesh.shape["red"]

    def swap(x):
        return lax.ppermute(x, "tok", [(0, 1), (1, 0)])

    def sum_red(x):
        total = x.astype(jnp.float32)
        for shift in range(1, n_red):
            pairs = [(i, (i + shift) % n_red) for i in range(n_red)]
            total = total + lax.ppermute(x, "red", pairs).astype(jnp.float32)
        return total

    def body(tokens, ln_gain, q_gain, k_gain, w_qkv, w_up, w_attn, w_down):
        core = lax.axis_index("tok")
        rows = tokens.shape[0] // CHUNKS
        qkv_rows = w_qkv.reshape(w_qkv.shape[0], w_qkv.shape[1] * w_qkv.shape[2])
        attn_rows = w_attn.reshape(w_attn.shape[0] * w_attn.shape[1], w_attn.shape[2])
        depth = w_up.shape[0]
        piece = w_up.shape[1] // PIECES
        gain = lax.all_gather(ln_gain, "wide", axis=0, tiled=True)

        inputs = []
        ups = []
        for c in range(CHUNKS):
            raw = lax.all_gather(
                tokens[c * rows : (c + 1) * rows], "wide", axis=1, tiled=True
            ).astype(jnp.float32)
            sums = sum_red(jnp.stack([jnp.sum(raw, axis=1), jnp.sum(raw * raw, axis=1)]))
            normed = normalize(raw, sums[0][:, None] / D, sums[1][:, None] / D, gain)
            normed = normed.astype(jnp.bfloat16)
            mine = lax.dynamic_slice_in_dim(normed, core * depth, depth, axis=1)
            theirs = lax.dynamic_slice_in_dim(normed, (1 - core) * depth, depth, axis=1)
            inputs.append(jnp.concatenate([mine, swap(theirs)], axis=0))

        def project(x, weight):
            half = x.shape[0] // 2
            part = jnp.dot(x, weight, preferred_element_type=jnp.float32)
            other = swap(part[half:].astype(jnp.bfloat16)).astype(jnp.float32)
            return sum_red((part[:half] + other).astype(jnp.bfloat16))

        for c in range(CHUNKS):
            ups.append(
                [
                    project(inputs[c], w_up[:, p * piece : (p + 1) * piece])
                    for p in range(PIECES)
                ]
            )
        qkv = jnp.concatenate([project(x, qkv_rows) for x in inputs], axis=0)
        attended = attend(qkv, q_gain, k_gain)
        attended_other = swap(attended)

        outs = []
        for c in range(CHUNKS):
            pick = slice(c * rows, (c + 1) * rows)
            both = jnp.concatenate([attended[pick], attended_other[pick]], axis=0)
            terms = jnp.dot(both, attn_rows, preferred_element_type=jnp.float32)
            for p in range(PIECES):
                hidden = jax.nn.gelu(ups[c][p], approximate=False).astype(jnp.bfloat16)
                both = jnp.concatenate([hidden, swap(hidden)], axis=0)
                terms = terms + jnp.dot(
                    both,
                    w_down[p * piece : (p + 1) * piece],
                    preferred_element_type=jnp.float32,
                )
            terms = terms.astype(jnp.bfloat16)
            kept, got = terms[:rows], swap(terms[rows:])
            lower = jnp.where(core == 0, kept, got)
            upper = jnp.where(core == 0, got, kept)
            summed = lax.psum_scatter(
                jnp.concatenate([lower, upper], axis=1), "wide", scatter_dimension=1, tiled=True
            ).astype(jnp.float32)
            outs.append(tokens[pick].astype(jnp.float32) + summed)
        return jnp.concatenate(outs, axis=0)

    return body


def solution(mesh):
    return jax.shard_map(
        make_body(mesh),
        mesh=mesh,
        in_specs=(
            P(("grp", "tok"), ("red", "wide")),
            P(("red", "wide")),
            P("wide", None),
            P("wide", None),
            P(("red", "tok"), "wide", None),
            P(("red", "tok"), "wide"),
            P("wide", None, ("red", "tok")),
            P("wide", ("red", "tok")),
        ),
        out_specs=P(("grp", "tok"), ("red", "wide")),
        check_vma=False,
    )
```

```python
import jax
import jax.numpy as jnp
from jax import lax
from jax.sharding import PartitionSpec as P

D = 6144
PATCHES = 256
EPS = 1e-06
SHARES = (1, 2, 1)
PIECES = 2


def normalize(values, mean, meansq, gain):
    return (values - mean) * lax.rsqrt(meansq - mean * mean + EPS) * gain.astype(jnp.float32)


def head_norm(values, gain):
    mean = jnp.mean(values, axis=-1, keepdims=True)
    meansq = jnp.mean(values * values, axis=-1, keepdims=True)
    return normalize(values, mean, meansq, gain)


def attend(qkv, q_gain, k_gain):
    width = q_gain.shape[1]
    query = head_norm(qkv[:, :width], q_gain[0]).astype(jnp.bfloat16)
    key = head_norm(qkv[:, width : 2 * width], k_gain[0]).astype(jnp.bfloat16)
    value = qkv[:, 2 * width :].astype(jnp.bfloat16)
    query, key, value = (a.reshape(-1, PATCHES, width) for a in (query, key, value))
    scores = jnp.einsum("ipd,iqd->ipq", query, key, preferred_element_type=jnp.float32)
    scores = scores * width ** (-0.5)
    weights = jnp.exp(scores - jnp.max(scores, axis=-1, keepdims=True))
    total = jnp.sum(weights, axis=-1, keepdims=True)
    acc = jnp.einsum(
        "ipq,iqd->ipd", weights, value.astype(jnp.float32), precision=lax.Precision.HIGHEST
    )
    return (acc / total).astype(jnp.bfloat16).reshape(-1, width)


def after(x, *earlier):
    return lax.optimization_barrier((x, *earlier))[0]


def make_body(mesh):
    n_red, n_wide = mesh.shape["red"], mesh.shape["wide"]
    half_wide = n_wide // 2
    ids = [(wide, core) for wide in range(n_wide) for core in range(2)]

    def swap(x):
        return lax.ppermute(x, "tok", [(0, 1), (1, 0)])

    def sum_red(x):
        total = x.astype(jnp.float32)
        for shift in range(1, n_red):
            pairs = [(i, (i + shift) % n_red) for i in range(n_red)]
            total = total + lax.ppermute(x, "red", pairs).astype(jnp.float32)
        return total

    def sum_holders(x):
        total = x
        n = n_red * 2
        for shift in range(1, n):
            pairs = [(i, (i + shift) % n) for i in range(n)]
            total = total + lax.ppermute(x, ("red", "tok"), pairs)
        return total

    def spread(x):
        got = []
        for k in range(n_wide):
            pairs = []
            for wide, core in ids:
                block = 2 * (wide % half_wide) + core
                target = ((block - k) % n_wide) * 2 + wide // half_wide
                pairs.append((wide * 2 + core, target))
            got.append(lax.ppermute(x, ("wide", "tok"), pairs))
        return jnp.stack(got)

    def collect(pick):
        chip = lax.axis_index("wide")
        total = None
        for k in range(n_wide):
            pairs = []
            for wide, core in ids:
                block = (wide + k) % n_wide
                pairs.append((wide * 2 + core, (core * half_wide + block // 2) * 2 + block % 2))
            got = lax.ppermute(pick((chip + k) % n_wide), ("wide", "tok"), pairs)
            got = got.astype(jnp.float32)
            total = got if total is None else total + got
        return total

    def body(tokens, ln_gain, q_gain, k_gain, w_qkv, w_up, w_attn, w_down):
        core = lax.axis_index("tok")
        chip = lax.axis_index("wide")
        width = tokens.shape[1]
        unit = tokens.shape[0] // sum(SHARES)
        qkv_rows = w_qkv.reshape(w_qkv.shape[0], w_qkv.shape[1] * w_qkv.shape[2])
        attn_rows = w_attn.reshape(w_attn.shape[0] * w_attn.shape[1], w_attn.shape[2])
        piece = w_up.shape[1] // PIECES
        cuts = []
        start = 0
        for share in SHARES:
            cuts.append(slice(start, start + share * unit))
            start += share * unit

        def place(block, image):
            return (2 * block + image - chip) % n_wide

        def take(stack, block, image):
            return lax.dynamic_index_in_dim(stack, place(block, image), 0, keepdims=False)

        raws = [spread(tokens[cut]) for cut in cuts]
        gains = spread(ln_gain)
        gain = jnp.concatenate([take(gains, block, 0) for block in range(half_wide)])

        def normed(raw):
            floats = raw.astype(jnp.float32)
            sums = jnp.stack([jnp.sum(floats, axis=2), jnp.sum(floats * floats, axis=2)], axis=1)
            sums = jnp.stack(
                [
                    sum(take(sums, block, image) for block in range(half_wide))
                    for image in range(2)
                ]
            )
            sums = sum_holders(sums) / D
            groups = []
            for image in (core, 1 - core):
                stat = lax.dynamic_index_in_dim(sums, image, 0, keepdims=False)
                values = jnp.concatenate(
                    [take(raw, block, image) for block in range(half_wide)], axis=1
                ).astype(jnp.float32)
                groups.append(normalize(values, stat[0][:, None], stat[1][:, None], gain))
            return jnp.concatenate(groups, axis=0).astype(jnp.bfloat16)

        def project(x, weight):
            half = x.shape[0] // 2
            part = jnp.dot(x, weight, preferred_element_type=jnp.float32)
            other = swap(part[half:].astype(jnp.bfloat16)).astype(jnp.float32)
            return (part[:half] + other).astype(jnp.bfloat16)

        n = len(cuts)
        inputs = []
        for c in range(n):
            inputs.append(normed(raws[c]))
        sums = [[None] * PIECES for _ in range(n)]
        order = [(c, p) for c in range(n) for p in range(PIECES)]
        done = []
        for at, (c, p) in enumerate(order):
            x = inputs[c] if len(done) < 2 else after(inputs[c], done[-2])
            sums[c][p] = project(x, w_up[:, p * piece : (p + 1) * piece])
            done.append(sums[c][p])
            if at == PIECES:
                pieces = [x[: x.shape[0] // 2] for x in inputs]
                pieces += [x[x.shape[0] // 2 :] for x in inputs]
                qkv = project(after(jnp.concatenate(pieces, axis=0), done[-1]), qkv_rows)
        ups = [[sum_red(s) for s in group] for group in sums]
        attended = attend(sum_red(qkv), q_gain, k_gain)
        attended_other = swap(attended)

        outs = []
        for c, cut in enumerate(cuts):
            rows = cut.stop - cut.start
            both = jnp.concatenate([attended[cut], attended_other[cut]], axis=0)
            terms = jnp.dot(both, attn_rows, preferred_element_type=jnp.float32)
            for p in range(PIECES):
                hidden = jax.nn.gelu(ups[c][p], approximate=False).astype(jnp.bfloat16)
                both = jnp.concatenate([hidden, swap(hidden)], axis=0)
                terms = terms + jnp.dot(
                    both,
                    w_down[p * piece : (p + 1) * piece],
                    preferred_element_type=jnp.float32,
                )
            terms = terms.astype(jnp.bfloat16)

            def pick(block):
                other = (block % 2) ^ core
                return lax.dynamic_slice(
                    terms, (other * rows, (block // 2) * width), (rows, width)
                )

            outs.append(tokens[cut].astype(jnp.float32) + collect(pick))
        return jnp.concatenate(outs, axis=0)

    return body


def solution(mesh):
    return jax.shard_map(
        make_body(mesh),
        mesh=mesh,
        in_specs=(
            P(("grp", "tok"), ("red", "wide")),
            P(("red", "wide")),
            P("wide", None),
            P("wide", None),
            P(("red", "tok"), "wide", None),
            P(("red", "tok"), "wide"),
            P("wide", None, ("red", "tok")),
            P("wide", ("red", "tok")),
        ),
        out_specs=P(("grp", "tok"), ("red", "wide")),
        check_vma=False,
    )
```

```python
import functools
import math

import jax
import jax.numpy as jnp
from jax import lax
from jax.experimental import pallas as pl
from jax.experimental.pallas import tpu as pltpu
from jax.sharding import PartitionSpec as P

D = 6144
PATCHES = 256
EPS = 1e-06
SHARES = (7, 5, 4)
PIECES = (2, 1)
GAIN_ROWS = 8


def normalize(values, mean, meansq, gain):
    return (values - mean) * lax.rsqrt(meansq - mean * mean + EPS) * gain.astype(jnp.float32)


def head_norm(values, gain):
    mean = jnp.mean(values, axis=-1, keepdims=True)
    meansq = jnp.mean(values * values, axis=-1, keepdims=True)
    return normalize(values, mean, meansq, gain)


def attend(qkv, q_gain, k_gain):
    width = q_gain.shape[1]
    query = head_norm(qkv[:, :width], q_gain[0]).astype(jnp.bfloat16)
    key = head_norm(qkv[:, width : 2 * width], k_gain[0]).astype(jnp.bfloat16)
    value = qkv[:, 2 * width :].astype(jnp.bfloat16)
    query, key, value = (a.reshape(-1, PATCHES, width) for a in (query, key, value))
    scores = jnp.einsum("ipd,iqd->ipq", query, key, preferred_element_type=jnp.float32)
    scores = scores * width ** (-0.5)
    weights = jnp.exp(scores - jnp.max(scores, axis=-1, keepdims=True))
    total = jnp.sum(weights, axis=-1, keepdims=True)
    acc = jnp.einsum(
        "ipq,iqd->ipd", weights, value.astype(jnp.float32), precision=lax.Precision.HIGHEST
    )
    return (acc / total).astype(jnp.bfloat16).reshape(-1, width)


def nothing(x):
    corner = x[(0,) * x.ndim].astype(jnp.int32)
    return lax.shift_right_logical(corner & 1, 1).astype(jnp.float32)


def slices(size, shares):
    ends = [sum(shares[: i + 1]) * size // sum(shares) for i in range(len(shares))]
    return [slice(a, b) for a, b in zip([0] + ends[:-1], ends)]


def block_of(size):
    return next(b for b in (512, 384, 256, 128) if size % b == 0)


PARAMS = pltpu.CompilerParams(vmem_limit_bytes=20 * 2**20)
SOON = pl.CostEstimate(flops=0, bytes_accessed=0, transcendentals=0)
WHOLE = pl.BlockSpec(memory_space=pl.ANY)


def project_kernel(n_earlier, own_ref, other_ref, w_ref, *refs):
    near_ref, far_ref, x_ref = refs[n_earlier:]
    rows = own_ref.shape[0]

    @pl.when(pl.program_id(0) == 0)
    def _():
        x_ref[:rows] = own_ref[...]
        x_ref[rows:] = other_ref[...]

    part = jnp.dot(x_ref[...], w_ref[...], preferred_element_type=jnp.float32)
    near_ref[...] = part[:rows]
    far_ref[...] = part[rows:].astype(jnp.bfloat16)


def project_tokens(own, other, weight, piece, earlier):
    rows, depth = own.shape
    columns = piece.stop - piece.start
    block = block_of(math.gcd(columns, piece.start))
    steps, skipped = columns // block, piece.start // block
    whole = pl.BlockSpec((rows, depth), lambda j: (0, 0))
    out = pl.BlockSpec((rows, block), lambda j: (0, j))
    return pl.pallas_call(
        functools.partial(project_kernel, len(earlier)),
        grid=(steps,),
        in_specs=[
            whole,
            whole,
            pl.BlockSpec((depth, block), lambda j: (0, skipped + j)),
        ]
        + [WHOLE] * len(earlier),
        out_specs=[out, out],
        out_shape=[
            jax.ShapeDtypeStruct((rows, columns), jnp.float32),
            jax.ShapeDtypeStruct((rows, columns), jnp.bfloat16),
        ],
        scratch_shapes=[pltpu.VMEM((2 * rows, depth), jnp.bfloat16)],
        compiler_params=PARAMS,
        cost_estimate=SOON,
    )(own, other, weight, *earlier)


def output_kernel(n_added, n_earlier, own_ref, other_ref, w_ref, *refs):
    added = refs[:n_added]
    out_ref, total_ref = refs[n_added + n_earlier :]
    k = pl.program_id(0)
    hidden = jnp.concatenate([own_ref[...], other_ref[...]], axis=0)
    part = jnp.dot(hidden, w_ref[...], preferred_element_type=jnp.float32)

    @pl.when(k == 0)
    def _():
        total_ref[...] = sum([a[...] for a in added], part)

    @pl.when(k > 0)
    def _():
        total_ref[...] += part

    @pl.when(k == pl.num_programs(0) - 1)
    def _():
        out_ref[...] = total_ref[...].astype(out_ref.dtype)


def project_hidden(own, other, weight, piece, added, dtype, earlier):
    rows, units = own.shape
    columns = weight.shape[1]
    block = block_of(math.gcd(units, piece.start))
    steps, skipped = units // block, piece.start // block
    whole = pl.BlockSpec((2 * rows, columns), lambda k: (0, 0))
    part = pl.BlockSpec((rows, block), lambda k: (0, k))
    return pl.pallas_call(
        functools.partial(output_kernel, len(added), len(earlier)),
        grid=(steps,),
        in_specs=[
            part,
            part,
            pl.BlockSpec((block, columns), lambda k: (skipped + k, 0)),
        ]
        + [whole] * len(added)
        + [WHOLE] * len(earlier),
        out_specs=whole,
        out_shape=jax.ShapeDtypeStruct((2 * rows, columns), dtype),
        scratch_shapes=[pltpu.VMEM((2 * rows, columns), jnp.float32)],
        compiler_params=PARAMS,
        cost_estimate=SOON,
    )(own, other, weight, *added, *earlier)


def make_body(mesh):
    n_red, n_wide = mesh.shape["red"], mesh.shape["wide"]

    def swap(x):
        return lax.ppermute(x, "tok", [(0, 1), (1, 0)])

    def sum_red(x):
        total = x.astype(jnp.float32)
        for shift in range(1, n_red):
            pairs = [(i, (i + shift) % n_red) for i in range(n_red)]
            total = total + lax.ppermute(x, "red", pairs).astype(jnp.float32)
        return total

    def collect(x, width):
        chip = lax.axis_index("wide")
        total = lax.dynamic_slice_in_dim(x, chip * width, width, axis=1).astype(jnp.float32)
        for k in range(n_wide - 1, 0, -1):
            sent = lax.dynamic_slice_in_dim(x, (chip ^ k) * width, width, axis=1)
            got = lax.ppermute(sent, "wide", [(i, i ^ k) for i in range(n_wide)])
            total = total + got.astype(jnp.float32)
        return total

    def body(tokens, ln_gain, q_gain, k_gain, w_qkv, w_up, w_attn, w_down):
        core = lax.axis_index("tok")
        width = tokens.shape[1]
        qkv_rows = w_qkv.reshape(w_qkv.shape[0], w_qkv.shape[1] * w_qkv.shape[2])
        attn_rows = w_attn.reshape(w_attn.shape[0] * w_attn.shape[1], w_attn.shape[2])
        depth = w_up.shape[0]
        cuts = slices(tokens.shape[0], SHARES)
        pieces = slices(w_up.shape[1], PIECES)
        first = cuts[0].stop

        gain_rows = jnp.broadcast_to(ln_gain[None], (GAIN_ROWS, width))
        lead = jnp.concatenate([gain_rows, tokens[:first]], axis=0)
        lead = lax.all_gather(lead, "wide", axis=1, tiled=True)
        gain = lead[:1]

        def normed(floats):
            sums = jnp.stack([jnp.sum(floats, axis=1), jnp.sum(floats * floats, axis=1)])
            sums = sum_red(sums)[:, :, None] / D
            values = normalize(floats, sums[0], sums[1], gain).astype(jnp.bfloat16)
            mine = lax.dynamic_slice_in_dim(values, core * depth, depth, axis=1)
            theirs = lax.dynamic_slice_in_dim(values, (1 - core) * depth, depth, axis=1)
            return mine, swap(theirs)

        n = len(cuts)
        pairs = [normed(lead[GAIN_ROWS:].astype(jnp.float32))]
        sums, ups = [], [[] for _ in range(n)]
        qkv = None
        for c in range(n):
            if c == 1:
                rest = tokens[first:] + nothing(sums[-1]).astype(jnp.bfloat16)
                rest = lax.all_gather(rest, "wide", axis=1, tiled=True)
                rest_pair = normed(rest.astype(jnp.float32) + nothing(ups[0][0]))
                for cut in cuts[1:]:
                    part = slice(cut.start - first, cut.stop - first)
                    pairs.append([a[part] for a in rest_pair])
                own, other = (
                    jnp.concatenate([a, b], axis=0) for a, b in zip(pairs[0], rest_pair)
                )
                near, far = project_tokens(own, other, qkv_rows, slice(0, qkv_rows.shape[1]), ())
                qkv = (near + swap(far).astype(jnp.float32)).astype(jnp.bfloat16)
            for piece in pieces:
                near, far = project_tokens(*pairs[c], w_up, piece, sums[-2:-1])
                sums.append((near + swap(far).astype(jnp.float32)).astype(jnp.bfloat16))
                ups[c].append(sum_red(sums[-1]))
        ups[0][1] = ups[0][1] + nothing(sums[-1])
        attended = attend(sum_red(qkv), q_gain, k_gain)
        attended_other = swap(attended)

        outs = []
        for c, cut in enumerate(cuts):
            rows = cut.stop - cut.start
            both = jnp.concatenate([attended[cut], attended_other[cut]], axis=0)
            added = [jnp.dot(both, attn_rows, preferred_element_type=jnp.float32)]
            terms = None
            if c == n - 1 and n > 2:
                ups[c][0] = ups[c][0] + nothing(outs[0])
            for p, piece in enumerate(pieces):
                hidden = jax.nn.gelu(ups[c][p], approximate=False).astype(jnp.bfloat16)
                last = p == len(pieces) - 1
                terms = project_hidden(
                    hidden,
                    swap(hidden),
                    w_down,
                    piece,
                    ([] if terms is None else [terms]) + (added if last else []),
                    jnp.bfloat16 if last else jnp.float32,
                    (),
                )
            kept, got = terms[:rows], swap(terms[rows:])
            lower = jnp.where(core == 0, kept, got)
            upper = jnp.where(core == 0, got, kept)
            terms = jnp.concatenate([lower, upper], axis=1)
            if c < n - 1:
                summed = lax.psum_scatter(terms, "wide", scatter_dimension=1, tiled=True)
                summed = summed.astype(jnp.float32)
            else:
                summed = collect(terms, width)
            outs.append(tokens[cut].astype(jnp.float32) + summed)
        return jnp.concatenate(outs, axis=0)

    return body


def solution(mesh):
    return jax.shard_map(
        make_body(mesh),
        mesh=mesh,
        in_specs=(
            P(("grp", "tok"), ("red", "wide")),
            P(("red", "wide")),
            P("wide", None),
            P("wide", None),
            P(("red", "tok"), "wide", None),
            P(("red", "tok"), "wide"),
            P("wide", None, ("red", "tok")),
            P("wide", ("red", "tok")),
        ),
        out_specs=P(("grp", "tok"), ("red", "wide")),
        check_vma=False,
    )
```

```python
import jax
import jax.numpy as jnp
from jax import lax
from jax.sharding import PartitionSpec as P

D = 6144
PATCHES = 256
EPS = 1e-06
SHARES = (7, 5, 4)
PIECES = (1, 1)
GAIN_ROWS = 8


def normalize(values, mean, meansq, gain):
    return (values - mean) * lax.rsqrt(meansq - mean * mean + EPS) * gain.astype(jnp.float32)


def head_norm(values, gain):
    mean = jnp.mean(values, axis=-1, keepdims=True)
    meansq = jnp.mean(values * values, axis=-1, keepdims=True)
    return normalize(values, mean, meansq, gain)


def attend(qkv, q_gain, k_gain):
    width = q_gain.shape[1]
    query = head_norm(qkv[:, :width], q_gain[0]).astype(jnp.bfloat16)
    key = head_norm(qkv[:, width : 2 * width], k_gain[0]).astype(jnp.bfloat16)
    value = qkv[:, 2 * width :].astype(jnp.bfloat16)
    query, key, value = (a.reshape(-1, PATCHES, width) for a in (query, key, value))
    scores = jnp.einsum("ipd,iqd->ipq", query, key, preferred_element_type=jnp.float32)
    scores = scores * width ** (-0.5)
    weights = jnp.exp(scores - jnp.max(scores, axis=-1, keepdims=True))
    total = jnp.sum(weights, axis=-1, keepdims=True)
    acc = jnp.einsum(
        "ipq,iqd->ipd", weights, value.astype(jnp.float32), precision=lax.Precision.HIGHEST
    )
    return (acc / total).astype(jnp.bfloat16).reshape(-1, width)


def nothing(x):
    corner = x[(0,) * x.ndim].astype(jnp.int32)
    return lax.shift_right_logical(corner & 1, 1).astype(jnp.float32)


def slices(size, shares):
    ends = [sum(shares[: i + 1]) * size // sum(shares) for i in range(len(shares))]
    return [slice(a, b) for a, b in zip([0] + ends[:-1], ends)]


def make_body(mesh):
    n_red, n_wide = mesh.shape["red"], mesh.shape["wide"]

    def swap(x):
        return lax.ppermute(x, "tok", [(0, 1), (1, 0)])

    def sum_red(x):
        total = x.astype(jnp.float32)
        for shift in range(1, n_red):
            pairs = [(i, (i + shift) % n_red) for i in range(n_red)]
            total = total + lax.ppermute(x, "red", pairs).astype(jnp.float32)
        return total

    def collect(x, width):
        chip = lax.axis_index("wide")
        total = lax.dynamic_slice_in_dim(x, chip * width, width, axis=1).astype(jnp.float32)
        for k in range(n_wide - 1, 0, -1):
            sent = lax.dynamic_slice_in_dim(x, (chip ^ k) * width, width, axis=1)
            got = lax.ppermute(sent, "wide", [(i, i ^ k) for i in range(n_wide)])
            total = total + got.astype(jnp.float32)
        return total

    def body(tokens, ln_gain, q_gain, k_gain, w_qkv, w_up, w_attn, w_down):
        core = lax.axis_index("tok")
        width = tokens.shape[1]
        qkv_rows = w_qkv.reshape(w_qkv.shape[0], w_qkv.shape[1] * w_qkv.shape[2])
        attn_rows = w_attn.reshape(w_attn.shape[0] * w_attn.shape[1], w_attn.shape[2])
        depth = w_up.shape[0]
        cuts = slices(tokens.shape[0], SHARES)
        pieces = slices(w_up.shape[1], PIECES)

        gain_rows = jnp.broadcast_to(ln_gain[None], (GAIN_ROWS, width))
        raw = jnp.concatenate([gain_rows, tokens], axis=0)
        raw = lax.all_gather(raw, "wide", axis=1, tiled=True)
        near_ups = lax.optimization_barrier([w_up[:, piece] for piece in pieces])
        floats = raw[GAIN_ROWS:].astype(jnp.float32) + sum(nothing(w) for w in near_ups)

        sums = jnp.stack([jnp.sum(floats, axis=1), jnp.sum(floats * floats, axis=1)])
        sums = sum_red(sums)[:, :, None] / D
        normed = normalize(floats, sums[0], sums[1], raw[:1]).astype(jnp.bfloat16)
        mine = lax.dynamic_slice_in_dim(normed, core * depth, depth, axis=1)
        theirs = lax.dynamic_slice_in_dim(normed, (1 - core) * depth, depth, axis=1)
        theirs = swap(theirs)

        def project(own, other, weight, start=0.0):
            far = jnp.dot(other, weight, preferred_element_type=jnp.float32)
            far = swap(far.astype(jnp.bfloat16))
            near = jnp.dot(own, weight, preferred_element_type=jnp.float32)
            return (near + far.astype(jnp.float32) + start).astype(jnp.bfloat16)

        n = len(cuts)
        qkv = sum_red(project(mine, theirs, qkv_rows))
        attended = attend(qkv, q_gain, k_gain)
        attended_other = swap(attended)
        hidden = []
        sent = None
        for cut in cuts:
            own, other = mine[cut], theirs[cut]
            start = 0.0
            if sent is not None:
                own, other = (a + nothing(sent).astype(jnp.bfloat16) for a in (own, other))
                start = nothing(hidden[-1][0])
            ups = []
            for weight in near_ups:
                sent = project(own, other, weight, start)
                ups.append(sum_red(sent))
            hidden.append([jax.nn.gelu(up, approximate=False).astype(jnp.bfloat16) for up in ups])

        outs = []
        for c, cut in enumerate(cuts):
            rows = cut.stop - cut.start
            both = jnp.concatenate([attended[cut], attended_other[cut]], axis=0)
            terms = jnp.dot(both, attn_rows, preferred_element_type=jnp.float32)
            for units, piece in zip(hidden[c], pieces):
                both = jnp.concatenate([units, swap(units)], axis=0)
                terms = terms + jnp.dot(
                    both, w_down[piece], preferred_element_type=jnp.float32
                )
            terms = terms.astype(jnp.bfloat16)
            kept, got = terms[:rows], swap(terms[rows:])
            lower = jnp.where(core == 0, kept, got)
            upper = jnp.where(core == 0, got, kept)
            terms = jnp.concatenate([lower, upper], axis=1)
            if c < n - 1:
                summed = lax.psum_scatter(terms, "wide", scatter_dimension=1, tiled=True)
                summed = summed.astype(jnp.float32)
                if c == 0 and n > 2:
                    last = hidden[-1][-1]
                    hidden[-1][-1] = last + nothing(summed).astype(jnp.bfloat16)
                hidden[c + 1][0] = hidden[c + 1][0] + nothing(terms).astype(jnp.bfloat16)
            else:
                summed = collect(terms, width)
            outs.append(tokens[cut].astype(jnp.float32) + summed)
        return jnp.concatenate(outs, axis=0)

    return body


def solution(mesh):
    return jax.shard_map(
        make_body(mesh),
        mesh=mesh,
        in_specs=(
            P(("grp", "tok"), ("red", "wide")),
            P(("red", "wide")),
            P("wide", None),
            P("wide", None),
            P(("red", "tok"), "wide", None),
            P(("red", "tok"), "wide"),
            P("wide", None, ("red", "tok")),
            P("wide", ("red", "tok")),
        ),
        out_specs=P(("grp", "tok"), ("red", "wide")),
        check_vma=False,
    )
```

```python
import functools
import math

import jax
import jax.numpy as jnp
from jax import lax
from jax.experimental import pallas as pl
from jax.experimental.pallas import tpu as pltpu
from jax.sharding import PartitionSpec as P

D = 6144
PATCHES = 256
EPS = 1e-06
SHARES = (7, 5, 4)
PIECES = (1, 1)
GAIN_ROWS = 8
BF16, F32 = jnp.bfloat16, jnp.float32
PARAMS = pltpu.CompilerParams(vmem_limit_bytes=44 * 2**20)
SOON = pl.CostEstimate(flops=0, bytes_accessed=0, transcendentals=0)
WHOLE = pl.BlockSpec(memory_space=pl.ANY)


def normalize(values, mean, meansq, gain):
    return (values - mean) * lax.rsqrt(meansq - mean * mean + EPS) * gain.astype(F32)


def head_norm(values, gain):
    mean = jnp.mean(values, axis=-1, keepdims=True)
    meansq = jnp.mean(values * values, axis=-1, keepdims=True)
    return normalize(values, mean, meansq, gain)


def attend(qkv, q_gain, k_gain):
    width = q_gain.shape[1]
    query = head_norm(qkv[:, :width], q_gain[0]).astype(BF16)
    key = head_norm(qkv[:, width : 2 * width], k_gain[0]).astype(BF16)
    value = qkv[:, 2 * width :].astype(BF16)
    query, key, value = (a.reshape(-1, PATCHES, width) for a in (query, key, value))
    scores = jnp.einsum("ipd,iqd->ipq", query, key, preferred_element_type=F32)
    scores = scores * width ** (-0.5)
    weights = jnp.exp(scores - jnp.max(scores, axis=-1, keepdims=True))
    total = jnp.sum(weights, axis=-1, keepdims=True)
    acc = jnp.einsum("ipq,iqd->ipd", weights, value.astype(F32), precision=lax.Precision.HIGHEST)
    return (acc / total).astype(BF16).reshape(-1, width)


def nothing(x):
    corner = x[(0,) * x.ndim].astype(jnp.int32)
    return lax.shift_right_logical(corner & 1, 1).astype(F32)


def slices(size, shares):
    ends = [sum(shares[: i + 1]) * size // sum(shares) for i in range(len(shares))]
    return [slice(a, b) for a, b in zip([0] + ends[:-1], ends)]


def steps_of(piece):
    size = math.gcd(piece.stop - piece.start, piece.start)
    block = next(b for b in (512, 384, 256, 128) if size % b == 0)
    return block, (piece.stop - piece.start) // block, piece.start // block


def call(kernel, earlier, operands, specs, **options):
    def body(*refs):
        n = len(operands)
        kernel(refs[:n], refs[n + len(earlier) :])

    return pl.pallas_call(
        body,
        in_specs=list(specs) + [WHOLE] * len(earlier),
        compiler_params=PARAMS,
        cost_estimate=SOON,
        **options,
    )(*operands, *earlier)


def project_far(other, weight, piece, earlier=()):
    rows, depth = other.shape
    block, steps, skipped = steps_of(piece)

    def kernel(ins, outs):
        part = jnp.dot(ins[0][...], ins[1][...], preferred_element_type=F32)
        outs[0][...] = part.astype(BF16)

    return call(
        kernel,
        earlier,
        (other, weight),
        [
            pl.BlockSpec((rows, depth), lambda j: (0, 0)),
            pl.BlockSpec((depth, block), lambda j: (0, skipped + j)),
        ],
        grid=(steps,),
        out_specs=pl.BlockSpec((rows, block), lambda j: (0, j)),
        out_shape=jax.ShapeDtypeStruct((rows, block * steps), BF16),
    )


def project_near(own, weight, piece, far, cuts, earlier=()):
    rows, depth = own.shape
    block, steps, skipped = steps_of(piece)

    def kernel(ins, outs):
        part = jnp.dot(ins[0][...], ins[1][...], preferred_element_type=F32)
        part = (part + ins[2][...].astype(F32)).astype(BF16)
        for cut, out in zip(cuts, outs):
            out[...] = part[cut]

    heights = [cut.stop - cut.start for cut in cuts]
    return call(
        kernel,
        earlier,
        (own, weight, far),
        [
            pl.BlockSpec((rows, depth), lambda j: (0, 0)),
            pl.BlockSpec((depth, block), lambda j: (0, skipped + j)),
            pl.BlockSpec((rows, block), lambda j: (0, j)),
        ],
        grid=(steps,),
        out_specs=[pl.BlockSpec((height, block), lambda j: (0, j)) for height in heights],
        out_shape=[jax.ShapeDtypeStruct((height, block * steps), BF16) for height in heights],
    )


def gelu_sum(parts, earlier=()):
    rows, units = parts[0].shape
    block, steps, _ = steps_of(slice(0, units))
    spec = pl.BlockSpec((rows, block), lambda j: (0, j))

    def kernel(ins, outs):
        up = ins[0][...].astype(F32)
        for part in ins[1:]:
            up = up + part[...].astype(F32)
        outs[0][...] = (0.5 * up * (1.0 + lax.erf(up * 0.5**0.5))).astype(BF16)

    return call(
        kernel,
        earlier,
        parts,
        [spec] * len(parts),
        grid=(steps,),
        out_specs=spec,
        out_shape=jax.ShapeDtypeStruct((rows, units), BF16),
    )


def project_hidden(own, other, weight, piece, added, attention, last, earlier=()):
    rows = own.shape[0]
    columns = weight.shape[1]
    block, steps, skipped = steps_of(piece)
    whole = pl.BlockSpec((rows, columns), lambda k: (0, 0))
    part = pl.BlockSpec((rows, block), lambda k: (0, k))
    specs = [part, part, pl.BlockSpec((block, columns), lambda k: (skipped + k, 0))]
    specs += [whole] * len(added)
    specs += [pl.BlockSpec(a.shape, lambda k: (0, 0)) for a in attention]

    def kernel(ins, refs):
        outs, totals = refs[:2], refs[2:]
        k = pl.program_id(0)
        both = jnp.concatenate([ins[0][...], ins[1][...]], axis=0)
        product = jnp.dot(both, ins[2][...], preferred_element_type=F32)
        halves = [product[:rows], product[rows:]]

        @pl.when(k == 0)
        def _():
            first = list(halves)
            for at in range(2):
                if added:
                    first[at] = first[at] + ins[3 + at][...]
                if attention:
                    first[at] = first[at] + jnp.dot(
                        ins[-3 + at][...], ins[-1][...], preferred_element_type=F32
                    )
                totals[at][...] = first[at]

        @pl.when(k > 0)
        def _():
            for at in range(2):
                totals[at][...] += halves[at]

        @pl.when(k == steps - 1)
        def _():
            for at in range(2):
                outs[at][...] = totals[at][...].astype(outs[at].dtype)

    return call(
        kernel,
        earlier,
        (own, other, weight, *added, *attention),
        specs,
        grid=(steps,),
        out_specs=[whole] * 2,
        out_shape=[jax.ShapeDtypeStruct((rows, columns), BF16 if last else F32)] * 2,
        scratch_shapes=[pltpu.VMEM((rows, columns), F32)] * 2,
    )


def make_body(mesh):
    n_red, n_wide = mesh.shape["red"], mesh.shape["wide"]
    half_wide = n_wide // 2

    def swap(x):
        return lax.ppermute(x, "tok", [(0, 1), (1, 0)])

    def all_red(x):
        parts = [x]
        for shift in range(1, n_red):
            pairs = [(i, (i + shift) % n_red) for i in range(n_red)]
            parts.append(lax.ppermute(x, "red", pairs))
        return parts

    def sum_red(x):
        return sum(a.astype(F32) for a in all_red(x))

    def collect(kept, got, width):
        core, chip = lax.axis_index("tok"), lax.axis_index("wide")
        terms = jnp.concatenate([kept, got], axis=1)

        def block(at):
            start = ((at // half_wide) ^ core) * half_wide + at % half_wide
            return lax.dynamic_slice_in_dim(terms, start * width, width, axis=1)

        total = block(chip).astype(F32)
        for k in range(n_wide - 1, 0, -1):
            pairs = [(i, i ^ k) for i in range(n_wide)]
            total = total + lax.ppermute(block(chip ^ k), "wide", pairs).astype(F32)
        return total

    def body(tokens, ln_gain, q_gain, k_gain, w_qkv, w_up, w_attn, w_down):
        core = lax.axis_index("tok")
        width = tokens.shape[1]
        qkv_rows = w_qkv.reshape(w_qkv.shape[0], w_qkv.shape[1] * w_qkv.shape[2])
        attn_rows = w_attn.reshape(w_attn.shape[0] * w_attn.shape[1], w_attn.shape[2])
        depth, units = w_up.shape
        cuts = slices(tokens.shape[0], SHARES)
        pieces = slices(units, PIECES)
        n = len(cuts)

        gain_rows = jnp.broadcast_to(ln_gain[None], (GAIN_ROWS, width))
        raw = jnp.concatenate([gain_rows, tokens], axis=0)
        raw = lax.all_gather(raw, "wide", axis=1, tiled=True)
        floats = raw[GAIN_ROWS:].astype(F32)
        sums = jnp.stack([jnp.sum(floats, axis=1), jnp.sum(floats * floats, axis=1)])
        sums = sum_red(sums)[:, :, None] / D
        normed = normalize(floats, sums[0], sums[1], raw[:1]).astype(BF16)
        own = lax.dynamic_slice_in_dim(normed, core * depth, depth, axis=1)
        other = lax.dynamic_slice_in_dim(normed, (1 - core) * depth, depth, axis=1)
        other = swap(other)

        every = slice(0, qkv_rows.shape[1])
        far_qkv = project_far(other, qkv_rows, every)
        fars, earlier = [], far_qkv
        for piece in pieces:
            fars.append(project_far(other, w_up, piece, [earlier]))
            earlier = fars[-1]
        (qkv,) = project_near(
            own, qkv_rows, every, swap(far_qkv), [slice(0, tokens.shape[0])], [earlier]
        )
        earlier = qkv
        sums = []
        for piece, far in zip(pieces, fars):
            sums.append(project_near(own, w_up, piece, swap(far), cuts, [earlier]))
            earlier = sums[-1][-1]

        order = [(c, p) for c in range(n) for p in range(len(pieces))]
        outs, scattered = [], []
        terms, waiting = (), None
        earlier = [earlier]

        def output(at, have, terms, earlier):
            c, p = order[at]
            attention = (attended[cuts[c]], attended_other[cuts[c]], attn_rows)
            return project_hidden(
                have,
                swap(have),
                w_down,
                pieces[p],
                terms if p else (),
                () if p else attention,
                p == len(pieces) - 1,
                earlier,
            )

        def scatter(kept, got):
            lower = jnp.where(core == 0, kept, got)
            upper = jnp.where(core == 0, got, kept)
            full = jnp.concatenate([lower, upper], axis=1)
            scattered.append(lax.psum_scatter(full, "wide", scatter_dimension=1, tiled=True))
            return full

        hidden = None
        for at, (c, p) in enumerate(order):
            arrived = gelu_sum(all_red(sums[p][c]), earlier)
            earlier = [arrived]
            if at == 0:
                attended = attend(sum_red(qkv) + nothing(arrived), q_gain, k_gain)
                attended_other = swap(attended)
                earlier = [attended]
            if waiting is not None:
                earlier.append(scatter(*waiting))
                waiting = None
            if at:
                terms = output(at - 1, hidden, terms, earlier)
                earlier = [terms[0]]
                if p == 0:
                    waiting = (terms[0], swap(terms[1]))
            hidden = arrived
        if waiting is not None:
            earlier.append(scatter(*waiting))
        terms = output(len(order) - 1, hidden, terms, earlier + scattered[:1])
        for cut, summed in zip(cuts, scattered):
            outs.append(tokens[cut].astype(F32) + summed.astype(F32))
        outs.append(tokens[cuts[-1]].astype(F32) + collect(terms[0], swap(terms[1]), width))
        return jnp.concatenate(outs, axis=0)

    return body


def solution(mesh):
    return jax.shard_map(
        make_body(mesh),
        mesh=mesh,
        in_specs=(
            P(("grp", "tok"), ("red", "wide")),
            P(("red", "wide")),
            P("wide", None),
            P("wide", None),
            P(("red", "tok"), "wide", None),
            P(("red", "tok"), "wide"),
            P("wide", None, ("red", "tok")),
            P("wide", ("red", "tok")),
        ),
        out_specs=P(("grp", "tok"), ("red", "wide")),
        check_vma=False,
    )
```

```python
import functools
import math

import jax
import jax.numpy as jnp
from jax import lax
from jax.experimental import pallas as pl
from jax.experimental.pallas import tpu as pltpu
from jax.sharding import PartitionSpec as P

D = 6144
PATCHES = 256
EPS = 1e-06
SHARES = (7, 5, 4)
PIECES = (1, 1)
PARTS = 4
BF16, F32 = jnp.bfloat16, jnp.float32
PARAMS = pltpu.CompilerParams(vmem_limit_bytes=44 * 2**20)
SOON = pl.CostEstimate(flops=0, bytes_accessed=0, transcendentals=0)
WHOLE = pl.BlockSpec(memory_space=pl.ANY)


def normalize(values, mean, meansq, gain):
    return (values - mean) * lax.rsqrt(meansq - mean * mean + EPS) * gain.astype(F32)


def head_norm(values, gain):
    mean = jnp.mean(values, axis=-1, keepdims=True)
    meansq = jnp.mean(values * values, axis=-1, keepdims=True)
    return normalize(values, mean, meansq, gain)


def attend(qkv, q_gain, k_gain):
    width = q_gain.shape[1]
    query = head_norm(qkv[:, :width], q_gain[0]).astype(BF16)
    key = head_norm(qkv[:, width : 2 * width], k_gain[0]).astype(BF16)
    value = qkv[:, 2 * width :].astype(BF16)
    query, key, value = (a.reshape(-1, PATCHES, width) for a in (query, key, value))
    scores = jnp.einsum("ipd,iqd->ipq", query, key, preferred_element_type=F32)
    scores = scores * width ** (-0.5)
    weights = jnp.exp(scores - jnp.max(scores, axis=-1, keepdims=True))
    total = jnp.sum(weights, axis=-1, keepdims=True)
    acc = jnp.einsum("ipq,iqd->ipd", weights, value.astype(F32), precision=lax.Precision.HIGHEST)
    return (acc / total).astype(BF16).reshape(-1, width)


def nothing(x):
    corner = x[(0,) * x.ndim].astype(jnp.int32)
    return lax.shift_right_logical(corner & 1, 1).astype(F32)


def slices(size, shares):
    ends = [sum(shares[: i + 1]) * size // sum(shares) for i in range(len(shares))]
    return [slice(a, b) for a, b in zip([0] + ends[:-1], ends)]


def steps_of(piece, blocks=(512, 384, 256, 128)):
    size = math.gcd(piece.stop - piece.start, piece.start)
    block = next(b for b in blocks if size % b == 0)
    return block, (piece.stop - piece.start) // block, piece.start // block


def row_parts(block, columns, index):
    return [
        pl.BlockSpec(
            (block // PARTS, columns),
            lambda j, part=part: (PARTS * index(j)[0] + part, index(j)[1]),
        )
        for part in range(PARTS)
    ]


def dot_parts(x, weights):
    depth = x.shape[1] // PARTS
    return sum(
        jnp.dot(x[:, at * depth : (at + 1) * depth], w[...], preferred_element_type=F32)
        for at, w in enumerate(weights)
    )


def call(kernel, earlier, operands, specs, **options):
    def body(*refs):
        n = len(operands)
        kernel(refs[:n], refs[n + len(earlier) :])

    return pl.pallas_call(
        body,
        in_specs=list(specs) + [WHOLE] * len(earlier),
        compiler_params=PARAMS,
        cost_estimate=SOON,
        **options,
    )(*operands, *earlier)


def project_far(other, weight, piece, earlier=()):
    rows, depth = other.shape
    block, steps, skipped = steps_of(piece)

    def kernel(ins, outs):
        outs[0][...] = dot_parts(ins[0][...], ins[1:]).astype(BF16)

    return call(
        kernel,
        earlier,
        (other, *[weight] * PARTS),
        [pl.BlockSpec((rows, depth), lambda j: (0, 0))]
        + row_parts(depth, block, lambda j: (0, skipped + j)),
        grid=(steps,),
        out_specs=pl.BlockSpec((rows, block), lambda j: (0, j)),
        out_shape=jax.ShapeDtypeStruct((rows, block * steps), BF16),
    )


def project_near(own, weight, piece, far, cuts, earlier=()):
    rows, depth = own.shape
    block, steps, skipped = steps_of(piece)

    def kernel(ins, outs):
        part = dot_parts(ins[0][...], ins[2:])
        part = (part + ins[1][...].astype(F32)).astype(BF16)
        for cut, out in zip(cuts, outs):
            out[...] = part[cut]

    heights = [cut.stop - cut.start for cut in cuts]
    return call(
        kernel,
        earlier,
        (own, far, *[weight] * PARTS),
        [
            pl.BlockSpec((rows, depth), lambda j: (0, 0)),
            pl.BlockSpec((rows, block), lambda j: (0, j)),
        ]
        + row_parts(depth, block, lambda j: (0, skipped + j)),
        grid=(steps,),
        out_specs=[pl.BlockSpec((height, block), lambda j: (0, j)) for height in heights],
        out_shape=[jax.ShapeDtypeStruct((height, block * steps), BF16) for height in heights],
    )


def gelu_sum(parts, earlier=()):
    rows, units = parts[0].shape
    block, steps, _ = steps_of(slice(0, units))
    spec = pl.BlockSpec((rows, block), lambda j: (0, j))

    def kernel(ins, outs):
        up = ins[0][...].astype(F32)
        for part in ins[1:]:
            up = up + part[...].astype(F32)
        outs[0][...] = (0.5 * up * (1.0 + lax.erf(up * 0.5**0.5))).astype(BF16)

    return call(
        kernel,
        earlier,
        parts,
        [spec] * len(parts),
        grid=(steps,),
        out_specs=spec,
        out_shape=jax.ShapeDtypeStruct((rows, units), BF16),
    )


def project_hidden(own, other, weight, piece, added, attention, last, earlier=()):
    rows = own.shape[0]
    columns = weight.shape[1]
    block, steps, skipped = steps_of(piece, (1024, 768, 512, 384, 256, 128))
    whole = pl.BlockSpec((rows, columns), lambda k: (0, 0))
    part = pl.BlockSpec((rows, block), lambda k: (0, k))
    specs = [part, part, *row_parts(block, columns, lambda k: (skipped + k, 0))]
    specs += [whole] * len(added)
    specs += [pl.BlockSpec(a.shape, lambda k: (0, 0)) for a in attention]

    def kernel(ins, refs):
        outs, totals = refs[:2], refs[2:]
        k = pl.program_id(0)
        both = jnp.concatenate([ins[0][...], ins[1][...]], axis=0)
        product = dot_parts(both, ins[2 : 2 + PARTS])
        halves = [product[:rows], product[rows:]]

        @pl.when(k == 0)
        def _():
            first = list(halves)
            for at in range(2):
                if added:
                    first[at] = first[at] + ins[2 + PARTS + at][...]
                if attention:
                    first[at] = first[at] + jnp.dot(
                        ins[-3 + at][...], ins[-1][...], preferred_element_type=F32
                    )
                totals[at][...] = first[at]

        @pl.when(k > 0)
        def _():
            for at in range(2):
                totals[at][...] += halves[at]

        @pl.when(k == steps - 1)
        def _():
            for at in range(2):
                outs[at][...] = totals[at][...].astype(outs[at].dtype)

    return call(
        kernel,
        earlier,
        (own, other, *[weight] * PARTS, *added, *attention),
        specs,
        grid=(steps,),
        out_specs=[whole] * 2,
        out_shape=[jax.ShapeDtypeStruct((rows, columns), BF16 if last else F32)] * 2,
        scratch_shapes=[pltpu.VMEM((rows, columns), F32)] * 2,
    )


def make_body(mesh):
    n_red, n_wide = mesh.shape["red"], mesh.shape["wide"]
    half_wide = n_wide // 2

    def swap(x):
        return lax.ppermute(x, "tok", [(0, 1), (1, 0)])

    def all_red(x):
        parts = [x]
        for shift in range(1, n_red):
            pairs = [(i, (i + shift) % n_red) for i in range(n_red)]
            parts.append(lax.ppermute(x, "red", pairs))
        return parts

    def sum_red(x):
        return sum(a.astype(F32) for a in all_red(x))

    def collect(kept, got, width):
        core, chip = lax.axis_index("tok"), lax.axis_index("wide")
        terms = jnp.concatenate([kept, got], axis=1)

        def block(at):
            start = ((at // half_wide) ^ core) * half_wide + at % half_wide
            return lax.dynamic_slice_in_dim(terms, start * width, width, axis=1)

        total = block(chip).astype(F32)
        for k in range(n_wide - 1, 0, -1):
            pairs = [(i, i ^ k) for i in range(n_wide)]
            total = total + lax.ppermute(block(chip ^ k), "wide", pairs).astype(F32)
        return total

    def body(tokens, ln_gain, q_gain, k_gain, w_qkv, w_up, w_attn, w_down):
        core = lax.axis_index("tok")
        width = tokens.shape[1]
        qkv_rows = w_qkv.reshape(w_qkv.shape[0], w_qkv.shape[1] * w_qkv.shape[2])
        attn_rows = w_attn.reshape(w_attn.shape[0] * w_attn.shape[1], w_attn.shape[2])
        depth, units = w_up.shape
        cuts = slices(tokens.shape[0], SHARES)
        pieces = slices(units, PIECES)
        n = len(cuts)

        raw = lax.all_gather(tokens, "wide", axis=1, tiled=True)
        gain = lax.all_gather(ln_gain, "wide", axis=0, tiled=True)
        floats = tokens.astype(F32)
        sums = jnp.stack([jnp.sum(floats, axis=1), jnp.sum(floats * floats, axis=1)])
        sums = lax.psum(sums, ("wide", "red"))[:, :, None] / D
        normed = normalize(raw.astype(F32), sums[0], sums[1], gain).astype(BF16)
        own = lax.dynamic_slice_in_dim(normed, core * depth, depth, axis=1)
        other = lax.dynamic_slice_in_dim(normed, (1 - core) * depth, depth, axis=1)
        other = swap(other)

        every = slice(0, qkv_rows.shape[1])
        far_qkv = project_far(other, qkv_rows, every)
        fars, earlier = [], far_qkv
        for piece in pieces:
            fars.append(project_far(other, w_up, piece, [earlier]))
            earlier = fars[-1]
        (qkv,) = project_near(
            own, qkv_rows, every, swap(far_qkv), [slice(0, tokens.shape[0])], [earlier]
        )
        earlier = qkv
        sums = []
        for piece, far in zip(pieces, fars):
            sums.append(project_near(own, w_up, piece, swap(far), cuts, [earlier]))
            earlier = sums[-1][-1]

        order = [(c, p) for c in range(n) for p in range(len(pieces))]
        outs, scattered = [], []
        terms, waiting = (), None
        earlier = [earlier]

        def output(at, have, terms, earlier):
            c, p = order[at]
            attention = (attended[cuts[c]], attended_other[cuts[c]], attn_rows)
            return project_hidden(
                have,
                swap(have),
                w_down,
                pieces[p],
                terms if p else (),
                () if p else attention,
                p == len(pieces) - 1,
                earlier,
            )

        def scatter(kept, got):
            lower = jnp.where(core == 0, kept, got)
            upper = jnp.where(core == 0, got, kept)
            full = jnp.concatenate([lower, upper], axis=1)
            scattered.append(lax.psum_scatter(full, "wide", scatter_dimension=1, tiled=True))
            return full

        hidden = None
        for at, (c, p) in enumerate(order):
            arrived = gelu_sum(all_red(sums[p][c]), earlier)
            earlier = [arrived]
            if at == 0:
                attended = attend(sum_red(qkv) + nothing(arrived), q_gain, k_gain)
                attended_other = swap(attended)
                earlier = [attended]
            if waiting is not None:
                earlier.append(scatter(*waiting))
                waiting = None
            if at:
                terms = output(at - 1, hidden, terms, earlier)
                earlier = [terms[0]]
                if p == 0:
                    waiting = (terms[0], swap(terms[1]))
            hidden = arrived
        if waiting is not None:
            earlier.append(scatter(*waiting))
        terms = output(len(order) - 1, hidden, terms, earlier + scattered[:1])
        for cut, summed in zip(cuts, scattered):
            outs.append(tokens[cut].astype(F32) + summed.astype(F32))
        outs.append(tokens[cuts[-1]].astype(F32) + collect(terms[0], swap(terms[1]), width))
        return jnp.concatenate(outs, axis=0)

    return body


def solution(mesh):
    return jax.shard_map(
        make_body(mesh),
        mesh=mesh,
        in_specs=(
            P(("grp", "tok"), ("red", "wide")),
            P(("red", "wide")),
            P("wide", None),
            P("wide", None),
            P(("red", "tok"), "wide", None),
            P(("red", "tok"), "wide"),
            P("wide", None, ("red", "tok")),
            P("wide", ("red", "tok")),
        ),
        out_specs=P(("grp", "tok"), ("red", "wide")),
        check_vma=False,
    )
```

```python
import functools
import math

import jax
import jax.numpy as jnp
from jax import lax
from jax.experimental import pallas as pl
from jax.experimental.pallas import tpu as pltpu
from jax.sharding import PartitionSpec as P

D = 6144
PATCHES = 256
EPS = 1e-06
SHARES = (7, 5, 4)
PIECES = (1, 1)
PARTS = 4
BF16, F32 = jnp.bfloat16, jnp.float32
PARAMS = pltpu.CompilerParams(vmem_limit_bytes=32 * 2**20)
SOON = pl.CostEstimate(flops=0, bytes_accessed=0, transcendentals=0)


def normalize(values, mean, meansq, gain):
    return (values - mean) * lax.rsqrt(meansq - mean * mean + EPS) * gain.astype(F32)


def head_norm(values, gain):
    mean = jnp.mean(values, axis=-1, keepdims=True)
    meansq = jnp.mean(values * values, axis=-1, keepdims=True)
    return normalize(values, mean, meansq, gain)


def attend(qkv, q_gain, k_gain):
    width = q_gain.shape[1]
    query = head_norm(qkv[:, :width], q_gain[0]).astype(BF16)
    key = head_norm(qkv[:, width : 2 * width], k_gain[0]).astype(BF16)
    value = qkv[:, 2 * width :].astype(BF16)
    query, key, value = (a.reshape(-1, PATCHES, width) for a in (query, key, value))
    scores = jnp.einsum("ipd,iqd->ipq", query, key, preferred_element_type=F32)
    scores = scores * width ** (-0.5)
    weights = jnp.exp(scores - jnp.max(scores, axis=-1, keepdims=True))
    total = jnp.sum(weights, axis=-1, keepdims=True)
    acc = jnp.einsum("ipq,iqd->ipd", weights, value.astype(F32), precision=lax.Precision.HIGHEST)
    return (acc / total).astype(BF16).reshape(-1, width)


def nothing(x):
    corner = x[(0,) * x.ndim].astype(jnp.int32)
    return lax.shift_right_logical(corner & 1, 1).astype(F32)


def slices(size, shares):
    ends = [sum(shares[: i + 1]) * size // sum(shares) for i in range(len(shares))]
    return [slice(a, b) for a, b in zip([0] + ends[:-1], ends)]


def steps_of(piece, blocks=(512, 384, 256, 128)):
    size = math.gcd(piece.stop - piece.start, piece.start)
    block = next(b for b in blocks if size % b == 0)
    return block, (piece.stop - piece.start) // block, piece.start // block


def row_parts(block, columns, index):
    return [
        pl.BlockSpec(
            (block // PARTS, columns),
            lambda j, part=part: (PARTS * index(j)[0] + part, index(j)[1]),
        )
        for part in range(PARTS)
    ]


def dot_parts(x, weights):
    depth = x.shape[1] // PARTS
    return sum(
        jnp.dot(x[:, at * depth : (at + 1) * depth], w[...], preferred_element_type=F32)
        for at, w in enumerate(weights)
    )


def corner_of(x):
    shape = (min(16, x.shape[0]), min(128, x.shape[1]))
    return pl.BlockSpec(shape, lambda *_: (0, 0))


def call(kernel, earlier, operands, specs, **options):
    def body(*refs):
        n = len(operands)
        kernel(refs[:n], refs[n + len(earlier) :])

    return pl.pallas_call(
        body,
        in_specs=list(specs) + [corner_of(a) for a in earlier],
        compiler_params=PARAMS,
        cost_estimate=SOON,
        **options,
    )(*operands, *earlier)


def gelu_sum(parts, earlier=()):
    rows, units = parts[0].shape
    block, steps, _ = steps_of(slice(0, units))
    spec = pl.BlockSpec((rows, block), lambda j: (0, j))

    def kernel(ins, outs):
        up = ins[0][...].astype(F32)
        for part in ins[1:]:
            up = up + part[...].astype(F32)
        outs[0][...] = (0.5 * up * (1.0 + lax.erf(up * 0.5**0.5))).astype(BF16)

    return call(
        kernel,
        earlier,
        parts,
        [spec] * len(parts),
        grid=(steps,),
        out_specs=spec,
        out_shape=jax.ShapeDtypeStruct((rows, units), BF16),
    )


def project_hidden(own, other, weight, piece, added, attention, last, earlier=()):
    rows = own.shape[0]
    columns = weight.shape[1]
    block, steps, skipped = steps_of(piece, (1024, 768, 512, 384, 256, 128))
    whole = pl.BlockSpec((rows, columns), lambda k: (0, 0))
    part = pl.BlockSpec((rows, block), lambda k: (0, k))
    specs = [part, part, *row_parts(block, columns, lambda k: (skipped + k, 0))]
    specs += [whole] * len(added)
    specs += [pl.BlockSpec(a.shape, lambda k: (0, 0)) for a in attention]

    def kernel(ins, refs):
        outs, totals = refs[:2], refs[2:]
        k = pl.program_id(0)
        both = jnp.concatenate([ins[0][...], ins[1][...]], axis=0)
        product = dot_parts(both, ins[2 : 2 + PARTS])
        halves = [product[:rows], product[rows:]]

        @pl.when(k == 0)
        def _():
            first = list(halves)
            for at in range(2):
                if added:
                    first[at] = first[at] + ins[2 + PARTS + at][...]
                if attention:
                    first[at] = first[at] + jnp.dot(
                        ins[-3 + at][...], ins[-1][...], preferred_element_type=F32
                    )
                totals[at][...] = first[at]

        @pl.when(k > 0)
        def _():
            for at in range(2):
                totals[at][...] += halves[at]

        @pl.when(k == steps - 1)
        def _():
            for at in range(2):
                outs[at][...] = totals[at][...].astype(outs[at].dtype)

    return call(
        kernel,
        earlier,
        (own, other, *[weight] * PARTS, *added, *attention),
        specs,
        grid=(steps,),
        out_specs=[whole] * 2,
        out_shape=[jax.ShapeDtypeStruct((rows, columns), BF16 if last else F32)] * 2,
        scratch_shapes=[pltpu.VMEM((rows, columns), F32)] * 2,
    )


def make_body(mesh):
    n_red, n_wide = mesh.shape["red"], mesh.shape["wide"]
    half_wide = n_wide // 2

    def swap(x):
        return lax.ppermute(x, "tok", [(0, 1), (1, 0)])

    def all_red(x):
        parts = [x]
        for shift in range(1, n_red):
            pairs = [(i, (i + shift) % n_red) for i in range(n_red)]
            parts.append(lax.ppermute(x, "red", pairs))
        return parts

    def sum_red(x):
        return sum(a.astype(F32) for a in all_red(x))

    def collect(kept, got, width):
        core, chip = lax.axis_index("tok"), lax.axis_index("wide")
        terms = jnp.concatenate([kept, got], axis=1)

        def block(at):
            start = ((at // half_wide) ^ core) * half_wide + at % half_wide
            return lax.dynamic_slice_in_dim(terms, start * width, width, axis=1)

        total = block(chip).astype(F32)
        for k in range(n_wide - 1, 0, -1):
            pairs = [(i, i ^ k) for i in range(n_wide)]
            total = total + lax.ppermute(block(chip ^ k), "wide", pairs).astype(F32)
        return total

    def body(tokens, ln_gain, q_gain, k_gain, w_qkv, w_up, w_attn, w_down):
        core = lax.axis_index("tok")
        width = tokens.shape[1]
        qkv_rows = w_qkv.reshape(w_qkv.shape[0], w_qkv.shape[1] * w_qkv.shape[2])
        attn_rows = w_attn.reshape(w_attn.shape[0] * w_attn.shape[1], w_attn.shape[2])
        depth, units = w_up.shape
        cuts = slices(tokens.shape[0], SHARES)
        pieces = slices(units, PIECES)
        n = len(cuts)

        raw = lax.all_gather(tokens, "wide", axis=1, tiled=True)
        gain = lax.all_gather(ln_gain, "wide", axis=0, tiled=True)
        floats = tokens.astype(F32)
        sums = jnp.stack([jnp.sum(floats, axis=1), jnp.sum(floats * floats, axis=1)])
        sums = lax.psum(sums, ("wide", "red"))[:, :, None] / D
        normed = normalize(raw.astype(F32), sums[0], sums[1], gain).astype(BF16)
        own = lax.dynamic_slice_in_dim(normed, core * depth, depth, axis=1)
        other = lax.dynamic_slice_in_dim(normed, (1 - core) * depth, depth, axis=1)
        other = swap(other)

        both = jnp.concatenate([own, other], axis=0)
        rows = tokens.shape[0]

        def project(weight):
            part = jnp.dot(both, weight, preferred_element_type=F32).astype(BF16)
            return part[:rows], swap(part[rows:])

        def block_sum(parts, start=0.0):
            return (parts[0].astype(F32) + parts[1].astype(F32) + start).astype(BF16)

        halves = [project(w_up[:, piece]) for piece in pieces]
        qkv = block_sum(project(qkv_rows))

        order = [(c, p) for c in range(n) for p in range(len(pieces))]
        outs, scattered = [], []
        terms, waiting, firsts = (), None, []
        earlier = ()

        def output(at, have, terms, earlier):
            c, p = order[at]
            attention = (attended[cuts[c]], attended_other[cuts[c]], attn_rows)
            return project_hidden(
                have,
                swap(have),
                w_down,
                pieces[p],
                terms if p else (),
                () if p else attention,
                p == len(pieces) - 1,
                earlier,
            )

        def scatter(kept, got):
            lower = jnp.where(core == 0, kept, got)
            upper = jnp.where(core == 0, got, kept)
            full = jnp.concatenate([lower, upper], axis=1)
            scattered.append(lax.psum_scatter(full, "wide", scatter_dimension=1, tiled=True))
            return full

        hidden = None
        for at, (c, p) in enumerate(order):
            start = nothing(firsts[c - 1]) if c else 0.0
            parts = all_red(block_sum([a[cuts[c]] for a in halves[p]], start))
            arrived = gelu_sum(parts, earlier)
            earlier = [arrived]
            if p == 0:
                firsts.append(arrived)
            if at == 0:
                attended = attend(sum_red(qkv) + nothing(arrived), q_gain, k_gain)
                attended_other = swap(attended)
                earlier = [attended]
            if waiting is not None:
                earlier.append(scatter(*waiting))
                waiting = None
            if at == len(order) - 1:
                earlier += scattered[:1]
            if at:
                terms = output(at - 1, hidden, terms, earlier)
                earlier = [terms[0]]
                if p == 0:
                    waiting = (terms[0], swap(terms[1]))
            hidden = arrived
        if waiting is not None:
            earlier.append(scatter(*waiting))
        terms = output(len(order) - 1, hidden, terms, earlier)
        for cut, summed in zip(cuts, scattered):
            outs.append(tokens[cut].astype(F32) + summed.astype(F32))
        outs.append(tokens[cuts[-1]].astype(F32) + collect(terms[0], swap(terms[1]), width))
        return jnp.concatenate(outs, axis=0)

    return body


def solution(mesh):
    return jax.shard_map(
        make_body(mesh),
        mesh=mesh,
        in_specs=(
            P(("grp", "tok"), ("red", "wide")),
            P(("red", "wide")),
            P("wide", None),
            P("wide", None),
            P(("red", "tok"), "wide", None),
            P(("red", "tok"), "wide"),
            P("wide", None, ("red", "tok")),
            P("wide", ("red", "tok")),
        ),
        out_specs=P(("grp", "tok"), ("red", "wide")),
        check_vma=False,
    )
```

```python
import functools
import math

import jax
import jax.numpy as jnp
from jax import lax
from jax.experimental import pallas as pl
from jax.experimental.pallas import tpu as pltpu
from jax.sharding import PartitionSpec as P

D = 6144
PATCHES = 256
EPS = 1e-06
SHARES = (7, 5, 4)
PIECES = (1, 1)
AHEAD = 4
BF16, F32 = jnp.bfloat16, jnp.float32
PARAMS = pltpu.CompilerParams(vmem_limit_bytes=48 * 2**20)
SOON = pl.CostEstimate(flops=0, bytes_accessed=0, transcendentals=0)


def normalize(values, mean, meansq, gain):
    return (values - mean) * lax.rsqrt(meansq - mean * mean + EPS) * gain.astype(F32)


def head_norm(values, gain):
    mean = jnp.mean(values, axis=-1, keepdims=True)
    meansq = jnp.mean(values * values, axis=-1, keepdims=True)
    return normalize(values, mean, meansq, gain)


def attend(qkv, q_gain, k_gain):
    width = q_gain.shape[1]
    query = head_norm(qkv[:, :width], q_gain[0]).astype(BF16)
    key = head_norm(qkv[:, width : 2 * width], k_gain[0]).astype(BF16)
    value = qkv[:, 2 * width :].astype(BF16)
    query, key, value = (a.reshape(-1, PATCHES, width) for a in (query, key, value))
    scores = jnp.einsum("ipd,iqd->ipq", query, key, preferred_element_type=F32)
    scores = scores * width ** (-0.5)
    weights = jnp.exp(scores - jnp.max(scores, axis=-1, keepdims=True))
    total = jnp.sum(weights, axis=-1, keepdims=True)
    acc = jnp.einsum("ipq,iqd->ipd", weights, value.astype(F32), precision=lax.Precision.HIGHEST)
    return (acc / total).astype(BF16).reshape(-1, width)


def nothing(x):
    corner = x[(0,) * x.ndim].astype(jnp.int32)
    return lax.shift_right_logical(corner & 1, 1).astype(F32)


def slices(size, shares):
    ends = [sum(shares[: i + 1]) * size // sum(shares) for i in range(len(shares))]
    return [slice(a, b) for a, b in zip([0] + ends[:-1], ends)]


def steps_of(piece):
    size = math.gcd(piece.stop - piece.start, piece.start)
    block = next(b for b in (512, 384, 256, 128) if size % b == 0)
    return block, (piece.stop - piece.start) // block, piece.start // block


def corner_of(x):
    shape = (min(16, x.shape[0]), min(128, x.shape[1]))
    return pl.BlockSpec(shape, lambda *_: (0, 0))


def call(kernel, earlier, operands, specs, **options):
    def body(*refs):
        n = len(operands)
        kernel(refs[:n], refs[n + len(earlier) :])

    return pl.pallas_call(
        body,
        in_specs=list(specs) + [corner_of(a) for a in earlier],
        compiler_params=PARAMS,
        cost_estimate=SOON,
        **options,
    )(*operands, *earlier)


def gelu_sum(parts, earlier=()):
    rows, units = parts[0].shape
    block, steps, _ = steps_of(slice(0, units))
    spec = pl.BlockSpec((rows, block), lambda j: (0, j))

    def kernel(ins, outs):
        up = ins[0][...].astype(F32)
        for part in ins[1:]:
            up = up + part[...].astype(F32)
        outs[0][...] = (0.5 * up * (1.0 + lax.erf(up * 0.5**0.5))).astype(BF16)

    return call(
        kernel,
        earlier,
        parts,
        [spec] * len(parts),
        grid=(steps,),
        out_specs=spec,
        out_shape=jax.ShapeDtypeStruct((rows, units), BF16),
    )


def project_rows(own, other, weight, piece, earlier=()):
    rows, depth = own.shape
    columns = piece.stop - piece.start
    block, steps, _ = steps_of(piece)
    whole = pl.BlockSpec((rows, depth), lambda *_: (0, 0))
    out = pl.BlockSpec((rows, columns), lambda *_: (0, 0))

    def kernel(ins, refs):
        near, far, both, landed, sems = refs

        def bring(at):
            start = pl.multiple_of(piece.start + at * block, block)
            source = ins[2].at[:, pl.ds(start, block)]
            return pltpu.make_async_copy(source, landed.at[at], sems.at[at])

        for at in range(min(AHEAD, steps)):
            bring(at).start()
        both[:rows] = ins[0][...]
        both[rows:] = ins[1][...]

        @pl.loop(0, steps)
        def _(at):
            bring(at).wait()

            @pl.when(at + AHEAD < steps)
            def _():
                bring(at + AHEAD).start()

            part = jnp.dot(both[...], landed[at], preferred_element_type=F32).astype(BF16)
            here = pl.ds(pl.multiple_of(at * block, block), block)
            near[:, here] = part[:rows]
            far[:, here] = part[rows:]

    return call(
        kernel,
        earlier,
        (own, other, weight),
        [whole, whole, pl.BlockSpec(memory_space=pltpu.HBM)],
        grid=(1,),
        out_specs=[out] * 2,
        out_shape=[jax.ShapeDtypeStruct((rows, columns), BF16)] * 2,
        scratch_shapes=[
            pltpu.VMEM((2 * rows, depth), BF16),
            pltpu.VMEM((steps, depth, block), BF16),
            pltpu.SemaphoreType.DMA((steps,)),
        ],
    )


def project_hidden(own, other, weight, piece, added, attention, last, earlier=()):
    rows, units = own.shape
    columns = weight.shape[1]
    block, steps, _ = steps_of(piece)
    whole = pl.BlockSpec((rows, columns), lambda *_: (0, 0))
    part = pl.BlockSpec((rows, units), lambda *_: (0, 0))
    specs = [part, part, pl.BlockSpec(memory_space=pltpu.HBM)]
    specs += [whole] * len(added)
    specs += [pl.BlockSpec(a.shape, lambda *_: (0, 0)) for a in attention]

    def kernel(ins, refs):
        outs, (both, total, landed, sems) = refs[:2], refs[2:]

        def bring(at):
            start = pl.multiple_of(piece.start + at * block, block)
            source = ins[2].at[pl.ds(start, block), :]
            return pltpu.make_async_copy(source, landed.at[at], sems.at[at])

        for at in range(min(AHEAD, steps)):
            bring(at).start()
        halves = (slice(0, rows), slice(rows, 2 * rows))
        for at, half in enumerate(halves):
            both[half] = ins[at][...]
            first = jnp.zeros((rows, columns), F32)
            if added:
                first = ins[3 + at][...]
            if attention:
                first = first + jnp.dot(
                    ins[-3 + at][...], ins[-1][...], preferred_element_type=F32
                )
            total[half] = first

        @pl.loop(0, steps)
        def _(at):
            bring(at).wait()

            @pl.when(at + AHEAD < steps)
            def _():
                bring(at + AHEAD).start()

            here = pl.ds(pl.multiple_of(at * block, block), block)
            total[...] += jnp.dot(both[:, here], landed[at], preferred_element_type=F32)

        for out, half in zip(outs, halves):
            out[...] = total[half].astype(out.dtype)

    return call(
        kernel,
        earlier,
        (own, other, weight, *added, *attention),
        specs,
        grid=(1,),
        out_specs=[whole] * 2,
        out_shape=[jax.ShapeDtypeStruct((rows, columns), BF16 if last else F32)] * 2,
        scratch_shapes=[
            pltpu.VMEM((2 * rows, units), BF16),
            pltpu.VMEM((2 * rows, columns), F32),
            pltpu.VMEM((steps, block, columns), BF16),
            pltpu.SemaphoreType.DMA((steps,)),
        ],
    )


def make_body(mesh):
    n_red, n_wide = mesh.shape["red"], mesh.shape["wide"]
    half_wide = n_wide // 2

    def swap(x):
        return lax.ppermute(x, "tok", [(0, 1), (1, 0)])

    def all_red(x):
        parts = [x]
        for shift in range(1, n_red):
            pairs = [(i, (i + shift) % n_red) for i in range(n_red)]
            parts.append(lax.ppermute(x, "red", pairs))
        return parts

    def sum_red(x):
        return sum(a.astype(F32) for a in all_red(x))

    def collect(kept, got, width):
        core, chip = lax.axis_index("tok"), lax.axis_index("wide")
        terms = jnp.concatenate([kept, got], axis=1)

        def block(at):
            start = ((at // half_wide) ^ core) * half_wide + at % half_wide
            return lax.dynamic_slice_in_dim(terms, start * width, width, axis=1)

        total = block(chip).astype(F32)
        for k in range(n_wide - 1, 0, -1):
            pairs = [(i, i ^ k) for i in range(n_wide)]
            total = total + lax.ppermute(block(chip ^ k), "wide", pairs).astype(F32)
        return total

    def body(tokens, ln_gain, q_gain, k_gain, w_qkv, w_up, w_attn, w_down):
        core = lax.axis_index("tok")
        width = tokens.shape[1]
        qkv_rows = w_qkv.reshape(w_qkv.shape[0], w_qkv.shape[1] * w_qkv.shape[2])
        attn_rows = w_attn.reshape(w_attn.shape[0] * w_attn.shape[1], w_attn.shape[2])
        depth, units = w_up.shape
        cuts = slices(tokens.shape[0], SHARES)
        pieces = slices(units, PIECES)
        n = len(cuts)

        raw = lax.all_gather(tokens, "wide", axis=1, tiled=True)
        gain = lax.all_gather(ln_gain, "wide", axis=0, tiled=True)
        floats = tokens.astype(F32)
        sums = jnp.stack([jnp.sum(floats, axis=1), jnp.sum(floats * floats, axis=1)])
        sums = lax.psum(sums, ("wide", "red"))[:, :, None] / D
        normed = normalize(raw.astype(F32), sums[0], sums[1], gain).astype(BF16)
        own = lax.dynamic_slice_in_dim(normed, core * depth, depth, axis=1)
        other = lax.dynamic_slice_in_dim(normed, (1 - core) * depth, depth, axis=1)
        other = swap(other)

        def project(weight, piece, earlier):
            near, far = project_rows(own, other, weight, piece, earlier)
            return near, swap(far)

        def block_sum(parts, start=0.0):
            return (parts[0].astype(F32) + parts[1].astype(F32) + start).astype(BF16)

        halves, earlier = [], ()
        for piece in pieces:
            halves.append(project(w_up, piece, earlier))
            earlier = [halves[-1][0]]
        qkv = block_sum(project(qkv_rows, slice(0, qkv_rows.shape[1]), earlier))

        order = [(c, p) for c in range(n) for p in range(len(pieces))]
        outs, scattered = [], []
        terms, waiting, firsts = (), None, []
        earlier = ()

        def output(at, have, terms, earlier):
            c, p = order[at]
            attention = (attended[cuts[c]], attended_other[cuts[c]], attn_rows)
            return project_hidden(
                have,
                swap(have),
                w_down,
                pieces[p],
                terms if p else (),
                () if p else attention,
                p == len(pieces) - 1,
                earlier,
            )

        def scatter(kept, got):
            lower = jnp.where(core == 0, kept, got)
            upper = jnp.where(core == 0, got, kept)
            full = jnp.concatenate([lower, upper], axis=1)
            scattered.append(lax.psum_scatter(full, "wide", scatter_dimension=1, tiled=True))
            return full

        hidden = None
        for at, (c, p) in enumerate(order):
            start = nothing(firsts[c - 1]) if c else 0.0
            parts = all_red(block_sum([a[cuts[c]] for a in halves[p]], start))
            arrived = gelu_sum(parts, earlier)
            earlier = [arrived]
            if p == 0:
                firsts.append(arrived)
            if at == 0:
                attended = attend(sum_red(qkv) + nothing(arrived), q_gain, k_gain)
                attended_other = swap(attended)
                earlier = [attended]
            if waiting is not None:
                earlier.append(scatter(*waiting))
                waiting = None
            if at == len(order) - 1:
                earlier += scattered[:1]
            if at:
                terms = output(at - 1, hidden, terms, earlier)
                earlier = [terms[0]]
                if p == 0:
                    waiting = (terms[0], swap(terms[1]))
            hidden = arrived
        if waiting is not None:
            earlier.append(scatter(*waiting))
        terms = output(len(order) - 1, hidden, terms, earlier)
        for cut, summed in zip(cuts, scattered):
            outs.append(tokens[cut].astype(F32) + summed.astype(F32))
        outs.append(tokens[cuts[-1]].astype(F32) + collect(terms[0], swap(terms[1]), width))
        return jnp.concatenate(outs, axis=0)

    return body


def solution(mesh):
    return jax.shard_map(
        make_body(mesh),
        mesh=mesh,
        in_specs=(
            P(("grp", "tok"), ("red", "wide")),
            P(("red", "wide")),
            P("wide", None),
            P("wide", None),
            P(("red", "tok"), "wide", None),
            P(("red", "tok"), "wide"),
            P("wide", None, ("red", "tok")),
            P("wide", ("red", "tok")),
        ),
        out_specs=P(("grp", "tok"), ("red", "wide")),
        check_vma=False,
    )
```

```python
import functools
import math

import jax
import jax.numpy as jnp
from jax import lax
from jax.experimental import pallas as pl
from jax.experimental.pallas import tpu as pltpu
from jax.sharding import PartitionSpec as P

D = 6144
PATCHES = 256
EPS = 1e-06
SHARES = (7, 5, 4)
PIECES = (1, 1)
AHEAD = 4
BF16, F32 = jnp.bfloat16, jnp.float32
PARAMS = pltpu.CompilerParams(vmem_limit_bytes=48 * 2**20)
SMALL = pltpu.CompilerParams(vmem_limit_bytes=8 * 2**20)
LONG = pl.CostEstimate(flops=0, bytes_accessed=10**8, transcendentals=0)
SOON = pl.CostEstimate(flops=0, bytes_accessed=0, transcendentals=0)


def normalize(values, mean, meansq, gain):
    return (values - mean) * lax.rsqrt(meansq - mean * mean + EPS) * gain.astype(F32)


def head_norm(values, gain):
    mean = jnp.mean(values, axis=-1, keepdims=True)
    meansq = jnp.mean(values * values, axis=-1, keepdims=True)
    return normalize(values, mean, meansq, gain)


def attend(qkv, q_gain, k_gain):
    width = q_gain.shape[1]
    query = head_norm(qkv[:, :width], q_gain[0]).astype(BF16)
    key = head_norm(qkv[:, width : 2 * width], k_gain[0]).astype(BF16)
    value = qkv[:, 2 * width :].astype(BF16)
    query, key, value = (a.reshape(-1, PATCHES, width) for a in (query, key, value))
    scores = jnp.einsum("ipd,iqd->ipq", query, key, preferred_element_type=F32)
    scores = scores * width ** (-0.5)
    weights = jnp.exp(scores - jnp.max(scores, axis=-1, keepdims=True))
    total = jnp.sum(weights, axis=-1, keepdims=True)
    acc = jnp.einsum("ipq,iqd->ipd", weights, value.astype(F32), precision=lax.Precision.HIGHEST)
    return (acc / total).astype(BF16).reshape(-1, width)


def nothing(x):
    corner = x[(0,) * x.ndim].astype(jnp.int32)
    return lax.shift_right_logical(corner & 1, 1).astype(F32)


def slices(size, shares):
    ends = [sum(shares[: i + 1]) * size // sum(shares) for i in range(len(shares))]
    return [slice(a, b) for a, b in zip([0] + ends[:-1], ends)]


def steps_of(piece):
    size = math.gcd(piece.stop - piece.start, piece.start)
    block = next(b for b in (512, 384, 256, 128) if size % b == 0)
    return block, (piece.stop - piece.start) // block, piece.start // block


def corner_of(x):
    shape = (min(16, x.shape[0]), min(128, x.shape[1]))
    return pl.BlockSpec(shape, lambda *_: (0, 0))


def call(kernel, earlier, operands, specs, params=None, cost=None, **options):
    def body(*refs):
        n = len(operands)
        kernel(refs[:n], refs[n + len(earlier) :])

    return pl.pallas_call(
        body,
        in_specs=list(specs) + [corner_of(a) for a in earlier],
        compiler_params=params or PARAMS,
        cost_estimate=cost or SOON,
        **options,
    )(*operands, *earlier)


def token_sums(tokens):
    rows = tokens.shape[0]

    def kernel(ins, outs):
        floats = ins[0][...].astype(F32)
        outs[0][...] = jnp.sum(floats, axis=1, keepdims=True)
        outs[1][...] = jnp.sum(floats * floats, axis=1, keepdims=True)

    return call(
        kernel,
        (),
        (tokens,),
        [pl.BlockSpec(tokens.shape, lambda *_: (0, 0))],
        params=SMALL,
        cost=LONG,
        grid=(1,),
        out_specs=[pl.BlockSpec((rows, 1), lambda *_: (0, 0))] * 2,
        out_shape=[jax.ShapeDtypeStruct((rows, 1), F32)] * 2,
    )


def gelu_sum(parts, earlier=()):
    rows, units = parts[0].shape
    block, steps, _ = steps_of(slice(0, units))
    spec = pl.BlockSpec((rows, block), lambda j: (0, j))

    def kernel(ins, outs):
        up = ins[0][...].astype(F32)
        for part in ins[1:]:
            up = up + part[...].astype(F32)
        outs[0][...] = (0.5 * up * (1.0 + lax.erf(up * 0.5**0.5))).astype(BF16)

    return call(
        kernel,
        earlier,
        parts,
        [spec] * len(parts),
        params=SMALL,
        grid=(steps,),
        out_specs=spec,
        out_shape=jax.ShapeDtypeStruct((rows, units), BF16),
    )


def project_hidden(own, other, weight, piece, added, attention, last, earlier=()):
    rows, units = own.shape
    columns = weight.shape[1]
    block, steps, _ = steps_of(piece)
    whole = pl.BlockSpec((rows, columns), lambda *_: (0, 0))
    part = pl.BlockSpec((rows, units), lambda *_: (0, 0))
    specs = [part, part, pl.BlockSpec(memory_space=pltpu.HBM)]
    specs += [whole] * len(added)
    specs += [pl.BlockSpec(a.shape, lambda *_: (0, 0)) for a in attention]

    def kernel(ins, refs):
        outs, (both, total, landed, sems) = refs[:2], refs[2:]

        def bring(at):
            start = pl.multiple_of(piece.start + at * block, block)
            source = ins[2].at[pl.ds(start, block), :]
            return pltpu.make_async_copy(source, landed.at[at], sems.at[at])

        for at in range(min(AHEAD, steps)):
            bring(at).start()
        halves = (slice(0, rows), slice(rows, 2 * rows))
        for at, half in enumerate(halves):
            both[half] = ins[at][...]
            first = jnp.zeros((rows, columns), F32)
            if added:
                first = ins[3 + at][...]
            if attention:
                first = first + jnp.dot(
                    ins[-3 + at][...], ins[-1][...], preferred_element_type=F32
                )
            total[half] = first

        @pl.loop(0, steps)
        def _(at):
            bring(at).wait()

            @pl.when(at + AHEAD < steps)
            def _():
                bring(at + AHEAD).start()

            here = pl.ds(pl.multiple_of(at * block, block), block)
            total[...] += jnp.dot(both[:, here], landed[at], preferred_element_type=F32)

        for out, half in zip(outs, halves):
            out[...] = total[half].astype(out.dtype)

    return call(
        kernel,
        earlier,
        (own, other, weight, *added, *attention),
        specs,
        grid=(1,),
        out_specs=[whole] * 2,
        out_shape=[jax.ShapeDtypeStruct((rows, columns), BF16 if last else F32)] * 2,
        scratch_shapes=[
            pltpu.VMEM((2 * rows, units), BF16),
            pltpu.VMEM((2 * rows, columns), F32),
            pltpu.VMEM((steps, block, columns), BF16),
            pltpu.SemaphoreType.DMA((steps,)),
        ],
    )


def make_body(mesh):
    n_red, n_wide = mesh.shape["red"], mesh.shape["wide"]
    half_wide = n_wide // 2

    def swap(x):
        return lax.ppermute(x, "tok", [(0, 1), (1, 0)])

    def all_red(x):
        parts = [x]
        for shift in range(1, n_red):
            pairs = [(i, (i + shift) % n_red) for i in range(n_red)]
            parts.append(lax.ppermute(x, "red", pairs))
        return parts

    def sum_red(x):
        return sum(a.astype(F32) for a in all_red(x))

    def collect(kept, got, width):
        core, chip = lax.axis_index("tok"), lax.axis_index("wide")
        terms = jnp.concatenate([kept, got], axis=1)

        def block(at):
            start = ((at // half_wide) ^ core) * half_wide + at % half_wide
            return lax.dynamic_slice_in_dim(terms, start * width, width, axis=1)

        total = block(chip).astype(F32)
        for k in range(n_wide - 1, 0, -1):
            pairs = [(i, i ^ k) for i in range(n_wide)]
            total = total + lax.ppermute(block(chip ^ k), "wide", pairs).astype(F32)
        return total

    def body(tokens, ln_gain, q_gain, k_gain, w_qkv, w_up, w_attn, w_down):
        core = lax.axis_index("tok")
        width = tokens.shape[1]
        qkv_rows = w_qkv.reshape(w_qkv.shape[0], w_qkv.shape[1] * w_qkv.shape[2])
        attn_rows = w_attn.reshape(w_attn.shape[0] * w_attn.shape[1], w_attn.shape[2])
        depth, units = w_up.shape
        cuts = slices(tokens.shape[0], SHARES)
        pieces = slices(units, PIECES)
        n = len(cuts)

        raw = lax.all_gather(tokens, "wide", axis=1, tiled=True)
        gain = lax.all_gather(ln_gain, "wide", axis=0, tiled=True)
        sums = lax.psum(jnp.stack(token_sums(tokens)), ("wide", "red")) / D
        normed = normalize(raw.astype(F32), sums[0], sums[1], gain).astype(BF16)
        own = lax.dynamic_slice_in_dim(normed, core * depth, depth, axis=1)
        other = lax.dynamic_slice_in_dim(normed, (1 - core) * depth, depth, axis=1)
        other = swap(other)

        def far_part(weight):
            return swap(jnp.dot(other, weight, preferred_element_type=F32).astype(BF16))

        def near_sum(cut, weight, far):
            near = jnp.dot(own[cut], weight, preferred_element_type=F32)
            return (near + far[cut].astype(F32)).astype(BF16)

        rows = slice(0, tokens.shape[0])
        rest = slice(cuts[0].stop, rows.stop)
        weights = [w_up[:, piece] for piece in pieces]
        fars = [far_part(weight) for weight in weights]
        leads = [near_sum(cuts[0], weight, far) for weight, far in zip(weights, fars)]
        rests = [near_sum(rest, weight, far) for weight, far in zip(weights, fars)]
        qkv = near_sum(rows, qkv_rows, far_part(qkv_rows))

        order = [(c, p) for c in range(n) for p in range(len(pieces))]
        outs, scattered = [], []
        terms, waiting, firsts = (), None, []
        earlier = ()

        def output(at, have, terms, earlier):
            c, p = order[at]
            attention = (attended[cuts[c]], attended_other[cuts[c]], attn_rows)
            return project_hidden(
                have,
                swap(have),
                w_down,
                pieces[p],
                terms if p else (),
                () if p else attention,
                p == len(pieces) - 1,
                earlier,
            )

        def scatter(kept, got):
            lower = jnp.where(core == 0, kept, got)
            upper = jnp.where(core == 0, got, kept)
            full = jnp.concatenate([lower, upper], axis=1)
            scattered.append(lax.psum_scatter(full, "wide", scatter_dimension=1, tiled=True))
            return full

        hidden = None
        for at, (c, p) in enumerate(order):
            if c:
                part = slice(cuts[c].start - rest.start, cuts[c].stop - rest.start)
                parts = all_red(rests[p][part] + nothing(firsts[c - 1]).astype(BF16))
            else:
                parts = all_red(leads[p])
            arrived = gelu_sum(parts, earlier)
            earlier = [arrived]
            if p == 0:
                firsts.append(arrived)
            if at == 0:
                attended = attend(sum_red(qkv) + nothing(arrived), q_gain, k_gain)
                attended_other = swap(attended)
                earlier = [attended]
            if waiting is not None:
                earlier.append(scatter(*waiting))
                waiting = None
            if at == len(order) - 1:
                earlier += scattered[:1]
            if at:
                terms = output(at - 1, hidden, terms, earlier)
                earlier = [terms[0]]
                if p == 0:
                    waiting = (terms[0], swap(terms[1]))
            hidden = arrived
        if waiting is not None:
            earlier.append(scatter(*waiting))
        terms = output(len(order) - 1, hidden, terms, earlier)
        for cut, summed in zip(cuts, scattered):
            outs.append(tokens[cut].astype(F32) + summed.astype(F32))
        outs.append(tokens[cuts[-1]].astype(F32) + collect(terms[0], swap(terms[1]), width))
        return jnp.concatenate(outs, axis=0)

    return body


def solution(mesh):
    return jax.shard_map(
        make_body(mesh),
        mesh=mesh,
        in_specs=(
            P(("grp", "tok"), ("red", "wide")),
            P(("red", "wide")),
            P("wide", None),
            P("wide", None),
            P(("red", "tok"), "wide", None),
            P(("red", "tok"), "wide"),
            P("wide", None, ("red", "tok")),
            P("wide", ("red", "tok")),
        ),
        out_specs=P(("grp", "tok"), ("red", "wide")),
        check_vma=False,
    )
```

```python
import functools
import math

import jax
import jax.numpy as jnp
from jax import lax
from jax.experimental import pallas as pl
from jax.experimental.pallas import tpu as pltpu
from jax.sharding import PartitionSpec as P

D = 6144
PATCHES = 256
EPS = 1e-06
SHARES = (8, 4, 4)
PIECES = (1, 1)
AHEAD = 4
GAIN_ROWS = 8
BF16, F32 = jnp.bfloat16, jnp.float32
PARAMS = pltpu.CompilerParams(vmem_limit_bytes=48 * 2**20)
SMALL = pltpu.CompilerParams(vmem_limit_bytes=8 * 2**20)
SOON = pl.CostEstimate(flops=0, bytes_accessed=0, transcendentals=0)


def normalize(values, mean, meansq, gain):
    return (values - mean) * lax.rsqrt(meansq - mean * mean + EPS) * gain.astype(F32)


def head_norm(values, gain):
    mean = jnp.mean(values, axis=-1, keepdims=True)
    meansq = jnp.mean(values * values, axis=-1, keepdims=True)
    return normalize(values, mean, meansq, gain)


def attend(qkv, q_gain, k_gain):
    width = q_gain.shape[1]
    query = head_norm(qkv[:, :width], q_gain[0]).astype(BF16)
    key = head_norm(qkv[:, width : 2 * width], k_gain[0]).astype(BF16)
    value = qkv[:, 2 * width :].astype(BF16)
    query, key, value = (a.reshape(-1, PATCHES, width) for a in (query, key, value))
    scores = jnp.einsum("ipd,iqd->ipq", query, key, preferred_element_type=F32)
    scores = scores * width ** (-0.5)
    weights = jnp.exp(scores - jnp.max(scores, axis=-1, keepdims=True))
    total = jnp.sum(weights, axis=-1, keepdims=True)
    acc = jnp.einsum("ipq,iqd->ipd", weights, value.astype(F32), precision=lax.Precision.HIGHEST)
    return (acc / total).astype(BF16).reshape(-1, width)


def nothing(x):
    corner = x[(0,) * x.ndim].astype(jnp.int32)
    return lax.shift_right_logical(corner & 1, 1).astype(F32)


def slices(size, shares):
    ends = [sum(shares[: i + 1]) * size // sum(shares) for i in range(len(shares))]
    return [slice(a, b) for a, b in zip([0] + ends[:-1], ends)]


def steps_of(piece):
    size = math.gcd(piece.stop - piece.start, piece.start)
    block = next(b for b in (512, 384, 256, 128) if size % b == 0)
    return block, (piece.stop - piece.start) // block, piece.start // block


def corner_of(x):
    shape = (min(16, x.shape[0]), min(128, x.shape[1]))
    return pl.BlockSpec(shape, lambda *_: (0, 0))


def call(kernel, earlier, operands, specs, params=None, **options):
    def body(*refs):
        n = len(operands)
        kernel(refs[:n], refs[n + len(earlier) :])

    return pl.pallas_call(
        body,
        in_specs=list(specs) + [corner_of(a) for a in earlier],
        compiler_params=params or PARAMS,
        cost_estimate=SOON,
        **options,
    )(*operands, *earlier)


def gelu_sum(parts, earlier=()):
    rows, units = parts[0].shape
    block, steps, _ = steps_of(slice(0, units))
    spec = pl.BlockSpec((rows, block), lambda j: (0, j))

    def kernel(ins, outs):
        up = ins[0][...].astype(F32)
        for part in ins[1:]:
            up = up + part[...].astype(F32)
        outs[0][...] = (0.5 * up * (1.0 + lax.erf(up * 0.5**0.5))).astype(BF16)

    return call(
        kernel,
        earlier,
        parts,
        [spec] * len(parts),
        params=SMALL,
        grid=(steps,),
        out_specs=spec,
        out_shape=jax.ShapeDtypeStruct((rows, units), BF16),
    )


def project_hidden(own, other, weight, piece, added, attention, last, earlier=()):
    rows, units = own.shape
    columns = weight.shape[1]
    block, steps, _ = steps_of(piece)
    whole = pl.BlockSpec((rows, columns), lambda *_: (0, 0))
    part = pl.BlockSpec((rows, units), lambda *_: (0, 0))
    specs = [part, part, pl.BlockSpec(memory_space=pltpu.HBM)]
    specs += [whole] * len(added)
    specs += [pl.BlockSpec(a.shape, lambda *_: (0, 0)) for a in attention]

    def kernel(ins, refs):
        outs, (both, total, landed, sems) = refs[:2], refs[2:]

        def bring(at):
            start = pl.multiple_of(piece.start + at * block, block)
            source = ins[2].at[pl.ds(start, block), :]
            return pltpu.make_async_copy(source, landed.at[at], sems.at[at])

        for at in range(min(AHEAD, steps)):
            bring(at).start()
        halves = (slice(0, rows), slice(rows, 2 * rows))
        for at, half in enumerate(halves):
            both[half] = ins[at][...]
            first = jnp.zeros((rows, columns), F32)
            if added:
                first = ins[3 + at][...]
            if attention:
                first = first + jnp.dot(
                    ins[-3 + at][...], ins[-1][...], preferred_element_type=F32
                )
            total[half] = first

        @pl.loop(0, steps)
        def _(at):
            bring(at).wait()

            @pl.when(at + AHEAD < steps)
            def _():
                bring(at + AHEAD).start()

            here = pl.ds(pl.multiple_of(at * block, block), block)
            total[...] += jnp.dot(both[:, here], landed[at], preferred_element_type=F32)

        for out, half in zip(outs, halves):
            out[...] = total[half].astype(out.dtype)

    return call(
        kernel,
        earlier,
        (own, other, weight, *added, *attention),
        specs,
        grid=(1,),
        out_specs=[whole] * 2,
        out_shape=[jax.ShapeDtypeStruct((rows, columns), BF16 if last else F32)] * 2,
        scratch_shapes=[
            pltpu.VMEM((2 * rows, units), BF16),
            pltpu.VMEM((2 * rows, columns), F32),
            pltpu.VMEM((steps, block, columns), BF16),
            pltpu.SemaphoreType.DMA((steps,)),
        ],
    )


def make_body(mesh):
    n_red, n_wide = mesh.shape["red"], mesh.shape["wide"]
    half_wide = n_wide // 2

    def swap(x):
        return lax.ppermute(x, "tok", [(0, 1), (1, 0)])

    def all_red(x):
        parts = [x]
        for shift in range(1, n_red):
            pairs = [(i, (i + shift) % n_red) for i in range(n_red)]
            parts.append(lax.ppermute(x, "red", pairs))
        return parts

    def sum_red(x):
        return sum(a.astype(F32) for a in all_red(x))

    def collect(kept, got, width):
        core, chip = lax.axis_index("tok"), lax.axis_index("wide")
        terms = jnp.concatenate([kept, got], axis=1)

        def block(at):
            start = ((at // half_wide) ^ core) * half_wide + at % half_wide
            return lax.dynamic_slice_in_dim(terms, start * width, width, axis=1)

        total = block(chip).astype(F32)
        for k in range(n_wide - 1, 0, -1):
            pairs = [(i, i ^ k) for i in range(n_wide)]
            total = total + lax.ppermute(block(chip ^ k), "wide", pairs).astype(F32)
        return total

    def body(tokens, ln_gain, q_gain, k_gain, w_qkv, w_up, w_attn, w_down):
        core = lax.axis_index("tok")
        width = tokens.shape[1]
        qkv_rows = w_qkv.reshape(w_qkv.shape[0], w_qkv.shape[1] * w_qkv.shape[2])
        attn_rows = w_attn.reshape(w_attn.shape[0] * w_attn.shape[1], w_attn.shape[2])
        depth, units = w_up.shape
        cuts = slices(tokens.shape[0], SHARES)
        pieces = slices(units, PIECES)
        n = len(cuts)

        first = cuts[0].stop
        gain_rows = jnp.broadcast_to(ln_gain[None], (GAIN_ROWS, width))
        lead = jnp.concatenate([gain_rows, tokens[:first]], axis=0)
        lead = lax.all_gather(lead, "wide", axis=1, tiled=True)
        gain = lead[:1]

        def normed(floats):
            sums = jnp.stack([jnp.sum(floats, axis=1), jnp.sum(floats * floats, axis=1)])
            sums = sum_red(sums)[:, :, None] / D
            values = normalize(floats, sums[0], sums[1], gain).astype(BF16)
            mine = lax.dynamic_slice_in_dim(values, core * depth, depth, axis=1)
            theirs = lax.dynamic_slice_in_dim(values, (1 - core) * depth, depth, axis=1)
            return mine, swap(theirs)

        def project(pair, weight):
            both = jnp.concatenate(pair, axis=0)
            half = both.shape[0] // 2
            part = jnp.dot(both, weight, preferred_element_type=F32)
            far = swap(part[half:].astype(BF16)).astype(F32)
            return (part[:half] + far).astype(BF16)

        weights = [w_up[:, piece] for piece in pieces]
        lead_pair = normed(lead[GAIN_ROWS:].astype(F32))
        leads = [project(lead_pair, weight) for weight in weights]
        lead_parts = [all_red(x) for x in leads]
        arrived = gelu_sum(lead_parts[0])

        rest = tokens[first:] + nothing(leads[-1]).astype(BF16)
        rest = lax.all_gather(rest, "wide", axis=1, tiled=True)
        rest_pair = normed(rest.astype(F32) + nothing(arrived))
        qkv = project([jnp.concatenate(p, axis=0) for p in zip(lead_pair, rest_pair)], qkv_rows)
        rests = [project(rest_pair, weight) for weight in weights]

        order = [(c, p) for c in range(n) for p in range(len(pieces))]
        outs, scattered = [], []
        terms, waiting, firsts = (), None, []
        earlier = [rests[-1]]

        def output(at, have, terms, earlier):
            c, p = order[at]
            attention = ()
            if p == len(pieces) - 1:
                attention = (attended[cuts[c]], attended_other[cuts[c]], attn_rows)
            return project_hidden(
                have,
                swap(have),
                w_down,
                pieces[p],
                terms if p else (),
                attention,
                p == len(pieces) - 1,
                earlier,
            )

        def scatter(kept, got):
            lower = jnp.where(core == 0, kept, got)
            upper = jnp.where(core == 0, got, kept)
            full = jnp.concatenate([lower, upper], axis=1)
            scattered.append(lax.psum_scatter(full, "wide", scatter_dimension=1, tiled=True))
            return full

        hidden = None
        for at, (c, p) in enumerate(order):
            if c:
                part = slice(cuts[c].start - first, cuts[c].stop - first)
                parts = all_red(rests[p][part] + nothing(firsts[c - 1]).astype(BF16))
            else:
                parts = lead_parts[p]
            if at:
                arrived = gelu_sum(parts, earlier)
                earlier = [arrived]
            if p == 0:
                firsts.append(arrived)
            if at == 1:
                attended = attend(sum_red(qkv) + nothing(arrived), q_gain, k_gain)
                attended_other = swap(attended)
                earlier = [attended]
            if waiting is not None:
                earlier.append(scatter(*waiting))
                waiting = None
            if at == len(order) - 1:
                earlier += scattered[:1]
            if at:
                terms = output(at - 1, hidden, terms, earlier)
                earlier = [terms[0]]
                if p == 0:
                    waiting = (terms[0], swap(terms[1]))
            hidden = arrived
        if waiting is not None:
            earlier.append(scatter(*waiting))
        terms = output(len(order) - 1, hidden, terms, earlier)
        for cut, summed in zip(cuts, scattered):
            outs.append(tokens[cut].astype(F32) + summed.astype(F32))
        outs.append(tokens[cuts[-1]].astype(F32) + collect(terms[0], swap(terms[1]), width))
        return jnp.concatenate(outs, axis=0)

    return body


def solution(mesh):
    return jax.shard_map(
        make_body(mesh),
        mesh=mesh,
        in_specs=(
            P(("grp", "tok"), ("red", "wide")),
            P(("red", "wide")),
            P("wide", None),
            P("wide", None),
            P(("red", "tok"), "wide", None),
            P(("red", "tok"), "wide"),
            P("wide", None, ("red", "tok")),
            P("wide", ("red", "tok")),
        ),
        out_specs=P(("grp", "tok"), ("red", "wide")),
        check_vma=False,
    )
```

```python
import functools
import math

import jax
import jax.numpy as jnp
from jax import lax
from jax.experimental import pallas as pl
from jax.experimental.pallas import tpu as pltpu
from jax.sharding import PartitionSpec as P

D = 6144
PATCHES = 256
EPS = 1e-06
SHARES = (9, 4, 3)
PIECES = (1, 1)
AHEAD = 4
GAIN_ROWS = 8
BF16, F32 = jnp.bfloat16, jnp.float32
PARAMS = pltpu.CompilerParams(vmem_limit_bytes=48 * 2**20)
SMALL = pltpu.CompilerParams(vmem_limit_bytes=8 * 2**20)
SOON = pl.CostEstimate(flops=0, bytes_accessed=0, transcendentals=0)


def normalize(values, mean, meansq, gain):
    return (values - mean) * lax.rsqrt(meansq - mean * mean + EPS) * gain.astype(F32)


def head_norm(values, gain):
    mean = jnp.mean(values, axis=-1, keepdims=True)
    meansq = jnp.mean(values * values, axis=-1, keepdims=True)
    return normalize(values, mean, meansq, gain)


def nothing(x):
    corner = x[(0,) * x.ndim].astype(jnp.int32)
    return lax.shift_right_logical(corner & 1, 1).astype(F32)


def slices(size, shares):
    ends = [sum(shares[: i + 1]) * size // sum(shares) for i in range(len(shares))]
    return [slice(a, b) for a, b in zip([0] + ends[:-1], ends)]


def steps_of(piece):
    size = math.gcd(piece.stop - piece.start, piece.start)
    block = next(b for b in (512, 384, 256, 128) if size % b == 0)
    return block, (piece.stop - piece.start) // block, piece.start // block


def corner_of(x):
    shape = (min(16, x.shape[0]), min(128, x.shape[1]))
    return pl.BlockSpec(shape, lambda *_: (0, 0))


def call(kernel, earlier, operands, specs, params=None, **options):
    def body(*refs):
        n = len(operands)
        kernel(refs[:n], refs[n + len(earlier) :])

    return pl.pallas_call(
        body,
        in_specs=list(specs) + [corner_of(a) for a in earlier],
        compiler_params=params or PARAMS,
        cost_estimate=SOON,
        **options,
    )(*operands, *earlier)


def gelu_sum(parts, earlier=()):
    rows, units = parts[0].shape
    block, steps, _ = steps_of(slice(0, units))
    spec = pl.BlockSpec((rows, block), lambda j: (0, j))

    def kernel(ins, outs):
        up = ins[0][...].astype(F32)
        for part in ins[1:]:
            up = up + part[...].astype(F32)
        outs[0][...] = (0.5 * up * (1.0 + lax.erf(up * 0.5**0.5))).astype(BF16)

    return call(
        kernel,
        earlier,
        parts,
        [spec] * len(parts),
        params=SMALL,
        grid=(steps,),
        out_specs=spec,
        out_shape=jax.ShapeDtypeStruct((rows, units), BF16),
    )


def sum_rows(near, far, cut, earlier=()):
    spec = pl.BlockSpec(near.shape, lambda *_: (0, 0))
    shape = (cut.stop - cut.start, near.shape[1])

    def kernel(ins, outs):
        outs[0][...] = (ins[0][cut].astype(F32) + ins[1][cut].astype(F32)).astype(BF16)

    return call(
        kernel,
        earlier,
        (near, far),
        [spec, spec],
        params=SMALL,
        grid=(1,),
        out_specs=pl.BlockSpec(shape, lambda *_: (0, 0)),
        out_shape=jax.ShapeDtypeStruct(shape, BF16),
    )


def side_by_side(kept, got, core, earlier=()):
    rows, columns = kept.shape
    spec = pl.BlockSpec(kept.shape, lambda *_: (0, 0))

    def kernel(ins, outs):
        first = ins[2][0] == 0
        outs[0][:, :columns] = jnp.where(first, ins[0][...], ins[1][...])
        outs[0][:, columns:] = jnp.where(first, ins[1][...], ins[0][...])

    return call(
        kernel,
        earlier,
        (kept, got, core.reshape(1)),
        [spec, spec, pl.BlockSpec(memory_space=pltpu.SMEM)],
        params=SMALL,
        grid=(1,),
        out_specs=pl.BlockSpec((rows, 2 * columns), lambda *_: (0, 0)),
        out_shape=jax.ShapeDtypeStruct((rows, 2 * columns), kept.dtype),
    )


def attend(parts, q_gain, k_gain, earlier=()):
    rows, width = parts[0].shape[0], q_gain.shape[1]
    n = len(parts)

    def kernel(ins, outs):
        def columns(at):
            here = slice(at * width, (at + 1) * width)
            return sum(part[:, here].astype(F32) for part in ins[:n])

        query = head_norm(columns(0), ins[n][...]).astype(BF16)
        key = head_norm(columns(1), ins[n + 1][...]).astype(BF16)
        value = columns(2).astype(BF16).astype(F32)
        for at in range(0, rows, PATCHES):
            image = slice(at, at + PATCHES)
            scores = lax.dot_general(
                query[image], key[image], (((1,), (1,)), ((), ())), preferred_element_type=F32
            )
            scores = scores * width ** (-0.5)
            weights = jnp.exp(scores - jnp.max(scores, axis=-1, keepdims=True))
            total = jnp.sum(weights, axis=-1, keepdims=True)
            acc = jnp.dot(
                weights,
                value[image],
                precision=lax.Precision.HIGHEST,
                preferred_element_type=F32,
            )
            outs[0][image] = (acc / total).astype(BF16)

    whole = [pl.BlockSpec(a.shape, lambda *_: (0, 0)) for a in (*parts, q_gain, k_gain)]
    return call(
        kernel,
        earlier,
        (*parts, q_gain, k_gain),
        whole,
        params=SMALL,
        grid=(1,),
        out_specs=pl.BlockSpec((rows, width), lambda *_: (0, 0)),
        out_shape=jax.ShapeDtypeStruct((rows, width), BF16),
    )


def project_rows(own, other, weight, piece, earlier=()):
    rows, depth = own.shape
    columns = piece.stop - piece.start
    block, steps, _ = steps_of(piece)
    whole = pl.BlockSpec((rows, depth), lambda *_: (0, 0))
    out = pl.BlockSpec((rows, columns), lambda *_: (0, 0))

    def kernel(ins, refs):
        near, far, both, landed, sems = refs

        def bring(at):
            start = pl.multiple_of(piece.start + at * block, block)
            source = ins[2].at[:, pl.ds(start, block)]
            return pltpu.make_async_copy(source, landed.at[at], sems.at[at])

        for at in range(min(AHEAD, steps)):
            bring(at).start()
        both[:rows] = ins[0][...]
        both[rows:] = ins[1][...]

        @pl.loop(0, steps)
        def _(at):
            bring(at).wait()

            @pl.when(at + AHEAD < steps)
            def _():
                bring(at + AHEAD).start()

            part = jnp.dot(both[...], landed[at], preferred_element_type=F32).astype(BF16)
            here = pl.ds(pl.multiple_of(at * block, block), block)
            near[:, here] = part[:rows]
            far[:, here] = part[rows:]

    return call(
        kernel,
        earlier,
        (own, other, weight),
        [whole, whole, pl.BlockSpec(memory_space=pltpu.HBM)],
        grid=(1,),
        out_specs=[out] * 2,
        out_shape=[jax.ShapeDtypeStruct((rows, columns), BF16)] * 2,
        scratch_shapes=[
            pltpu.VMEM((2 * rows, depth), BF16),
            pltpu.VMEM((steps, depth, block), BF16),
            pltpu.SemaphoreType.DMA((steps,)),
        ],
    )


def project_hidden(own, other, weight, piece, added, attention, last, earlier=()):
    rows, units = own.shape
    columns = weight.shape[1]
    block, steps, _ = steps_of(piece)
    whole = pl.BlockSpec((rows, columns), lambda *_: (0, 0))
    part = pl.BlockSpec((rows, units), lambda *_: (0, 0))
    specs = [part, part, pl.BlockSpec(memory_space=pltpu.HBM)]
    specs += [whole] * len(added)
    specs += [pl.BlockSpec(a.shape, lambda *_: (0, 0)) for a in attention]

    def kernel(ins, refs):
        outs, (both, total, landed, sems) = refs[:2], refs[2:]

        def bring(at):
            start = pl.multiple_of(piece.start + at * block, block)
            source = ins[2].at[pl.ds(start, block), :]
            return pltpu.make_async_copy(source, landed.at[at], sems.at[at])

        for at in range(min(AHEAD, steps)):
            bring(at).start()
        halves = (slice(0, rows), slice(rows, 2 * rows))
        for at, half in enumerate(halves):
            both[half] = ins[at][...]
            first = jnp.zeros((rows, columns), F32)
            if added:
                first = ins[3 + at][...]
            if attention:
                first = first + jnp.dot(
                    ins[-3 + at][...], ins[-1][...], preferred_element_type=F32
                )
            total[half] = first

        @pl.loop(0, steps)
        def _(at):
            bring(at).wait()

            @pl.when(at + AHEAD < steps)
            def _():
                bring(at + AHEAD).start()

            here = pl.ds(pl.multiple_of(at * block, block), block)
            total[...] += jnp.dot(both[:, here], landed[at], preferred_element_type=F32)

        for out, half in zip(outs, halves):
            out[...] = total[half].astype(out.dtype)

    return call(
        kernel,
        earlier,
        (own, other, weight, *added, *attention),
        specs,
        grid=(1,),
        out_specs=[whole] * 2,
        out_shape=[jax.ShapeDtypeStruct((rows, columns), BF16 if last else F32)] * 2,
        scratch_shapes=[
            pltpu.VMEM((2 * rows, units), BF16),
            pltpu.VMEM((2 * rows, columns), F32),
            pltpu.VMEM((steps, block, columns), BF16),
            pltpu.SemaphoreType.DMA((steps,)),
        ],
    )


def make_body(mesh):
    n_red, n_wide = mesh.shape["red"], mesh.shape["wide"]
    half_wide = n_wide // 2

    def swap(x):
        return lax.ppermute(x, "tok", [(0, 1), (1, 0)])

    def all_red(x):
        parts = [x]
        for shift in range(1, n_red):
            pairs = [(i, (i + shift) % n_red) for i in range(n_red)]
            parts.append(lax.ppermute(x, "red", pairs))
        return parts

    def sum_red(x):
        return sum(a.astype(F32) for a in all_red(x))

    def collect(kept, got, width):
        core, chip = lax.axis_index("tok"), lax.axis_index("wide")
        terms = jnp.concatenate([kept, got], axis=1)

        def block(at):
            start = ((at // half_wide) ^ core) * half_wide + at % half_wide
            return lax.dynamic_slice_in_dim(terms, start * width, width, axis=1)

        total = block(chip).astype(F32)
        for k in range(n_wide - 1, 0, -1):
            pairs = [(i, i ^ k) for i in range(n_wide)]
            total = total + lax.ppermute(block(chip ^ k), "wide", pairs).astype(F32)
        return total

    def body(tokens, ln_gain, q_gain, k_gain, w_qkv, w_up, w_attn, w_down):
        core = lax.axis_index("tok")
        width = tokens.shape[1]
        qkv_rows = w_qkv.reshape(w_qkv.shape[0], w_qkv.shape[1] * w_qkv.shape[2])
        attn_rows = w_attn.reshape(w_attn.shape[0] * w_attn.shape[1], w_attn.shape[2])
        depth, units = w_up.shape
        cuts = slices(tokens.shape[0], SHARES)
        pieces = slices(units, PIECES)
        n = len(cuts)

        first = cuts[0].stop
        gain_rows = jnp.broadcast_to(ln_gain[None], (GAIN_ROWS, width))
        lead = jnp.concatenate([gain_rows, tokens[:first]], axis=0)
        lead = lax.all_gather(lead, "wide", axis=1, tiled=True)
        gain = lead[:1]

        def normed(floats):
            sums = jnp.stack([jnp.sum(floats, axis=1), jnp.sum(floats * floats, axis=1)])
            sums = sum_red(sums)[:, :, None] / D
            values = normalize(floats, sums[0], sums[1], gain).astype(BF16)
            mine = lax.dynamic_slice_in_dim(values, core * depth, depth, axis=1)
            theirs = lax.dynamic_slice_in_dim(values, (1 - core) * depth, depth, axis=1)
            return mine, swap(theirs)

        def project(pair, weight):
            both = jnp.concatenate(pair, axis=0)
            half = both.shape[0] // 2
            part = jnp.dot(both, weight, preferred_element_type=F32)
            far = swap(part[half:].astype(BF16)).astype(F32)
            return (part[:half] + far).astype(BF16)

        weights = [w_up[:, piece] for piece in pieces]
        lead_pair = normed(lead[GAIN_ROWS:].astype(F32))
        leads = [project(lead_pair, weight) for weight in weights]
        lead_parts = [all_red(x) for x in leads]
        arrived = gelu_sum(lead_parts[0])

        rest = tokens[first:] + nothing(leads[-1]).astype(BF16)
        rest = lax.all_gather(rest, "wide", axis=1, tiled=True)
        rest_pair = normed(rest.astype(F32) + nothing(arrived))
        halves, before = [], []
        for piece in pieces:
            near, far = project_rows(*rest_pair, w_up, piece, before)
            halves.append((near, swap(far)))
            before = [near]
        pair = [jnp.concatenate(p, axis=0) for p in zip(lead_pair, rest_pair)]
        near, far = project_rows(*pair, qkv_rows, slice(0, qkv_rows.shape[1]), before)
        qkv = sum_rows(near, swap(far), slice(0, tokens.shape[0]))

        order = [(c, p) for c in range(n) for p in range(len(pieces))]
        outs, scattered = [], []
        terms, waiting, firsts = (), None, []
        earlier = [near]

        def output(at, have, terms, earlier):
            c, p = order[at]
            attention = ()
            if p == len(pieces) - 1:
                attention = (attended[cuts[c]], attended_other[cuts[c]], attn_rows)
            return project_hidden(
                have,
                swap(have),
                w_down,
                pieces[p],
                terms if p else (),
                attention,
                p == len(pieces) - 1,
                earlier,
            )

        def scatter(kept, got, earlier):
            full = side_by_side(kept, got, core, scattered[-1:] + earlier)
            scattered.append(lax.psum_scatter(full, "wide", scatter_dimension=1, tiled=True))
            return full

        def sums_of(p, part, before):
            return sum_rows(*halves[p], part, [before])

        after_lead = [
            sums_of(p, slice(0, cuts[1].stop - first), arrived) for p in range(len(pieces))
        ]
        hidden = None
        for at, (c, p) in enumerate(order):
            if c:
                part = slice(cuts[c].start - first, cuts[c].stop - first)
                parts = all_red(sums_of(p, part, firsts[c - 1]) if c > 1 else after_lead[p])
            else:
                parts = lead_parts[p]
            if at:
                arrived = gelu_sum(parts, earlier)
                earlier = [arrived]
            if p == 0:
                firsts.append(arrived)
            if at == 1:
                attended = attend(all_red(qkv), q_gain, k_gain, earlier)
                attended_other = swap(attended)
                earlier = [attended, *after_lead]
            if waiting is not None and not scattered:
                earlier.append(scatter(*waiting, []))
                waiting = None
            if at:
                terms = output(at - 1, hidden, terms, earlier)
                earlier = [terms[0]]
            if waiting is not None:
                earlier = [scatter(*waiting, earlier)]
                waiting = None
            if at and p == 0:
                waiting = (terms[0], swap(terms[1]))
            hidden = arrived
        terms = output(len(order) - 1, hidden, terms, earlier)
        for cut, summed in zip(cuts, scattered):
            outs.append(tokens[cut].astype(F32) + summed.astype(F32))
        outs.append(tokens[cuts[-1]].astype(F32) + collect(terms[0], swap(terms[1]), width))
        return jnp.concatenate(outs, axis=0)

    return body


def solution(mesh):
    return jax.shard_map(
        make_body(mesh),
        mesh=mesh,
        in_specs=(
            P(("grp", "tok"), ("red", "wide")),
            P(("red", "wide")),
            P("wide", None),
            P("wide", None),
            P(("red", "tok"), "wide", None),
            P(("red", "tok"), "wide"),
            P("wide", None, ("red", "tok")),
            P("wide", ("red", "tok")),
        ),
        out_specs=P(("grp", "tok"), ("red", "wide")),
        check_vma=False,
    )
```

```python
import functools
import math

import jax
import jax.numpy as jnp
from jax import lax
from jax.experimental import pallas as pl
from jax.experimental.pallas import tpu as pltpu
from jax.sharding import PartitionSpec as P

D = 6144
PATCHES = 256
EPS = 1e-06
SHARES = (8, 5, 3)
PIECES = (1, 1)
AHEAD = 4
GAIN_ROWS = 8
BF16, F32 = jnp.bfloat16, jnp.float32
PARAMS = pltpu.CompilerParams(vmem_limit_bytes=48 * 2**20)
SMALL = pltpu.CompilerParams(vmem_limit_bytes=8 * 2**20)
SOON = pl.CostEstimate(flops=0, bytes_accessed=0, transcendentals=0)


def normalize(values, mean, meansq, gain):
    return (values - mean) * lax.rsqrt(meansq - mean * mean + EPS) * gain.astype(F32)


def head_norm(values, gain):
    mean = jnp.mean(values, axis=-1, keepdims=True)
    meansq = jnp.mean(values * values, axis=-1, keepdims=True)
    return normalize(values, mean, meansq, gain)


def nothing(x):
    corner = x[(0,) * x.ndim].astype(jnp.int32)
    return lax.shift_right_logical(corner & 1, 1).astype(F32)


def slices(size, shares):
    ends = [sum(shares[: i + 1]) * size // sum(shares) for i in range(len(shares))]
    return [slice(a, b) for a, b in zip([0] + ends[:-1], ends)]


def steps_of(piece):
    size = math.gcd(piece.stop - piece.start, piece.start)
    block = next(b for b in (512, 384, 256, 128) if size % b == 0)
    return block, (piece.stop - piece.start) // block, piece.start // block


def corner_of(x):
    shape = (min(16, x.shape[0]), min(128, x.shape[1]))
    return pl.BlockSpec(shape, lambda *_: (0, 0))


def call(kernel, earlier, operands, specs, params=None, **options):
    def body(*refs):
        n = len(operands)
        kernel(refs[:n], refs[n + len(earlier) :])

    return pl.pallas_call(
        body,
        in_specs=list(specs) + [corner_of(a) for a in earlier],
        compiler_params=params or PARAMS,
        cost_estimate=SOON,
        **options,
    )(*operands, *earlier)


def gelu_sum(parts, earlier=()):
    rows, units = parts[0].shape
    block, steps, _ = steps_of(slice(0, units))
    spec = pl.BlockSpec((rows, block), lambda j: (0, j))

    def kernel(ins, outs):
        up = ins[0][...].astype(F32)
        for part in ins[1:]:
            up = up + part[...].astype(F32)
        outs[0][...] = (0.5 * up * (1.0 + lax.erf(up * 0.5**0.5))).astype(BF16)

    return call(
        kernel,
        earlier,
        parts,
        [spec] * len(parts),
        params=SMALL,
        grid=(steps,),
        out_specs=spec,
        out_shape=jax.ShapeDtypeStruct((rows, units), BF16),
    )


def sum_rows(near, far, cut, earlier=()):
    spec = pl.BlockSpec(near.shape, lambda *_: (0, 0))
    shape = (cut.stop - cut.start, near.shape[1])

    def kernel(ins, outs):
        outs[0][...] = (ins[0][cut].astype(F32) + ins[1][cut].astype(F32)).astype(BF16)

    return call(
        kernel,
        earlier,
        (near, far),
        [spec, spec],
        params=SMALL,
        grid=(1,),
        out_specs=pl.BlockSpec(shape, lambda *_: (0, 0)),
        out_shape=jax.ShapeDtypeStruct(shape, BF16),
    )


def side_by_side(kept, got, core, earlier=()):
    rows, columns = kept.shape
    spec = pl.BlockSpec(kept.shape, lambda *_: (0, 0))

    def kernel(ins, outs):
        first = ins[2][0] == 0
        outs[0][:, :columns] = jnp.where(first, ins[0][...], ins[1][...])
        outs[0][:, columns:] = jnp.where(first, ins[1][...], ins[0][...])

    return call(
        kernel,
        earlier,
        (kept, got, core.reshape(1)),
        [spec, spec, pl.BlockSpec(memory_space=pltpu.SMEM)],
        params=SMALL,
        grid=(1,),
        out_specs=pl.BlockSpec((rows, 2 * columns), lambda *_: (0, 0)),
        out_shape=jax.ShapeDtypeStruct((rows, 2 * columns), kept.dtype),
    )


def attend(parts, q_gain, k_gain, earlier=()):
    rows, width = parts[0].shape[0], q_gain.shape[1]
    n = len(parts)

    def kernel(ins, outs):
        def columns(at):
            here = slice(at * width, (at + 1) * width)
            return sum(part[:, here].astype(F32) for part in ins[:n])

        query = head_norm(columns(0), ins[n][...]).astype(BF16)
        key = head_norm(columns(1), ins[n + 1][...]).astype(BF16)
        value = columns(2).astype(BF16).astype(F32)
        for at in range(0, rows, PATCHES):
            image = slice(at, at + PATCHES)
            scores = lax.dot_general(
                query[image], key[image], (((1,), (1,)), ((), ())), preferred_element_type=F32
            )
            scores = scores * width ** (-0.5)
            weights = jnp.exp(scores - jnp.max(scores, axis=-1, keepdims=True))
            total = jnp.sum(weights, axis=-1, keepdims=True)
            acc = jnp.dot(
                weights,
                value[image],
                precision=lax.Precision.HIGHEST,
                preferred_element_type=F32,
            )
            outs[0][image] = (acc / total).astype(BF16)

    whole = [pl.BlockSpec(a.shape, lambda *_: (0, 0)) for a in (*parts, q_gain, k_gain)]
    return call(
        kernel,
        earlier,
        (*parts, q_gain, k_gain),
        whole,
        params=SMALL,
        grid=(1,),
        out_specs=pl.BlockSpec((rows, width), lambda *_: (0, 0)),
        out_shape=jax.ShapeDtypeStruct((rows, width), BF16),
    )


def project_rows(own, other, weight, piece, earlier=()):
    rows, depth = own.shape
    columns = piece.stop - piece.start
    block, steps, _ = steps_of(piece)
    whole = pl.BlockSpec((rows, depth), lambda *_: (0, 0))
    out = pl.BlockSpec((rows, columns), lambda *_: (0, 0))

    def kernel(ins, refs):
        near, far, both, landed, sems = refs

        def bring(at):
            start = pl.multiple_of(piece.start + at * block, block)
            source = ins[2].at[:, pl.ds(start, block)]
            return pltpu.make_async_copy(source, landed.at[at], sems.at[at])

        for at in range(min(AHEAD, steps)):
            bring(at).start()
        both[:rows] = ins[0][...]
        both[rows:] = ins[1][...]

        @pl.loop(0, steps)
        def _(at):
            bring(at).wait()

            @pl.when(at + AHEAD < steps)
            def _():
                bring(at + AHEAD).start()

            part = jnp.dot(both[...], landed[at], preferred_element_type=F32).astype(BF16)
            here = pl.ds(pl.multiple_of(at * block, block), block)
            near[:, here] = part[:rows]
            far[:, here] = part[rows:]

    return call(
        kernel,
        earlier,
        (own, other, weight),
        [whole, whole, pl.BlockSpec(memory_space=pltpu.HBM)],
        grid=(1,),
        out_specs=[out] * 2,
        out_shape=[jax.ShapeDtypeStruct((rows, columns), BF16)] * 2,
        scratch_shapes=[
            pltpu.VMEM((2 * rows, depth), BF16),
            pltpu.VMEM((steps, depth, block), BF16),
            pltpu.SemaphoreType.DMA((steps,)),
        ],
    )


def project_hidden(own, other, weight, piece, added, attention, last, earlier=()):
    rows, units = own.shape
    columns = weight.shape[1]
    block, steps, _ = steps_of(piece)
    whole = pl.BlockSpec((rows, columns), lambda *_: (0, 0))
    part = pl.BlockSpec((rows, units), lambda *_: (0, 0))
    specs = [part, part, pl.BlockSpec(memory_space=pltpu.HBM)]
    specs += [whole] * len(added)
    specs += [pl.BlockSpec(a.shape, lambda *_: (0, 0)) for a in attention]

    def kernel(ins, refs):
        outs, (both, total, landed, sems) = refs[:2], refs[2:]

        def bring(at):
            start = pl.multiple_of(piece.start + at * block, block)
            source = ins[2].at[pl.ds(start, block), :]
            return pltpu.make_async_copy(source, landed.at[at], sems.at[at])

        for at in range(min(AHEAD, steps)):
            bring(at).start()
        halves = (slice(0, rows), slice(rows, 2 * rows))
        for at, half in enumerate(halves):
            both[half] = ins[at][...]
            first = jnp.zeros((rows, columns), F32)
            if added:
                first = ins[3 + at][...]
            if attention:
                first = first + jnp.dot(
                    ins[-3 + at][...], ins[-1][...], preferred_element_type=F32
                )
            total[half] = first

        @pl.loop(0, steps)
        def _(at):
            bring(at).wait()

            @pl.when(at + AHEAD < steps)
            def _():
                bring(at + AHEAD).start()

            here = pl.ds(pl.multiple_of(at * block, block), block)
            total[...] += jnp.dot(both[:, here], landed[at], preferred_element_type=F32)

        for out, half in zip(outs, halves):
            out[...] = total[half].astype(out.dtype)

    return call(
        kernel,
        earlier,
        (own, other, weight, *added, *attention),
        specs,
        grid=(1,),
        out_specs=[whole] * 2,
        out_shape=[jax.ShapeDtypeStruct((rows, columns), BF16 if last else F32)] * 2,
        scratch_shapes=[
            pltpu.VMEM((2 * rows, units), BF16),
            pltpu.VMEM((2 * rows, columns), F32),
            pltpu.VMEM((steps, block, columns), BF16),
            pltpu.SemaphoreType.DMA((steps,)),
        ],
    )


def make_body(mesh):
    n_red, n_wide = mesh.shape["red"], mesh.shape["wide"]
    half_wide = n_wide // 2

    def swap(x):
        return lax.ppermute(x, "tok", [(0, 1), (1, 0)])

    def all_red(x):
        parts = [x]
        for shift in range(1, n_red):
            pairs = [(i, (i + shift) % n_red) for i in range(n_red)]
            parts.append(lax.ppermute(x, "red", pairs))
        return parts

    def sum_red(x):
        return sum(a.astype(F32) for a in all_red(x))

    def collect(kept, got, width):
        core, chip = lax.axis_index("tok"), lax.axis_index("wide")
        terms = jnp.concatenate([kept, got], axis=1)

        def block(at):
            start = ((at // half_wide) ^ core) * half_wide + at % half_wide
            return lax.dynamic_slice_in_dim(terms, start * width, width, axis=1)

        total = block(chip).astype(F32)
        for k in range(n_wide - 1, 0, -1):
            pairs = [(i, i ^ k) for i in range(n_wide)]
            total = total + lax.ppermute(block(chip ^ k), "wide", pairs).astype(F32)
        return total

    def body(tokens, ln_gain, q_gain, k_gain, w_qkv, w_up, w_attn, w_down):
        core = lax.axis_index("tok")
        width = tokens.shape[1]
        qkv_rows = w_qkv.reshape(w_qkv.shape[0], w_qkv.shape[1] * w_qkv.shape[2])
        attn_rows = w_attn.reshape(w_attn.shape[0] * w_attn.shape[1], w_attn.shape[2])
        depth, units = w_up.shape
        cuts = slices(tokens.shape[0], SHARES)
        pieces = slices(units, PIECES)
        n = len(cuts)

        first = cuts[0].stop
        gain_rows = jnp.broadcast_to(ln_gain[None], (GAIN_ROWS, width))
        lead = jnp.concatenate([gain_rows, tokens[:first]], axis=0)
        lead = lax.all_gather(lead, "wide", axis=1, tiled=True)
        gain = lead[:1]

        def normed(floats):
            sums = jnp.stack([jnp.sum(floats, axis=1), jnp.sum(floats * floats, axis=1)])
            sums = sum_red(sums)[:, :, None] / D
            values = normalize(floats, sums[0], sums[1], gain).astype(BF16)
            mine = lax.dynamic_slice_in_dim(values, core * depth, depth, axis=1)
            theirs = lax.dynamic_slice_in_dim(values, (1 - core) * depth, depth, axis=1)
            return mine, swap(theirs)

        def project(pair, weight):
            both = jnp.concatenate(pair, axis=0)
            half = both.shape[0] // 2
            part = jnp.dot(both, weight, preferred_element_type=F32)
            far = swap(part[half:].astype(BF16)).astype(F32)
            return (part[:half] + far).astype(BF16)

        weights = [w_up[:, piece] for piece in pieces]
        lead_pair = normed(lead[GAIN_ROWS:].astype(F32))
        leads = [project(lead_pair, weight) for weight in weights]
        lead_parts = [all_red(x) for x in leads]
        arrived = gelu_sum(lead_parts[0])

        rest = tokens[first:] + nothing(leads[-1]).astype(BF16)
        rest = lax.all_gather(rest, "wide", axis=1, tiled=True)
        rest_pair = normed(rest.astype(F32) + nothing(arrived))
        pair = [jnp.concatenate(p, axis=0) for p in zip(lead_pair, rest_pair)]
        near, far = project_rows(*pair, qkv_rows, slice(0, qkv_rows.shape[1]))
        halves, before = [], [near]
        qkv = sum_rows(near, swap(far), slice(0, tokens.shape[0]))
        for piece in pieces:
            near, far = project_rows(*rest_pair, w_up, piece, before)
            halves.append((near, swap(far)))
            before = [near]

        order = [(c, p) for c in range(n) for p in range(len(pieces))]
        outs, scattered = [], []
        terms, waiting = (), None
        earlier = [near, qkv]

        def output(at, have, terms, earlier):
            c, p = order[at]
            attention = ()
            if p == len(pieces) - 1:
                attention = (attended[cuts[c]], attended_other[cuts[c]], attn_rows)
            return project_hidden(
                have,
                swap(have),
                w_down,
                pieces[p],
                terms if p else (),
                attention,
                p == len(pieces) - 1,
                earlier,
            )

        def scatter(kept, got, earlier):
            full = side_by_side(kept, got, core, scattered[-1:] + earlier)
            scattered.append(lax.psum_scatter(full, "wide", scatter_dimension=1, tiled=True))
            return full

        hidden, ready = None, lead_parts
        for at, (c, p) in enumerate(order):
            if at:
                arrived = gelu_sum(ready[p], earlier)
                earlier = [arrived]
            if p == (0 if c else len(pieces) - 1) and c < n - 1:
                part = slice(cuts[c + 1].start - first, cuts[c + 1].stop - first)
                sums = [sum_rows(*half, part, [arrived]) for half in halves]
                coming = [all_red(x) for x in sums]
                earlier = earlier + sums
            if at == len(pieces):
                attended = attend(all_red(qkv), q_gain, k_gain, earlier)
                attended_other = swap(attended)
                earlier = [attended]
            if p == len(pieces) - 1 and c < n - 1:
                ready = coming
            if waiting is not None and not scattered:
                earlier.append(scatter(*waiting, earlier))
                waiting = None
            if at:
                terms = output(at - 1, hidden, terms, earlier)
                earlier = [terms[0]]
            if waiting is not None:
                earlier = [scatter(*waiting, earlier)]
                waiting = None
            if at and p == 0:
                waiting = (terms[0], swap(terms[1]))
            hidden = arrived
        terms = output(len(order) - 1, hidden, terms, earlier)
        for cut, summed in zip(cuts, scattered):
            outs.append(tokens[cut].astype(F32) + summed.astype(F32))
        outs.append(tokens[cuts[-1]].astype(F32) + collect(terms[0], swap(terms[1]), width))
        return jnp.concatenate(outs, axis=0)

    return body


def solution(mesh):
    return jax.shard_map(
        make_body(mesh),
        mesh=mesh,
        in_specs=(
            P(("grp", "tok"), ("red", "wide")),
            P(("red", "wide")),
            P("wide", None),
            P("wide", None),
            P(("red", "tok"), "wide", None),
            P(("red", "tok"), "wide"),
            P("wide", None, ("red", "tok")),
            P("wide", ("red", "tok")),
        ),
        out_specs=P(("grp", "tok"), ("red", "wide")),
        check_vma=False,
    )
```

```python
import functools
import math

import jax
import jax.numpy as jnp
from jax import lax
from jax.experimental import pallas as pl
from jax.experimental.pallas import tpu as pltpu
from jax.sharding import PartitionSpec as P

D = 6144
PATCHES = 256
EPS = 1e-06
SHARES = (10, 6)
LEAD_PIECES = (1, 1)
REST_PIECES = (2, 1)
AHEAD = 4
GAIN_ROWS = 8
BF16, F32 = jnp.bfloat16, jnp.float32
PARAMS = pltpu.CompilerParams(vmem_limit_bytes=48 * 2**20)
SMALL = pltpu.CompilerParams(vmem_limit_bytes=8 * 2**20)
SOON = pl.CostEstimate(flops=0, bytes_accessed=0, transcendentals=0)


def normalize(values, mean, meansq, gain):
    return (values - mean) * lax.rsqrt(meansq - mean * mean + EPS) * gain.astype(F32)


def head_norm(values, gain):
    mean = jnp.mean(values, axis=-1, keepdims=True)
    meansq = jnp.mean(values * values, axis=-1, keepdims=True)
    return normalize(values, mean, meansq, gain)


def nothing(x):
    corner = x[(0,) * x.ndim].astype(jnp.int32)
    return lax.shift_right_logical(corner & 1, 1).astype(F32)


def slices(size, shares):
    ends = [sum(shares[: i + 1]) * size // sum(shares) for i in range(len(shares))]
    return [slice(a, b) for a, b in zip([0] + ends[:-1], ends)]


def steps_of(piece):
    size = math.gcd(piece.stop - piece.start, piece.start)
    block = next(b for b in (512, 384, 256, 128) if size % b == 0)
    return block, (piece.stop - piece.start) // block, piece.start // block


def corner_of(x):
    shape = (min(16, x.shape[0]), min(128, x.shape[1]))
    return pl.BlockSpec(shape, lambda *_: (0, 0))


def call(kernel, earlier, operands, specs, params=None, **options):
    def body(*refs):
        n = len(operands)
        kernel(refs[:n], refs[n + len(earlier) :])

    return pl.pallas_call(
        body,
        in_specs=list(specs) + [corner_of(a) for a in earlier],
        compiler_params=params or PARAMS,
        cost_estimate=SOON,
        **options,
    )(*operands, *earlier)


def gelu_sum(parts, earlier=()):
    rows, units = parts[0].shape
    block, steps, _ = steps_of(slice(0, units))
    spec = pl.BlockSpec((rows, block), lambda j: (0, j))

    def kernel(ins, outs):
        up = ins[0][...].astype(F32)
        for part in ins[1:]:
            up = up + part[...].astype(F32)
        outs[0][...] = (0.5 * up * (1.0 + lax.erf(up * 0.5**0.5))).astype(BF16)

    return call(
        kernel,
        earlier,
        parts,
        [spec] * len(parts),
        params=SMALL,
        grid=(steps,),
        out_specs=spec,
        out_shape=jax.ShapeDtypeStruct((rows, units), BF16),
    )


def sum_rows(near, far, cut, earlier=()):
    spec = pl.BlockSpec(near.shape, lambda *_: (0, 0))
    shape = (cut.stop - cut.start, near.shape[1])

    def kernel(ins, outs):
        outs[0][...] = (ins[0][cut].astype(F32) + ins[1][cut].astype(F32)).astype(BF16)

    return call(
        kernel,
        earlier,
        (near, far),
        [spec, spec],
        params=SMALL,
        grid=(1,),
        out_specs=pl.BlockSpec(shape, lambda *_: (0, 0)),
        out_shape=jax.ShapeDtypeStruct(shape, BF16),
    )


def side_by_side(kept, got, core, earlier=()):
    rows, columns = kept.shape
    spec = pl.BlockSpec(kept.shape, lambda *_: (0, 0))

    def kernel(ins, outs):
        first = ins[2][0] == 0
        outs[0][:, :columns] = jnp.where(first, ins[0][...], ins[1][...])
        outs[0][:, columns:] = jnp.where(first, ins[1][...], ins[0][...])

    return call(
        kernel,
        earlier,
        (kept, got, core.reshape(1)),
        [spec, spec, pl.BlockSpec(memory_space=pltpu.SMEM)],
        params=SMALL,
        grid=(1,),
        out_specs=pl.BlockSpec((rows, 2 * columns), lambda *_: (0, 0)),
        out_shape=jax.ShapeDtypeStruct((rows, 2 * columns), kept.dtype),
    )


def attend(parts, q_gain, k_gain, earlier=()):
    rows, width = parts[0].shape[0], q_gain.shape[1]
    n = len(parts)

    def kernel(ins, outs):
        def columns(at):
            here = slice(at * width, (at + 1) * width)
            return sum(part[:, here].astype(F32) for part in ins[:n])

        query = head_norm(columns(0), ins[n][...]).astype(BF16)
        key = head_norm(columns(1), ins[n + 1][...]).astype(BF16)
        value = columns(2).astype(BF16).astype(F32)
        for at in range(0, rows, PATCHES):
            image = slice(at, at + PATCHES)
            scores = lax.dot_general(
                query[image], key[image], (((1,), (1,)), ((), ())), preferred_element_type=F32
            )
            scores = scores * width ** (-0.5)
            weights = jnp.exp(scores - jnp.max(scores, axis=-1, keepdims=True))
            total = jnp.sum(weights, axis=-1, keepdims=True)
            acc = jnp.dot(
                weights,
                value[image],
                precision=lax.Precision.HIGHEST,
                preferred_element_type=F32,
            )
            outs[0][image] = (acc / total).astype(BF16)

    whole = [pl.BlockSpec(a.shape, lambda *_: (0, 0)) for a in (*parts, q_gain, k_gain)]
    return call(
        kernel,
        earlier,
        (*parts, q_gain, k_gain),
        whole,
        params=SMALL,
        grid=(1,),
        out_specs=pl.BlockSpec((rows, width), lambda *_: (0, 0)),
        out_shape=jax.ShapeDtypeStruct((rows, width), BF16),
    )


def project_rows(own, other, weight, piece, earlier=()):
    rows, depth = own.shape
    columns = piece.stop - piece.start
    block, steps, _ = steps_of(piece)
    whole = pl.BlockSpec((rows, depth), lambda *_: (0, 0))
    out = pl.BlockSpec((rows, columns), lambda *_: (0, 0))

    def kernel(ins, refs):
        near, far, both, landed, sems = refs

        def bring(at):
            start = pl.multiple_of(piece.start + at * block, block)
            source = ins[2].at[:, pl.ds(start, block)]
            return pltpu.make_async_copy(source, landed.at[at], sems.at[at])

        for at in range(min(AHEAD, steps)):
            bring(at).start()
        both[:rows] = ins[0][...]
        both[rows:] = ins[1][...]

        @pl.loop(0, steps)
        def _(at):
            bring(at).wait()

            @pl.when(at + AHEAD < steps)
            def _():
                bring(at + AHEAD).start()

            part = jnp.dot(both[...], landed[at], preferred_element_type=F32).astype(BF16)
            here = pl.ds(pl.multiple_of(at * block, block), block)
            near[:, here] = part[:rows]
            far[:, here] = part[rows:]

    return call(
        kernel,
        earlier,
        (own, other, weight),
        [whole, whole, pl.BlockSpec(memory_space=pltpu.HBM)],
        grid=(1,),
        out_specs=[out] * 2,
        out_shape=[jax.ShapeDtypeStruct((rows, columns), BF16)] * 2,
        scratch_shapes=[
            pltpu.VMEM((2 * rows, depth), BF16),
            pltpu.VMEM((steps, depth, block), BF16),
            pltpu.SemaphoreType.DMA((steps,)),
        ],
    )


def project_hidden(own, other, weight, piece, added, attention, last, earlier=()):
    rows, units = own.shape
    columns = weight.shape[1]
    block, steps, _ = steps_of(piece)
    whole = pl.BlockSpec((rows, columns), lambda *_: (0, 0))
    part = pl.BlockSpec((rows, units), lambda *_: (0, 0))
    specs = [part, part, pl.BlockSpec(memory_space=pltpu.HBM)]
    specs += [whole] * len(added)
    specs += [pl.BlockSpec(a.shape, lambda *_: (0, 0)) for a in attention]

    def kernel(ins, refs):
        outs, (both, total, landed, sems) = refs[:2], refs[2:]

        def bring(at):
            start = pl.multiple_of(piece.start + at * block, block)
            source = ins[2].at[pl.ds(start, block), :]
            return pltpu.make_async_copy(source, landed.at[at], sems.at[at])

        for at in range(min(AHEAD, steps)):
            bring(at).start()
        halves = (slice(0, rows), slice(rows, 2 * rows))
        for at, half in enumerate(halves):
            both[half] = ins[at][...]
            first = jnp.zeros((rows, columns), F32)
            if added:
                first = ins[3 + at][...]
            if attention:
                first = first + jnp.dot(
                    ins[-3 + at][...], ins[-1][...], preferred_element_type=F32
                )
            total[half] = first

        @pl.loop(0, steps)
        def _(at):
            bring(at).wait()

            @pl.when(at + AHEAD < steps)
            def _():
                bring(at + AHEAD).start()

            here = pl.ds(pl.multiple_of(at * block, block), block)
            total[...] += jnp.dot(both[:, here], landed[at], preferred_element_type=F32)

        for out, half in zip(outs, halves):
            out[...] = total[half].astype(out.dtype)

    return call(
        kernel,
        earlier,
        (own, other, weight, *added, *attention),
        specs,
        grid=(1,),
        out_specs=[whole] * 2,
        out_shape=[jax.ShapeDtypeStruct((rows, columns), BF16 if last else F32)] * 2,
        scratch_shapes=[
            pltpu.VMEM((2 * rows, units), BF16),
            pltpu.VMEM((2 * rows, columns), F32),
            pltpu.VMEM((steps, block, columns), BF16),
            pltpu.SemaphoreType.DMA((steps,)),
        ],
    )


def make_body(mesh):
    n_red, n_wide = mesh.shape["red"], mesh.shape["wide"]
    half_wide = n_wide // 2

    def swap(x):
        return lax.ppermute(x, "tok", [(0, 1), (1, 0)])

    def all_red(x):
        parts = [x]
        for shift in range(1, n_red):
            pairs = [(i, (i + shift) % n_red) for i in range(n_red)]
            parts.append(lax.ppermute(x, "red", pairs))
        return parts

    def sum_red(x):
        return sum(a.astype(F32) for a in all_red(x))

    def collect(kept, got, width, start):
        core, chip = lax.axis_index("tok"), lax.axis_index("wide")
        terms = jnp.concatenate([kept, got], axis=1) + start.astype(BF16)

        def block(at):
            start = ((at // half_wide) ^ core) * half_wide + at % half_wide
            return lax.dynamic_slice_in_dim(terms, start * width, width, axis=1)

        total = block(chip).astype(F32)
        for k in range(n_wide - 1, 0, -1):
            pairs = [(i, i ^ k) for i in range(n_wide)]
            total = total + lax.ppermute(block(chip ^ k), "wide", pairs).astype(F32)
        return total

    def body(tokens, ln_gain, q_gain, k_gain, w_qkv, w_up, w_attn, w_down):
        core = lax.axis_index("tok")
        width = tokens.shape[1]
        qkv_rows = w_qkv.reshape(w_qkv.shape[0], w_qkv.shape[1] * w_qkv.shape[2])
        attn_rows = w_attn.reshape(w_attn.shape[0] * w_attn.shape[1], w_attn.shape[2])
        depth, units = w_up.shape
        cuts = slices(tokens.shape[0], SHARES)
        lead_pieces, rest_pieces = slices(units, LEAD_PIECES), slices(units, REST_PIECES)

        first = cuts[0].stop
        gain_rows = jnp.broadcast_to(ln_gain[None], (GAIN_ROWS, width))
        lead = jnp.concatenate([gain_rows, tokens[:first]], axis=0)
        lead = lax.all_gather(lead, "wide", axis=1, tiled=True)
        gain = lead[:1]

        def normed(floats):
            sums = jnp.stack([jnp.sum(floats, axis=1), jnp.sum(floats * floats, axis=1)])
            sums = sum_red(sums)[:, :, None] / D
            values = normalize(floats, sums[0], sums[1], gain).astype(BF16)
            mine = lax.dynamic_slice_in_dim(values, core * depth, depth, axis=1)
            theirs = lax.dynamic_slice_in_dim(values, (1 - core) * depth, depth, axis=1)
            return mine, swap(theirs)

        def project(pair, weight):
            both = jnp.concatenate(pair, axis=0)
            half = both.shape[0] // 2
            part = jnp.dot(both, weight, preferred_element_type=F32)
            far = swap(part[half:].astype(BF16)).astype(F32)
            return (part[:half] + far).astype(BF16)

        weights = [w_up[:, piece] for piece in lead_pieces]
        lead_pair = normed(lead[GAIN_ROWS:].astype(F32))
        leads = [project(lead_pair, weight) for weight in weights]
        lead_parts = [all_red(x) for x in leads]
        arrived = gelu_sum(lead_parts[0])

        rest = tokens[first:] + nothing(leads[-1]).astype(BF16)
        rest = lax.all_gather(rest, "wide", axis=1, tiled=True)
        rest_pair = normed(rest.astype(F32) + nothing(arrived))
        pair = [jnp.concatenate(p, axis=0) for p in zip(lead_pair, rest_pair)]
        near, far = project_rows(*pair, qkv_rows, slice(0, qkv_rows.shape[1]))
        halves, before = [], [near]
        qkv = sum_rows(near, swap(far), slice(0, tokens.shape[0]))
        for piece in rest_pieces:
            near, far = project_rows(*rest_pair, w_up, piece, before)
            halves.append((near, swap(far)))
            before = [near]

        def output(have, piece, terms, cut, earlier=()):
            last = piece.stop == units
            attention = (attended[cut], attended_other[cut], attn_rows) if last else ()
            return project_hidden(have, swap(have), w_down, piece, terms, attention, last, earlier)

        second = gelu_sum(lead_parts[1], [halves[-1][0], qkv])
        attended = attend(all_red(qkv), q_gain, k_gain, [second])
        sums = [sum_rows(*half, slice(0, half[0].shape[0]), [attended]) for half in halves]
        parts = [all_red(x) for x in sums]
        attended_other = swap(attended)

        terms = output(arrived, lead_pieces[0], (), cuts[0], sums)
        terms = output(second, lead_pieces[1], terms, cuts[0])
        full = side_by_side(terms[0], swap(terms[1]), core)
        scattered = lax.psum_scatter(full, "wide", scatter_dimension=1, tiled=True)

        hidden = gelu_sum(parts[0], [full])
        terms = output(hidden, rest_pieces[0], (), cuts[1])
        hidden = gelu_sum(parts[1], [terms[0]])
        kept, got = output(hidden, rest_pieces[1], terms, cuts[1])
        collected = collect(kept, swap(got), width, nothing(scattered))
        outs = [
            tokens[cuts[0]].astype(F32) + scattered.astype(F32),
            tokens[cuts[1]].astype(F32) + collected,
        ]
        return jnp.concatenate(outs, axis=0)

    return body


def solution(mesh):
    return jax.shard_map(
        make_body(mesh),
        mesh=mesh,
        in_specs=(
            P(("grp", "tok"), ("red", "wide")),
            P(("red", "wide")),
            P("wide", None),
            P("wide", None),
            P(("red", "tok"), "wide", None),
            P(("red", "tok"), "wide"),
            P("wide", None, ("red", "tok")),
            P("wide", ("red", "tok")),
        ),
        out_specs=P(("grp", "tok"), ("red", "wide")),
        check_vma=False,
    )
```

```python
import functools
import math

import jax
import jax.numpy as jnp
from jax import lax
from jax.experimental import pallas as pl
from jax.experimental.pallas import tpu as pltpu
from jax.sharding import PartitionSpec as P

D = 6144
PATCHES = 256
EPS = 1e-06
SHARES = (8, 5, 3)
PIECES = (1, 1)
AHEAD = 4
GAIN_ROWS = 8
BF16, F32 = jnp.bfloat16, jnp.float32
PARAMS = pltpu.CompilerParams(vmem_limit_bytes=48 * 2**20)
SMALL = pltpu.CompilerParams(vmem_limit_bytes=8 * 2**20)
SOON = pl.CostEstimate(flops=0, bytes_accessed=0, transcendentals=0)


def normalize(values, mean, meansq, gain):
    return (values - mean) * lax.rsqrt(meansq - mean * mean + EPS) * gain.astype(F32)


def head_norm(values, gain):
    mean = jnp.mean(values, axis=-1, keepdims=True)
    meansq = jnp.mean(values * values, axis=-1, keepdims=True)
    return normalize(values, mean, meansq, gain)


def nothing(x):
    corner = x[(0,) * x.ndim].astype(jnp.int32)
    return lax.shift_right_logical(corner & 1, 1).astype(F32)


def slices(size, shares):
    ends = [sum(shares[: i + 1]) * size // sum(shares) for i in range(len(shares))]
    return [slice(a, b) for a, b in zip([0] + ends[:-1], ends)]


def steps_of(piece):
    size = math.gcd(piece.stop - piece.start, piece.start)
    block = next(b for b in (512, 384, 256, 128) if size % b == 0)
    return block, (piece.stop - piece.start) // block, piece.start // block


def corner_of(x):
    shape = (min(16, x.shape[0]), min(128, x.shape[1]))
    return pl.BlockSpec(shape, lambda *_: (0, 0))


def call(kernel, earlier, operands, specs, params=None, **options):
    def body(*refs):
        n = len(operands)
        kernel(refs[:n], refs[n + len(earlier) :])

    return pl.pallas_call(
        body,
        in_specs=list(specs) + [corner_of(a) for a in earlier],
        compiler_params=params or PARAMS,
        cost_estimate=SOON,
        **options,
    )(*operands, *earlier)


def gelu_sum(parts, earlier=()):
    rows, units = parts[0].shape
    block, steps, _ = steps_of(slice(0, units))
    spec = pl.BlockSpec((rows, block), lambda j: (0, j))

    def kernel(ins, outs):
        up = ins[0][...].astype(F32)
        for part in ins[1:]:
            up = up + part[...].astype(F32)
        outs[0][...] = (0.5 * up * (1.0 + lax.erf(up * 0.5**0.5))).astype(BF16)

    return call(
        kernel,
        earlier,
        parts,
        [spec] * len(parts),
        params=SMALL,
        grid=(steps,),
        out_specs=spec,
        out_shape=jax.ShapeDtypeStruct((rows, units), BF16),
    )


def sum_rows(near, far, cut, earlier=()):
    spec = pl.BlockSpec(near.shape, lambda *_: (0, 0))
    shape = (cut.stop - cut.start, near.shape[1])

    def kernel(ins, outs):
        outs[0][...] = (ins[0][cut].astype(F32) + ins[1][cut].astype(F32)).astype(BF16)

    return call(
        kernel,
        earlier,
        (near, far),
        [spec, spec],
        params=SMALL,
        grid=(1,),
        out_specs=pl.BlockSpec(shape, lambda *_: (0, 0)),
        out_shape=jax.ShapeDtypeStruct(shape, BF16),
    )


def side_by_side(kept, got, core, earlier=()):
    rows, columns = kept.shape
    spec = pl.BlockSpec(kept.shape, lambda *_: (0, 0))

    def kernel(ins, outs):
        first = ins[2][0] == 0
        outs[0][:, :columns] = jnp.where(first, ins[0][...], ins[1][...])
        outs[0][:, columns:] = jnp.where(first, ins[1][...], ins[0][...])

    return call(
        kernel,
        earlier,
        (kept, got, core.reshape(1)),
        [spec, spec, pl.BlockSpec(memory_space=pltpu.SMEM)],
        params=SMALL,
        grid=(1,),
        out_specs=pl.BlockSpec((rows, 2 * columns), lambda *_: (0, 0)),
        out_shape=jax.ShapeDtypeStruct((rows, 2 * columns), kept.dtype),
    )


def attend(parts, q_gain, k_gain, earlier=()):
    rows, width = parts[0].shape[0], q_gain.shape[1]
    n = len(parts)

    def kernel(ins, outs):
        def columns(at):
            here = slice(at * width, (at + 1) * width)
            return sum(part[:, here].astype(F32) for part in ins[:n])

        query = head_norm(columns(0), ins[n][...]).astype(BF16)
        key = head_norm(columns(1), ins[n + 1][...]).astype(BF16)
        value = columns(2).astype(BF16).astype(F32)
        for at in range(0, rows, PATCHES):
            image = slice(at, at + PATCHES)
            scores = lax.dot_general(
                query[image], key[image], (((1,), (1,)), ((), ())), preferred_element_type=F32
            )
            scores = scores * width ** (-0.5)
            weights = jnp.exp(scores - jnp.max(scores, axis=-1, keepdims=True))
            total = jnp.sum(weights, axis=-1, keepdims=True)
            acc = jnp.dot(
                weights,
                value[image],
                precision=lax.Precision.HIGHEST,
                preferred_element_type=F32,
            )
            outs[0][image] = (acc / total).astype(BF16)

    whole = [pl.BlockSpec(a.shape, lambda *_: (0, 0)) for a in (*parts, q_gain, k_gain)]
    return call(
        kernel,
        earlier,
        (*parts, q_gain, k_gain),
        whole,
        params=SMALL,
        grid=(1,),
        out_specs=pl.BlockSpec((rows, width), lambda *_: (0, 0)),
        out_shape=jax.ShapeDtypeStruct((rows, width), BF16),
    )


def project_rows(own, other, weight, piece, earlier=()):
    rows, depth = own.shape
    columns = piece.stop - piece.start
    block, steps, _ = steps_of(piece)
    whole = pl.BlockSpec((rows, depth), lambda *_: (0, 0))
    out = pl.BlockSpec((rows, columns), lambda *_: (0, 0))

    def kernel(ins, refs):
        near, far, both, landed, sems = refs

        def bring(at):
            start = pl.multiple_of(piece.start + at * block, block)
            source = ins[2].at[:, pl.ds(start, block)]
            return pltpu.make_async_copy(source, landed.at[at], sems.at[at])

        for at in range(min(AHEAD, steps)):
            bring(at).start()
        both[:rows] = ins[0][...]
        both[rows:] = ins[1][...]

        @pl.loop(0, steps)
        def _(at):
            bring(at).wait()

            @pl.when(at + AHEAD < steps)
            def _():
                bring(at + AHEAD).start()

            part = jnp.dot(both[...], landed[at], preferred_element_type=F32).astype(BF16)
            here = pl.ds(pl.multiple_of(at * block, block), block)
            near[:, here] = part[:rows]
            far[:, here] = part[rows:]

    return call(
        kernel,
        earlier,
        (own, other, weight),
        [whole, whole, pl.BlockSpec(memory_space=pltpu.HBM)],
        grid=(1,),
        out_specs=[out] * 2,
        out_shape=[jax.ShapeDtypeStruct((rows, columns), BF16)] * 2,
        scratch_shapes=[
            pltpu.VMEM((2 * rows, depth), BF16),
            pltpu.VMEM((steps, depth, block), BF16),
            pltpu.SemaphoreType.DMA((steps,)),
        ],
    )


def project_hidden(own, other, weight, piece, added, attention, last, earlier=()):
    rows, units = own.shape
    columns = weight.shape[1]
    block, steps, _ = steps_of(piece)
    whole = pl.BlockSpec((rows, columns), lambda *_: (0, 0))
    part = pl.BlockSpec((rows, units), lambda *_: (0, 0))
    specs = [part, part, pl.BlockSpec(memory_space=pltpu.HBM)]
    specs += [whole] * len(added)
    specs += [pl.BlockSpec(a.shape, lambda *_: (0, 0)) for a in attention]

    def kernel(ins, refs):
        outs, (both, total, landed, sems) = refs[:2], refs[2:]

        def bring(at):
            start = pl.multiple_of(piece.start + at * block, block)
            source = ins[2].at[pl.ds(start, block), :]
            return pltpu.make_async_copy(source, landed.at[at], sems.at[at])

        for at in range(min(AHEAD, steps)):
            bring(at).start()
        halves = (slice(0, rows), slice(rows, 2 * rows))
        for at, half in enumerate(halves):
            both[half] = ins[at][...]
            first = jnp.zeros((rows, columns), F32)
            if added:
                first = ins[3 + at][...]
            if attention:
                first = first + jnp.dot(
                    ins[-3 + at][...], ins[-1][...], preferred_element_type=F32
                )
            total[half] = first

        @pl.loop(0, steps)
        def _(at):
            bring(at).wait()

            @pl.when(at + AHEAD < steps)
            def _():
                bring(at + AHEAD).start()

            here = pl.ds(pl.multiple_of(at * block, block), block)
            total[...] += jnp.dot(both[:, here], landed[at], preferred_element_type=F32)

        for out, half in zip(outs, halves):
            out[...] = total[half].astype(out.dtype)

    return call(
        kernel,
        earlier,
        (own, other, weight, *added, *attention),
        specs,
        grid=(1,),
        out_specs=[whole] * 2,
        out_shape=[jax.ShapeDtypeStruct((rows, columns), BF16 if last else F32)] * 2,
        scratch_shapes=[
            pltpu.VMEM((2 * rows, units), BF16),
            pltpu.VMEM((2 * rows, columns), F32),
            pltpu.VMEM((steps, block, columns), BF16),
            pltpu.SemaphoreType.DMA((steps,)),
        ],
    )


def make_body(mesh):
    n_red, n_wide = mesh.shape["red"], mesh.shape["wide"]
    half_wide = n_wide // 2

    def swap(x):
        return lax.ppermute(x, "tok", [(0, 1), (1, 0)])

    def all_red(x):
        parts = [x]
        for shift in range(1, n_red):
            pairs = [(i, (i + shift) % n_red) for i in range(n_red)]
            parts.append(lax.ppermute(x, "red", pairs))
        return parts

    def sum_red(x):
        return sum(a.astype(F32) for a in all_red(x))

    def collect(kept, got, width):
        core, chip = lax.axis_index("tok"), lax.axis_index("wide")
        terms = jnp.concatenate([kept, got], axis=1)

        def block(at):
            start = ((at // half_wide) ^ core) * half_wide + at % half_wide
            return lax.dynamic_slice_in_dim(terms, start * width, width, axis=1)

        total = block(chip).astype(F32)
        for k in range(n_wide - 1, 0, -1):
            pairs = [(i, i ^ k) for i in range(n_wide)]
            total = total + lax.ppermute(block(chip ^ k), "wide", pairs).astype(F32)
        return total

    def body(tokens, ln_gain, q_gain, k_gain, w_qkv, w_up, w_attn, w_down):
        core = lax.axis_index("tok")
        width = tokens.shape[1]
        qkv_rows = w_qkv.reshape(w_qkv.shape[0], w_qkv.shape[1] * w_qkv.shape[2])
        attn_rows = w_attn.reshape(w_attn.shape[0] * w_attn.shape[1], w_attn.shape[2])
        depth, units = w_up.shape
        cuts = slices(tokens.shape[0], SHARES)
        pieces = slices(units, PIECES)

        first = cuts[0].stop
        gain_rows = jnp.broadcast_to(ln_gain[None], (GAIN_ROWS, width))
        lead = jnp.concatenate([gain_rows, tokens[:first]], axis=0)
        lead = lax.all_gather(lead, "wide", axis=1, tiled=True)
        gain = lead[:1]

        def normed(floats):
            sums = jnp.stack([jnp.sum(floats, axis=1), jnp.sum(floats * floats, axis=1)])
            sums = sum_red(sums)[:, :, None] / D
            values = normalize(floats, sums[0], sums[1], gain).astype(BF16)
            mine = lax.dynamic_slice_in_dim(values, core * depth, depth, axis=1)
            theirs = lax.dynamic_slice_in_dim(values, (1 - core) * depth, depth, axis=1)
            return mine, swap(theirs)

        def project(pair, weight):
            both = jnp.concatenate(pair, axis=0)
            half = both.shape[0] // 2
            part = jnp.dot(both, weight, preferred_element_type=F32)
            far = swap(part[half:].astype(BF16)).astype(F32)
            return (part[:half] + far).astype(BF16)

        weights = [w_up[:, piece] for piece in pieces]
        lead_pair = normed(lead[GAIN_ROWS:].astype(F32))
        leads = [project(lead_pair, weight) for weight in weights]
        lead_parts = [all_red(x) for x in leads]
        arrived = gelu_sum(lead_parts[0])

        rest = tokens[first:] + nothing(leads[-1]).astype(BF16)
        rest = lax.all_gather(rest, "wide", axis=1, tiled=True)
        rest_pair = normed(rest.astype(F32) + nothing(arrived))
        pair = [jnp.concatenate(p, axis=0) for p in zip(lead_pair, rest_pair)]
        near, far = project_rows(*pair, qkv_rows, slice(0, qkv_rows.shape[1]))
        halves, before = [], [near]
        qkv = sum_rows(near, swap(far), slice(0, tokens.shape[0]))
        for piece in pieces:
            near, far = project_rows(*rest_pair, w_up, piece, before)
            halves.append((near, swap(far)))
            before = [near]

        def output(have, piece, terms, cut, earlier=()):
            last = piece.stop == units
            attention = (attended[cut], attended_other[cut], attn_rows) if last else ()
            return project_hidden(have, swap(have), w_down, piece, terms, attention, last, earlier)

        def chunk_sums(c, earlier):
            part = slice(cuts[c].start - first, cuts[c].stop - first)
            return [sum_rows(*half, part, [earlier]) for half in halves]

        def scatter(kept, got, earlier):
            full = side_by_side(kept, got, core, earlier)
            return full, lax.psum_scatter(full, "wide", scatter_dimension=1, tiled=True)

        attended = attend(all_red(qkv), q_gain, k_gain, [halves[-1][0]])
        attended_other = swap(attended)
        second = gelu_sum(lead_parts[1], [attended])
        sums = chunk_sums(1, second)
        parts = [all_red(x) for x in sums]
        terms = output(arrived, pieces[0], (), cuts[0], sums)
        terms = output(second, pieces[1], terms, cuts[0])
        waiting = terms[0], swap(terms[1])

        hidden = gelu_sum(parts[0], [terms[0]])
        full, got = scatter(*waiting, [hidden])
        scattered = [got]
        sums = chunk_sums(2, hidden)
        coming = [all_red(x) for x in sums]
        second = gelu_sum(parts[1], [full, *sums])
        terms = output(hidden, pieces[0], (), cuts[1], [second])

        hidden = gelu_sum(coming[0], [terms[0]])
        terms = output(second, pieces[1], terms, cuts[1], [hidden])
        waiting = terms[0], swap(terms[1])

        second = gelu_sum(coming[1], [terms[0]])
        full, got = scatter(*waiting, [second, scattered[0]])
        scattered.append(got)
        terms = output(hidden, pieces[0], (), cuts[2], [full])
        kept, sent = output(second, pieces[1], terms, cuts[2])
        outs = [tokens[cut].astype(F32) + got.astype(F32) for cut, got in zip(cuts, scattered)]
        outs.append(tokens[cuts[2]].astype(F32) + collect(kept, swap(sent), width))
        return jnp.concatenate(outs, axis=0)

    return body


def solution(mesh):
    return jax.shard_map(
        make_body(mesh),
        mesh=mesh,
        in_specs=(
            P(("grp", "tok"), ("red", "wide")),
            P(("red", "wide")),
            P("wide", None),
            P("wide", None),
            P(("red", "tok"), "wide", None),
            P(("red", "tok"), "wide"),
            P("wide", None, ("red", "tok")),
            P("wide", ("red", "tok")),
        ),
        out_specs=P(("grp", "tok"), ("red", "wide")),
        check_vma=False,
    )
```

```python
import functools
import math

import jax
import jax.numpy as jnp
from jax import lax
from jax.experimental import pallas as pl
from jax.experimental.pallas import tpu as pltpu
from jax.sharding import PartitionSpec as P

D = 6144
PATCHES = 256
EPS = 1e-06
SHARES = (8, 5, 3)
LEAD_PIECES = (1, 1)
REST_PIECES = (2, 1)
AHEAD = 4
GAIN_ROWS = 8
BF16, F32 = jnp.bfloat16, jnp.float32
PARAMS = pltpu.CompilerParams(vmem_limit_bytes=48 * 2**20)
SMALL = pltpu.CompilerParams(vmem_limit_bytes=8 * 2**20)
MIDDLE = pltpu.CompilerParams(vmem_limit_bytes=16 * 2**20)
SOON = pl.CostEstimate(flops=0, bytes_accessed=0, transcendentals=0)


def normalize(values, mean, meansq, gain):
    return (values - mean) * lax.rsqrt(meansq - mean * mean + EPS) * gain.astype(F32)


def head_norm(values, gain):
    mean = jnp.mean(values, axis=-1, keepdims=True)
    meansq = jnp.mean(values * values, axis=-1, keepdims=True)
    return normalize(values, mean, meansq, gain)


def nothing(x):
    corner = x[(0,) * x.ndim].astype(jnp.int32)
    return lax.shift_right_logical(corner & 1, 1).astype(F32)


def slices(size, shares, grain):
    ends = [sum(shares[: i + 1]) * size // sum(shares) for i in range(len(shares))]
    ends = [end // grain * grain for end in ends]
    return [slice(a, b) for a, b in zip([0] + ends[:-1], ends)]


def steps_of(piece):
    size = math.gcd(piece.stop - piece.start, piece.start)
    block = next(b for b in (512, 384, 256, 128) if size % b == 0)
    return block, (piece.stop - piece.start) // block, piece.start // block


def corner_of(x):
    shape = (min(16, x.shape[0]), min(128, x.shape[1]))
    return pl.BlockSpec(shape, lambda *_: (0, 0))


def call(kernel, earlier, operands, specs, params=None, **options):
    def body(*refs):
        n = len(operands)
        kernel(refs[:n], refs[n + len(earlier) :])

    return pl.pallas_call(
        body,
        in_specs=list(specs) + [corner_of(a) for a in earlier],
        compiler_params=params or PARAMS,
        cost_estimate=SOON,
        **options,
    )(*operands, *earlier)


def gelu_sum(parts, earlier=()):
    rows, units = parts[0].shape
    block, steps, _ = steps_of(slice(0, units))
    spec = pl.BlockSpec((rows, block), lambda j: (0, j))

    def kernel(ins, outs):
        up = ins[0][...].astype(F32)
        for part in ins[1:]:
            up = up + part[...].astype(F32)
        outs[0][...] = (0.5 * up * (1.0 + lax.erf(up * 0.5**0.5))).astype(BF16)

    return call(
        kernel,
        earlier,
        parts,
        [spec] * len(parts),
        params=SMALL,
        grid=(steps,),
        out_specs=spec,
        out_shape=jax.ShapeDtypeStruct((rows, units), BF16),
    )


def sum_rows(pairs, cut, earlier=()):
    widths = [near.shape[1] for near, _ in pairs]
    shape = (cut.stop - cut.start, sum(widths))

    def kernel(ins, outs):
        start = 0
        for at, width in enumerate(widths):
            total = ins[2 * at][cut].astype(F32) + ins[2 * at + 1][cut].astype(F32)
            outs[0][:, start : start + width] = total.astype(BF16)
            start += width

    operands = [part for pair in pairs for part in pair]
    return call(
        kernel,
        earlier,
        operands,
        [pl.BlockSpec(part.shape, lambda *_: (0, 0)) for part in operands],
        params=MIDDLE,
        grid=(1,),
        out_specs=pl.BlockSpec(shape, lambda *_: (0, 0)),
        out_shape=jax.ShapeDtypeStruct(shape, BF16),
    )


def side_by_side(kept, got, core, earlier=()):
    rows, columns = kept.shape
    spec = pl.BlockSpec(kept.shape, lambda *_: (0, 0))

    def kernel(ins, outs):
        first = ins[2][0] == 0
        outs[0][:, :columns] = jnp.where(first, ins[0][...], ins[1][...])
        outs[0][:, columns:] = jnp.where(first, ins[1][...], ins[0][...])

    return call(
        kernel,
        earlier,
        (kept, got, core.reshape(1)),
        [spec, spec, pl.BlockSpec(memory_space=pltpu.SMEM)],
        params=SMALL,
        grid=(1,),
        out_specs=pl.BlockSpec((rows, 2 * columns), lambda *_: (0, 0)),
        out_shape=jax.ShapeDtypeStruct((rows, 2 * columns), kept.dtype),
    )


def attend(parts, q_gain, k_gain, earlier=()):
    rows, width = parts[0].shape[0], q_gain.shape[1]
    n = len(parts)

    def kernel(ins, outs):
        def columns(at):
            here = slice(at * width, (at + 1) * width)
            return sum(part[:, here].astype(F32) for part in ins[:n])

        query = head_norm(columns(0), ins[n][...]).astype(BF16)
        key = head_norm(columns(1), ins[n + 1][...]).astype(BF16)
        value = columns(2).astype(BF16).astype(F32)
        for at in range(0, rows, PATCHES):
            image = slice(at, at + PATCHES)
            scores = lax.dot_general(
                query[image], key[image], (((1,), (1,)), ((), ())), preferred_element_type=F32
            )
            scores = scores * width ** (-0.5)
            weights = jnp.exp(scores - jnp.max(scores, axis=-1, keepdims=True))
            total = jnp.sum(weights, axis=-1, keepdims=True)
            acc = jnp.dot(
                weights,
                value[image],
                precision=lax.Precision.HIGHEST,
                preferred_element_type=F32,
            )
            outs[0][image] = (acc / total).astype(BF16)

    whole = [pl.BlockSpec(a.shape, lambda *_: (0, 0)) for a in (*parts, q_gain, k_gain)]
    return call(
        kernel,
        earlier,
        (*parts, q_gain, k_gain),
        whole,
        params=SMALL,
        grid=(1,),
        out_specs=pl.BlockSpec((rows, width), lambda *_: (0, 0)),
        out_shape=jax.ShapeDtypeStruct((rows, width), BF16),
    )


def project_rows(own, other, weight, piece, earlier=()):
    rows, depth = own.shape
    columns = piece.stop - piece.start
    block, steps, _ = steps_of(piece)
    whole = pl.BlockSpec((rows, depth), lambda *_: (0, 0))
    out = pl.BlockSpec((rows, columns), lambda *_: (0, 0))

    def kernel(ins, refs):
        near, far, both, landed, sems = refs

        def bring(at):
            start = pl.multiple_of(piece.start + at * block, block)
            source = ins[2].at[:, pl.ds(start, block)]
            return pltpu.make_async_copy(source, landed.at[at], sems.at[at])

        for at in range(min(AHEAD, steps)):
            bring(at).start()
        both[:rows] = ins[0][...]
        both[rows:] = ins[1][...]

        @pl.loop(0, steps)
        def _(at):
            bring(at).wait()

            @pl.when(at + AHEAD < steps)
            def _():
                bring(at + AHEAD).start()

            part = jnp.dot(both[...], landed[at], preferred_element_type=F32).astype(BF16)
            here = pl.ds(pl.multiple_of(at * block, block), block)
            near[:, here] = part[:rows]
            far[:, here] = part[rows:]

    return call(
        kernel,
        earlier,
        (own, other, weight),
        [whole, whole, pl.BlockSpec(memory_space=pltpu.HBM)],
        grid=(1,),
        out_specs=[out] * 2,
        out_shape=[jax.ShapeDtypeStruct((rows, columns), BF16)] * 2,
        scratch_shapes=[
            pltpu.VMEM((2 * rows, depth), BF16),
            pltpu.VMEM((steps, depth, block), BF16),
            pltpu.SemaphoreType.DMA((steps,)),
        ],
    )


def project_hidden(own, other, weight, piece, added, attention, last, earlier=()):
    rows, units = own.shape
    columns = weight.shape[1]
    block, steps, _ = steps_of(piece)
    whole = pl.BlockSpec((rows, columns), lambda *_: (0, 0))
    part = pl.BlockSpec((rows, units), lambda *_: (0, 0))
    specs = [part, part, pl.BlockSpec(memory_space=pltpu.HBM)]
    specs += [whole] * len(added)
    specs += [pl.BlockSpec(a.shape, lambda *_: (0, 0)) for a in attention]

    def kernel(ins, refs):
        outs, (both, total, landed, sems) = refs[:2], refs[2:]

        def bring(at):
            start = pl.multiple_of(piece.start + at * block, block)
            source = ins[2].at[pl.ds(start, block), :]
            return pltpu.make_async_copy(source, landed.at[at], sems.at[at])

        for at in range(min(AHEAD, steps)):
            bring(at).start()
        halves = (slice(0, rows), slice(rows, 2 * rows))
        for at, half in enumerate(halves):
            both[half] = ins[at][...]
            first = jnp.zeros((rows, columns), F32)
            if added:
                first = ins[3 + at][...]
            if attention:
                first = first + jnp.dot(
                    ins[-3 + at][...], ins[-1][...], preferred_element_type=F32
                )
            total[half] = first

        @pl.loop(0, steps)
        def _(at):
            bring(at).wait()

            @pl.when(at + AHEAD < steps)
            def _():
                bring(at + AHEAD).start()

            here = pl.ds(pl.multiple_of(at * block, block), block)
            total[...] += jnp.dot(both[:, here], landed[at], preferred_element_type=F32)

        for out, half in zip(outs, halves):
            out[...] = total[half].astype(out.dtype)

    return call(
        kernel,
        earlier,
        (own, other, weight, *added, *attention),
        specs,
        grid=(1,),
        out_specs=[whole] * 2,
        out_shape=[jax.ShapeDtypeStruct((rows, columns), BF16 if last else F32)] * 2,
        scratch_shapes=[
            pltpu.VMEM((2 * rows, units), BF16),
            pltpu.VMEM((2 * rows, columns), F32),
            pltpu.VMEM((steps, block, columns), BF16),
            pltpu.SemaphoreType.DMA((steps,)),
        ],
    )


def make_body(mesh):
    n_red, n_wide = mesh.shape["red"], mesh.shape["wide"]
    half_wide = n_wide // 2

    def swap(x):
        return lax.ppermute(x, "tok", [(0, 1), (1, 0)])

    def all_red(x):
        parts = [x]
        for shift in range(1, n_red):
            pairs = [(i, (i + shift) % n_red) for i in range(n_red)]
            parts.append(lax.ppermute(x, "red", pairs))
        return parts

    def sum_red(x):
        return sum(a.astype(F32) for a in all_red(x))

    def collect(kept, got, width):
        core, chip = lax.axis_index("tok"), lax.axis_index("wide")
        terms = jnp.concatenate([kept, got], axis=1)

        def block(at):
            start = ((at // half_wide) ^ core) * half_wide + at % half_wide
            return lax.dynamic_slice_in_dim(terms, start * width, width, axis=1)

        total = block(chip).astype(F32)
        for k in range(n_wide - 1, 0, -1):
            pairs = [(i, i ^ k) for i in range(n_wide)]
            total = total + lax.ppermute(block(chip ^ k), "wide", pairs).astype(F32)
        return total

    def body(tokens, ln_gain, q_gain, k_gain, w_qkv, w_up, w_attn, w_down):
        core = lax.axis_index("tok")
        width = tokens.shape[1]
        qkv_rows = w_qkv.reshape(w_qkv.shape[0], w_qkv.shape[1] * w_qkv.shape[2])
        attn_rows = w_attn.reshape(w_attn.shape[0] * w_attn.shape[1], w_attn.shape[2])
        depth, units = w_up.shape
        cuts = slices(tokens.shape[0], SHARES, 16)
        pieces = slices(units, LEAD_PIECES, 128)
        rest_pieces = slices(units, REST_PIECES, 128)

        first = cuts[0].stop
        gain_rows = jnp.broadcast_to(ln_gain[None], (GAIN_ROWS, width))
        lead = jnp.concatenate([gain_rows, tokens[:first]], axis=0)
        lead = lax.all_gather(lead, "wide", axis=1, tiled=True)
        gain = lead[:1]

        def normed(floats):
            sums = jnp.stack([jnp.sum(floats, axis=1), jnp.sum(floats * floats, axis=1)])
            sums = sum_red(sums)[:, :, None] / D
            values = normalize(floats, sums[0], sums[1], gain).astype(BF16)
            mine = lax.dynamic_slice_in_dim(values, core * depth, depth, axis=1)
            theirs = lax.dynamic_slice_in_dim(values, (1 - core) * depth, depth, axis=1)
            return mine, swap(theirs)

        def project(pair, weight):
            both = jnp.concatenate(pair, axis=0)
            half = both.shape[0] // 2
            part = jnp.dot(both, weight, preferred_element_type=F32)
            far = swap(part[half:].astype(BF16)).astype(F32)
            return (part[:half] + far).astype(BF16)

        weights = [w_up[:, piece] for piece in pieces]
        lead_pair = normed(lead[GAIN_ROWS:].astype(F32))
        leads = [project(lead_pair, weight) for weight in weights]
        lead_parts = [all_red(x) for x in leads]
        arrived = gelu_sum(lead_parts[0])

        rest = tokens[first:] + nothing(leads[-1]).astype(BF16)
        rest = lax.all_gather(rest, "wide", axis=1, tiled=True)
        rest_pair = normed(rest.astype(F32) + nothing(arrived))
        pair = [jnp.concatenate(p, axis=0) for p in zip(lead_pair, rest_pair)]
        near, far = project_rows(*pair, qkv_rows, slice(0, qkv_rows.shape[1]))
        halves, before = [], [near]
        qkv = sum_rows([(near, swap(far))], slice(0, tokens.shape[0]))
        for piece in rest_pieces:
            near, far = project_rows(*rest_pair, w_up, piece, before)
            halves.append((near, swap(far)))
            before = [near]

        def output(have, piece, terms, cut, earlier=()):
            last = piece.stop == units
            attention = (attended[cut], attended_other[cut], attn_rows) if last else ()
            return project_hidden(have, swap(have), w_down, piece, terms, attention, last, earlier)

        def chunk_sums(pairs, c, earlier):
            part = slice(cuts[c].start - first, cuts[c].stop - first)
            return sum_rows(pairs, part, [earlier])

        def scatter(kept, got, earlier):
            full = side_by_side(kept, got, core, earlier)
            return full, lax.psum_scatter(full, "wide", scatter_dimension=1, tiled=True)

        attended = attend(all_red(qkv), q_gain, k_gain, [halves[-1][0]])
        attended_other = swap(attended)
        second = gelu_sum(lead_parts[1], [attended])
        sums = chunk_sums(halves, 1, second)
        parts = all_red(sums)
        terms = output(arrived, pieces[0], (), cuts[0], [sums])
        coming = [chunk_sums([half], 2, terms[0]) for half in halves]
        terms = output(second, pieces[1], terms, cuts[0], coming)
        coming = [all_red(x) for x in coming]
        full, got = scatter(terms[0], swap(terms[1]), [])
        scattered = [got]

        hidden = gelu_sum(parts, [full])
        terms = output(hidden, slice(0, units), (), cuts[1])
        waiting = terms[0], swap(terms[1])

        hidden = gelu_sum(coming[0], [terms[0]])
        full, got = scatter(*waiting, [hidden, scattered[0]])
        scattered.append(got)
        terms = output(hidden, rest_pieces[0], (), cuts[2], [full])
        hidden = gelu_sum(coming[1], [terms[0]])
        kept, sent = output(hidden, rest_pieces[1], terms, cuts[2])
        outs = [tokens[cut].astype(F32) + got.astype(F32) for cut, got in zip(cuts, scattered)]
        outs.append(tokens[cuts[2]].astype(F32) + collect(kept, swap(sent), width))
        return jnp.concatenate(outs, axis=0)

    return body


def solution(mesh):
    return jax.shard_map(
        make_body(mesh),
        mesh=mesh,
        in_specs=(
            P(("grp", "tok"), ("red", "wide")),
            P(("red", "wide")),
            P("wide", None),
            P("wide", None),
            P(("red", "tok"), "wide", None),
            P(("red", "tok"), "wide"),
            P("wide", None, ("red", "tok")),
            P("wide", ("red", "tok")),
        ),
        out_specs=P(("grp", "tok"), ("red", "wide")),
        check_vma=False,
    )
```

```python
import functools
import math

import jax
import jax.numpy as jnp
from jax import lax
from jax.experimental import pallas as pl
from jax.experimental.pallas import tpu as pltpu
from jax.sharding import PartitionSpec as P

D = 6144
PATCHES = 256
EPS = 1e-06
SHARES = (8, 5, 3)
LEAD_PIECES = (1, 1)
REST_PIECES = (2, 1)
AHEAD = 4
GAIN_ROWS = 8
BF16, F32 = jnp.bfloat16, jnp.float32
PARAMS = pltpu.CompilerParams(vmem_limit_bytes=48 * 2**20)
SMALL = pltpu.CompilerParams(vmem_limit_bytes=8 * 2**20)
MIDDLE = pltpu.CompilerParams(vmem_limit_bytes=16 * 2**20)
SOON = pl.CostEstimate(flops=0, bytes_accessed=0, transcendentals=0)


def normalize(values, mean, meansq, gain):
    return (values - mean) * lax.rsqrt(meansq - mean * mean + EPS) * gain.astype(F32)


def head_norm(values, gain):
    mean = jnp.mean(values, axis=-1, keepdims=True)
    meansq = jnp.mean(values * values, axis=-1, keepdims=True)
    return normalize(values, mean, meansq, gain)


def nothing(x):
    corner = x[(0,) * x.ndim].astype(jnp.int32)
    return lax.shift_right_logical(corner & 1, 1).astype(F32)


def slices(size, shares, grain):
    ends = [sum(shares[: i + 1]) * size // sum(shares) for i in range(len(shares))]
    ends = [end // grain * grain for end in ends]
    return [slice(a, b) for a, b in zip([0] + ends[:-1], ends)]


def steps_of(piece):
    size = math.gcd(piece.stop - piece.start, piece.start)
    block = next(b for b in (512, 384, 256, 128) if size % b == 0)
    return block, (piece.stop - piece.start) // block, piece.start // block


def corner_of(x):
    shape = (min(16, x.shape[0]), min(128, x.shape[1]))
    return pl.BlockSpec(shape, lambda *_: (0, 0))


def call(kernel, earlier, operands, specs, params=None, **options):
    def body(*refs):
        n = len(operands)
        kernel(refs[:n], refs[n + len(earlier) :])

    return pl.pallas_call(
        body,
        in_specs=list(specs) + [corner_of(a) for a in earlier],
        compiler_params=params or PARAMS,
        cost_estimate=SOON,
        **options,
    )(*operands, *earlier)


def gelu_sum(parts, earlier=()):
    rows, units = parts[0].shape
    block, steps, _ = steps_of(slice(0, units))
    spec = pl.BlockSpec((rows, block), lambda j: (0, j))

    def kernel(ins, outs):
        up = ins[0][...].astype(F32)
        for part in ins[1:]:
            up = up + part[...].astype(F32)
        outs[0][...] = (0.5 * up * (1.0 + lax.erf(up * 0.5**0.5))).astype(BF16)

    return call(
        kernel,
        earlier,
        parts,
        [spec] * len(parts),
        params=SMALL,
        grid=(steps,),
        out_specs=spec,
        out_shape=jax.ShapeDtypeStruct((rows, units), BF16),
    )


def sum_rows(pairs, cut, earlier=()):
    widths = [near.shape[1] for near, _ in pairs]
    shape = (cut.stop - cut.start, sum(widths))

    def kernel(ins, outs):
        start = 0
        for at, width in enumerate(widths):
            total = ins[2 * at][cut].astype(F32) + ins[2 * at + 1][cut].astype(F32)
            outs[0][:, start : start + width] = total.astype(BF16)
            start += width

    operands = [part for pair in pairs for part in pair]
    return call(
        kernel,
        earlier,
        operands,
        [pl.BlockSpec(part.shape, lambda *_: (0, 0)) for part in operands],
        params=MIDDLE,
        grid=(1,),
        out_specs=pl.BlockSpec(shape, lambda *_: (0, 0)),
        out_shape=jax.ShapeDtypeStruct(shape, BF16),
    )


def side_by_side(kept, got, core, earlier=()):
    rows, columns = kept.shape
    spec = pl.BlockSpec(kept.shape, lambda *_: (0, 0))

    def kernel(ins, outs):
        first = ins[2][0] == 0
        outs[0][:, :columns] = jnp.where(first, ins[0][...], ins[1][...])
        outs[0][:, columns:] = jnp.where(first, ins[1][...], ins[0][...])

    return call(
        kernel,
        earlier,
        (kept, got, core.reshape(1)),
        [spec, spec, pl.BlockSpec(memory_space=pltpu.SMEM)],
        params=SMALL,
        grid=(1,),
        out_specs=pl.BlockSpec((rows, 2 * columns), lambda *_: (0, 0)),
        out_shape=jax.ShapeDtypeStruct((rows, 2 * columns), kept.dtype),
    )


def attend(parts, q_gain, k_gain, earlier=()):
    rows, width = parts[0].shape[0], q_gain.shape[1]
    n = len(parts)

    def kernel(ins, outs):
        def columns(at):
            here = slice(at * width, (at + 1) * width)
            return sum(part[:, here].astype(F32) for part in ins[:n])

        query = head_norm(columns(0), ins[n][...]).astype(BF16)
        key = head_norm(columns(1), ins[n + 1][...]).astype(BF16)
        value = columns(2).astype(BF16).astype(F32)
        for at in range(0, rows, PATCHES):
            image = slice(at, at + PATCHES)
            scores = lax.dot_general(
                query[image], key[image], (((1,), (1,)), ((), ())), preferred_element_type=F32
            )
            scores = scores * width ** (-0.5)
            weights = jnp.exp(scores - jnp.max(scores, axis=-1, keepdims=True))
            total = jnp.sum(weights, axis=-1, keepdims=True)
            acc = jnp.dot(
                weights,
                value[image],
                precision=lax.Precision.HIGHEST,
                preferred_element_type=F32,
            )
            outs[0][image] = (acc / total).astype(BF16)

    whole = [pl.BlockSpec(a.shape, lambda *_: (0, 0)) for a in (*parts, q_gain, k_gain)]
    return call(
        kernel,
        earlier,
        (*parts, q_gain, k_gain),
        whole,
        params=SMALL,
        grid=(1,),
        out_specs=pl.BlockSpec((rows, width), lambda *_: (0, 0)),
        out_shape=jax.ShapeDtypeStruct((rows, width), BF16),
    )


def project_rows(own, other, weight, piece, earlier=()):
    rows, depth = own.shape
    columns = piece.stop - piece.start
    block, steps, _ = steps_of(piece)
    whole = pl.BlockSpec((rows, depth), lambda *_: (0, 0))
    out = pl.BlockSpec((rows, columns), lambda *_: (0, 0))

    def kernel(ins, refs):
        near, far, both, landed, sems = refs

        def bring(at):
            start = pl.multiple_of(piece.start + at * block, block)
            source = ins[2].at[:, pl.ds(start, block)]
            return pltpu.make_async_copy(source, landed.at[at], sems.at[at])

        for at in range(min(AHEAD, steps)):
            bring(at).start()
        both[:rows] = ins[0][...]
        both[rows:] = ins[1][...]

        @pl.loop(0, steps)
        def _(at):
            bring(at).wait()

            @pl.when(at + AHEAD < steps)
            def _():
                bring(at + AHEAD).start()

            part = jnp.dot(both[...], landed[at], preferred_element_type=F32).astype(BF16)
            here = pl.ds(pl.multiple_of(at * block, block), block)
            near[:, here] = part[:rows]
            far[:, here] = part[rows:]

    return call(
        kernel,
        earlier,
        (own, other, weight),
        [whole, whole, pl.BlockSpec(memory_space=pltpu.HBM)],
        grid=(1,),
        out_specs=[out] * 2,
        out_shape=[jax.ShapeDtypeStruct((rows, columns), BF16)] * 2,
        scratch_shapes=[
            pltpu.VMEM((2 * rows, depth), BF16),
            pltpu.VMEM((steps, depth, block), BF16),
            pltpu.SemaphoreType.DMA((steps,)),
        ],
    )


def project_hidden(own, other, weight, piece, added, attention, last, earlier=()):
    rows, units = own.shape
    columns = weight.shape[1]
    block, steps, _ = steps_of(piece)
    whole = pl.BlockSpec((rows, columns), lambda *_: (0, 0))
    part = pl.BlockSpec((rows, units), lambda *_: (0, 0))
    specs = [part, part, pl.BlockSpec(memory_space=pltpu.HBM)]
    specs += [whole] * len(added)
    specs += [pl.BlockSpec(a.shape, lambda *_: (0, 0)) for a in attention]

    def kernel(ins, refs):
        outs, (both, total, landed, sems) = refs[:2], refs[2:]

        def bring(at):
            start = pl.multiple_of(piece.start + at * block, block)
            source = ins[2].at[pl.ds(start, block), :]
            return pltpu.make_async_copy(source, landed.at[at], sems.at[at])

        for at in range(min(AHEAD, steps)):
            bring(at).start()
        halves = (slice(0, rows), slice(rows, 2 * rows))
        for at, half in enumerate(halves):
            both[half] = ins[at][...]
            first = jnp.zeros((rows, columns), F32)
            if added:
                first = ins[3 + at][...]
            if attention:
                first = first + jnp.dot(
                    ins[-3 + at][...], ins[-1][...], preferred_element_type=F32
                )
            total[half] = first

        @pl.loop(0, steps)
        def _(at):
            bring(at).wait()

            @pl.when(at + AHEAD < steps)
            def _():
                bring(at + AHEAD).start()

            here = pl.ds(pl.multiple_of(at * block, block), block)
            total[...] += jnp.dot(both[:, here], landed[at], preferred_element_type=F32)

        for out, half in zip(outs, halves):
            out[...] = total[half].astype(out.dtype)

    return call(
        kernel,
        earlier,
        (own, other, weight, *added, *attention),
        specs,
        grid=(1,),
        out_specs=[whole] * 2,
        out_shape=[jax.ShapeDtypeStruct((rows, columns), BF16 if last else F32)] * 2,
        scratch_shapes=[
            pltpu.VMEM((2 * rows, units), BF16),
            pltpu.VMEM((2 * rows, columns), F32),
            pltpu.VMEM((steps, block, columns), BF16),
            pltpu.SemaphoreType.DMA((steps,)),
        ],
    )


def make_body(mesh):
    n_red, n_wide = mesh.shape["red"], mesh.shape["wide"]
    half_wide = n_wide // 2

    def swap(x):
        return lax.ppermute(x, "tok", [(0, 1), (1, 0)])

    def all_red(x):
        parts = [x]
        for shift in range(1, n_red):
            pairs = [(i, (i + shift) % n_red) for i in range(n_red)]
            parts.append(lax.ppermute(x, "red", pairs))
        return parts

    def sum_red(x):
        return sum(a.astype(F32) for a in all_red(x))

    def collect(kept, got, width):
        core, chip = lax.axis_index("tok"), lax.axis_index("wide")
        terms = jnp.concatenate([kept, got], axis=1)

        def block(at):
            start = ((at // half_wide) ^ core) * half_wide + at % half_wide
            return lax.dynamic_slice_in_dim(terms, start * width, width, axis=1)

        total = block(chip).astype(F32)
        for k in range(n_wide - 1, 0, -1):
            pairs = [(i, i ^ k) for i in range(n_wide)]
            total = total + lax.ppermute(block(chip ^ k), "wide", pairs).astype(F32)
        return total

    def body(tokens, ln_gain, q_gain, k_gain, w_qkv, w_up, w_attn, w_down):
        core = lax.axis_index("tok")
        width = tokens.shape[1]
        qkv_rows = w_qkv.reshape(w_qkv.shape[0], w_qkv.shape[1] * w_qkv.shape[2])
        attn_rows = w_attn.reshape(w_attn.shape[0] * w_attn.shape[1], w_attn.shape[2])
        depth, units = w_up.shape
        cuts = slices(tokens.shape[0], SHARES, 16)
        pieces = slices(units, LEAD_PIECES, 128)
        rest_pieces = slices(units, REST_PIECES, 128)

        first = cuts[0].stop
        gain_rows = jnp.broadcast_to(ln_gain[None], (GAIN_ROWS, width))
        lead = jnp.concatenate([gain_rows, tokens[:first]], axis=0)
        lead = lax.all_gather(lead, "wide", axis=1, tiled=True)
        gain = lead[:1]

        def normed(floats):
            sums = jnp.stack([jnp.sum(floats, axis=1), jnp.sum(floats * floats, axis=1)])
            sums = sum_red(sums)[:, :, None] / D
            values = normalize(floats, sums[0], sums[1], gain).astype(BF16)
            mine = lax.dynamic_slice_in_dim(values, core * depth, depth, axis=1)
            theirs = lax.dynamic_slice_in_dim(values, (1 - core) * depth, depth, axis=1)
            return mine, swap(theirs)

        def project(pair, weight):
            both = jnp.concatenate(pair, axis=0)
            half = both.shape[0] // 2
            part = jnp.dot(both, weight, preferred_element_type=F32)
            far = swap(part[half:].astype(BF16)).astype(F32)
            return (part[:half] + far).astype(BF16)

        weights = [w_up[:, piece] for piece in pieces]
        lead_pair = normed(lead[GAIN_ROWS:].astype(F32))
        leads = [project(lead_pair, weight) for weight in weights]
        lead_parts = [all_red(x) for x in leads]
        arrived = gelu_sum(lead_parts[0])

        rest = tokens[first:] + nothing(leads[-1]).astype(BF16)
        rest = lax.all_gather(rest, "wide", axis=1, tiled=True)
        rest_pair = normed(rest.astype(F32) + nothing(arrived))
        pair = [jnp.concatenate(p, axis=0) for p in zip(lead_pair, rest_pair)]
        near, far = project_rows(*pair, qkv_rows, slice(0, qkv_rows.shape[1]))
        halves, before = [], [near]
        qkv = sum_rows([(near, swap(far))], slice(0, tokens.shape[0]))
        for piece in rest_pieces:
            near, far = project_rows(*rest_pair, w_up, piece, before)
            halves.append((near, swap(far)))
            before = [near]

        def output(have, piece, terms, cut, earlier=()):
            last = piece.stop == units
            attention = (attended[cut], attended_other[cut], attn_rows) if last else ()
            return project_hidden(have, swap(have), w_down, piece, terms, attention, last, earlier)

        def chunk_sums(pairs, c, earlier):
            part = slice(cuts[c].start - first, cuts[c].stop - first)
            return sum_rows(pairs, part, [earlier])

        def scatter(kept, got, earlier):
            full = side_by_side(kept, got, core, earlier)
            return full, lax.psum_scatter(full, "wide", scatter_dimension=1, tiled=True)

        attended = attend(all_red(qkv), q_gain, k_gain, [halves[-1][0]])
        attended_other = swap(attended)
        second = gelu_sum(lead_parts[1], [attended])
        sums = chunk_sums(halves, 1, second)
        parts = all_red(sums)
        terms = output(arrived, pieces[0], (), cuts[0], [sums])
        coming = chunk_sums(halves, 2, terms[0])
        terms = output(second, pieces[1], terms, cuts[0], [coming])
        coming = all_red(coming)
        full, got = scatter(terms[0], swap(terms[1]), [])
        scattered = [got]

        hidden = gelu_sum(parts, [full])
        terms = output(hidden, slice(0, units), (), cuts[1])
        full, got = scatter(terms[0], swap(terms[1]), [scattered[0]])
        scattered.append(got)

        hidden = gelu_sum(coming, [full])
        kept, sent = output(hidden, slice(0, units), (), cuts[2])
        outs = [tokens[cut].astype(F32) + got.astype(F32) for cut, got in zip(cuts, scattered)]
        outs.append(tokens[cuts[2]].astype(F32) + collect(kept, swap(sent), width))
        return jnp.concatenate(outs, axis=0)

    return body


def solution(mesh):
    return jax.shard_map(
        make_body(mesh),
        mesh=mesh,
        in_specs=(
            P(("grp", "tok"), ("red", "wide")),
            P(("red", "wide")),
            P("wide", None),
            P("wide", None),
            P(("red", "tok"), "wide", None),
            P(("red", "tok"), "wide"),
            P("wide", None, ("red", "tok")),
            P("wide", ("red", "tok")),
        ),
        out_specs=P(("grp", "tok"), ("red", "wide")),
        check_vma=False,
    )
```

```python
import functools
import math

import jax
import jax.numpy as jnp
from jax import lax
from jax.experimental import pallas as pl
from jax.experimental.pallas import tpu as pltpu
from jax.sharding import PartitionSpec as P

D = 6144
PATCHES = 256
EPS = 1e-06
SHARES = (8, 5, 3)
LEAD_PIECES = (1, 1)
REST_PIECES = (2, 1)
AHEAD = 4
GAIN_ROWS = 8
BF16, F32 = jnp.bfloat16, jnp.float32
PARAMS = pltpu.CompilerParams(vmem_limit_bytes=48 * 2**20)
SMALL = pltpu.CompilerParams(vmem_limit_bytes=8 * 2**20)
MIDDLE = pltpu.CompilerParams(vmem_limit_bytes=16 * 2**20)
SOON = pl.CostEstimate(flops=0, bytes_accessed=0, transcendentals=0)


def normalize(values, mean, meansq, gain):
    return (values - mean) * lax.rsqrt(meansq - mean * mean + EPS) * gain.astype(F32)


def head_norm(values, gain):
    mean = jnp.mean(values, axis=-1, keepdims=True)
    meansq = jnp.mean(values * values, axis=-1, keepdims=True)
    return normalize(values, mean, meansq, gain)


def nothing(x):
    corner = x[(0,) * x.ndim].astype(jnp.int32)
    return lax.shift_right_logical(corner & 1, 1).astype(F32)


def slices(size, shares, grain):
    ends = [sum(shares[: i + 1]) * size // sum(shares) for i in range(len(shares))]
    ends = [end // grain * grain for end in ends]
    return [slice(a, b) for a, b in zip([0] + ends[:-1], ends)]


def steps_of(piece):
    size = math.gcd(piece.stop - piece.start, piece.start)
    block = next(b for b in (512, 384, 256, 128) if size % b == 0)
    return block, (piece.stop - piece.start) // block, piece.start // block


def corner_of(x):
    shape = (min(16, x.shape[0]), min(128, x.shape[1]))
    return pl.BlockSpec(shape, lambda *_: (0, 0))


def call(kernel, earlier, operands, specs, params=None, **options):
    def body(*refs):
        n = len(operands)
        kernel(refs[:n], refs[n + len(earlier) :])

    return pl.pallas_call(
        body,
        in_specs=list(specs) + [corner_of(a) for a in earlier],
        compiler_params=params or PARAMS,
        cost_estimate=SOON,
        **options,
    )(*operands, *earlier)


def gelu_sum(parts, earlier=()):
    rows, units = parts[0].shape
    block, steps, _ = steps_of(slice(0, units))
    spec = pl.BlockSpec((rows, block), lambda j: (0, j))

    def kernel(ins, outs):
        up = ins[0][...].astype(F32)
        for part in ins[1:]:
            up = up + part[...].astype(F32)
        outs[0][...] = (0.5 * up * (1.0 + lax.erf(up * 0.5**0.5))).astype(BF16)

    return call(
        kernel,
        earlier,
        parts,
        [spec] * len(parts),
        params=SMALL,
        grid=(steps,),
        out_specs=spec,
        out_shape=jax.ShapeDtypeStruct((rows, units), BF16),
    )


def sum_rows(pairs, cut, earlier=()):
    widths = [near.shape[1] for near, _ in pairs]
    shape = (cut.stop - cut.start, sum(widths))

    def kernel(ins, outs):
        start = 0
        for at, width in enumerate(widths):
            total = ins[2 * at][cut].astype(F32) + ins[2 * at + 1][cut].astype(F32)
            outs[0][:, start : start + width] = total.astype(BF16)
            start += width

    operands = [part for pair in pairs for part in pair]
    return call(
        kernel,
        earlier,
        operands,
        [pl.BlockSpec(part.shape, lambda *_: (0, 0)) for part in operands],
        params=MIDDLE,
        grid=(1,),
        out_specs=pl.BlockSpec(shape, lambda *_: (0, 0)),
        out_shape=jax.ShapeDtypeStruct(shape, BF16),
    )


def side_by_side(kept, got, core, earlier=()):
    rows, columns = kept.shape
    spec = pl.BlockSpec(kept.shape, lambda *_: (0, 0))

    def kernel(ins, outs):
        first = ins[2][0] == 0
        outs[0][:, :columns] = jnp.where(first, ins[0][...], ins[1][...])
        outs[0][:, columns:] = jnp.where(first, ins[1][...], ins[0][...])

    return call(
        kernel,
        earlier,
        (kept, got, core.reshape(1)),
        [spec, spec, pl.BlockSpec(memory_space=pltpu.SMEM)],
        params=SMALL,
        grid=(1,),
        out_specs=pl.BlockSpec((rows, 2 * columns), lambda *_: (0, 0)),
        out_shape=jax.ShapeDtypeStruct((rows, 2 * columns), kept.dtype),
    )


def attend(parts, q_gain, k_gain, earlier=()):
    rows, width = parts[0].shape[0], q_gain.shape[1]
    n = len(parts)

    def kernel(ins, outs):
        def columns(at):
            here = slice(at * width, (at + 1) * width)
            return sum(part[:, here].astype(F32) for part in ins[:n])

        query = head_norm(columns(0), ins[n][...]).astype(BF16)
        key = head_norm(columns(1), ins[n + 1][...]).astype(BF16)
        value = columns(2).astype(BF16).astype(F32)
        for at in range(0, rows, PATCHES):
            image = slice(at, at + PATCHES)
            scores = lax.dot_general(
                query[image], key[image], (((1,), (1,)), ((), ())), preferred_element_type=F32
            )
            scores = scores * width ** (-0.5)
            weights = jnp.exp(scores - jnp.max(scores, axis=-1, keepdims=True))
            total = jnp.sum(weights, axis=-1, keepdims=True)
            acc = jnp.dot(
                weights,
                value[image],
                precision=lax.Precision.HIGHEST,
                preferred_element_type=F32,
            )
            outs[0][image] = (acc / total).astype(BF16)

    whole = [pl.BlockSpec(a.shape, lambda *_: (0, 0)) for a in (*parts, q_gain, k_gain)]
    return call(
        kernel,
        earlier,
        (*parts, q_gain, k_gain),
        whole,
        params=SMALL,
        grid=(1,),
        out_specs=pl.BlockSpec((rows, width), lambda *_: (0, 0)),
        out_shape=jax.ShapeDtypeStruct((rows, width), BF16),
    )


def project_rows(own, other, weight, piece, earlier=()):
    rows, depth = own.shape
    columns = piece.stop - piece.start
    block, steps, _ = steps_of(piece)
    whole = pl.BlockSpec((rows, depth), lambda *_: (0, 0))
    out = pl.BlockSpec((rows, columns), lambda *_: (0, 0))

    def kernel(ins, refs):
        near, far, both, landed, sems = refs

        def bring(at):
            start = pl.multiple_of(piece.start + at * block, block)
            source = ins[2].at[:, pl.ds(start, block)]
            return pltpu.make_async_copy(source, landed.at[at], sems.at[at])

        for at in range(min(AHEAD, steps)):
            bring(at).start()
        both[:rows] = ins[0][...]
        both[rows:] = ins[1][...]

        @pl.loop(0, steps)
        def _(at):
            bring(at).wait()

            @pl.when(at + AHEAD < steps)
            def _():
                bring(at + AHEAD).start()

            part = jnp.dot(both[...], landed[at], preferred_element_type=F32).astype(BF16)
            here = pl.ds(pl.multiple_of(at * block, block), block)
            near[:, here] = part[:rows]
            far[:, here] = part[rows:]

    return call(
        kernel,
        earlier,
        (own, other, weight),
        [whole, whole, pl.BlockSpec(memory_space=pltpu.HBM)],
        grid=(1,),
        out_specs=[out] * 2,
        out_shape=[jax.ShapeDtypeStruct((rows, columns), BF16)] * 2,
        scratch_shapes=[
            pltpu.VMEM((2 * rows, depth), BF16),
            pltpu.VMEM((steps, depth, block), BF16),
            pltpu.SemaphoreType.DMA((steps,)),
        ],
    )


def project_hidden(own, other, weight, piece, added, attention, last, earlier=()):
    rows, units = own.shape
    columns = weight.shape[1]
    block, steps, _ = steps_of(piece)
    whole = pl.BlockSpec((rows, columns), lambda *_: (0, 0))
    part = pl.BlockSpec((rows, units), lambda *_: (0, 0))
    specs = [part, part, pl.BlockSpec(memory_space=pltpu.HBM)]
    specs += [whole] * len(added)
    specs += [pl.BlockSpec(a.shape, lambda *_: (0, 0)) for a in attention]

    def kernel(ins, refs):
        outs, (both, total, landed, sems) = refs[:2], refs[2:]

        def bring(at):
            start = pl.multiple_of(piece.start + at * block, block)
            source = ins[2].at[pl.ds(start, block), :]
            return pltpu.make_async_copy(source, landed.at[at], sems.at[at])

        for at in range(min(AHEAD, steps)):
            bring(at).start()
        halves = (slice(0, rows), slice(rows, 2 * rows))
        for at, half in enumerate(halves):
            both[half] = ins[at][...]
            first = jnp.zeros((rows, columns), F32)
            if added:
                first = ins[3 + at][...]
            if attention:
                first = first + jnp.dot(
                    ins[-3 + at][...], ins[-1][...], preferred_element_type=F32
                )
            total[half] = first

        @pl.loop(0, steps)
        def _(at):
            bring(at).wait()

            @pl.when(at + AHEAD < steps)
            def _():
                bring(at + AHEAD).start()

            here = pl.ds(pl.multiple_of(at * block, block), block)
            total[...] += jnp.dot(both[:, here], landed[at], preferred_element_type=F32)

        for out, half in zip(outs, halves):
            out[...] = total[half].astype(out.dtype)

    return call(
        kernel,
        earlier,
        (own, other, weight, *added, *attention),
        specs,
        grid=(1,),
        out_specs=[whole] * 2,
        out_shape=[jax.ShapeDtypeStruct((rows, columns), BF16 if last else F32)] * 2,
        scratch_shapes=[
            pltpu.VMEM((2 * rows, units), BF16),
            pltpu.VMEM((2 * rows, columns), F32),
            pltpu.VMEM((steps, block, columns), BF16),
            pltpu.SemaphoreType.DMA((steps,)),
        ],
    )


def make_body(mesh):
    n_red, n_wide = mesh.shape["red"], mesh.shape["wide"]
    half_wide = n_wide // 2

    def swap(x):
        return lax.ppermute(x, "tok", [(0, 1), (1, 0)])

    def all_red(x):
        parts = [x]
        for shift in range(1, n_red):
            pairs = [(i, (i + shift) % n_red) for i in range(n_red)]
            parts.append(lax.ppermute(x, "red", pairs))
        return parts

    def sum_red(x):
        return sum(a.astype(F32) for a in all_red(x))

    def collect(kept, got, width):
        core, chip = lax.axis_index("tok"), lax.axis_index("wide")
        terms = jnp.concatenate([kept, got], axis=1)

        def block(at):
            start = ((at // half_wide) ^ core) * half_wide + at % half_wide
            return lax.dynamic_slice_in_dim(terms, start * width, width, axis=1)

        total = block(chip).astype(F32)
        for k in range(n_wide - 1, 0, -1):
            pairs = [(i, i ^ k) for i in range(n_wide)]
            total = total + lax.ppermute(block(chip ^ k), "wide", pairs).astype(F32)
        return total

    def body(tokens, ln_gain, q_gain, k_gain, w_qkv, w_up, w_attn, w_down):
        core = lax.axis_index("tok")
        width = tokens.shape[1]
        qkv_rows = w_qkv.reshape(w_qkv.shape[0], w_qkv.shape[1] * w_qkv.shape[2])
        attn_rows = w_attn.reshape(w_attn.shape[0] * w_attn.shape[1], w_attn.shape[2])
        depth, units = w_up.shape
        cuts = slices(tokens.shape[0], SHARES, 16)
        pieces = slices(units, LEAD_PIECES, 128)
        rest_pieces = slices(units, REST_PIECES, 128)

        first = cuts[0].stop
        gain_rows = jnp.broadcast_to(ln_gain[None], (GAIN_ROWS, width))
        lead = jnp.concatenate([gain_rows, tokens[:first]], axis=0)
        lead = lax.all_gather(lead, "wide", axis=1, tiled=True)
        gain = lead[:1]

        def normed(floats):
            sums = jnp.stack([jnp.sum(floats, axis=1), jnp.sum(floats * floats, axis=1)])
            sums = sum_red(sums)[:, :, None] / D
            values = normalize(floats, sums[0], sums[1], gain).astype(BF16)
            mine = lax.dynamic_slice_in_dim(values, core * depth, depth, axis=1)
            theirs = lax.dynamic_slice_in_dim(values, (1 - core) * depth, depth, axis=1)
            return mine, swap(theirs)

        def project(pair, weight):
            both = jnp.concatenate(pair, axis=0)
            half = both.shape[0] // 2
            part = jnp.dot(both, weight, preferred_element_type=F32)
            far = swap(part[half:].astype(BF16)).astype(F32)
            return (part[:half] + far).astype(BF16)

        weights = [w_up[:, piece] for piece in pieces]
        lead_pair = normed(lead[GAIN_ROWS:].astype(F32))
        leads = [project(lead_pair, weights[0])]
        lead_parts = [all_red(leads[0])]
        arrived = gelu_sum(lead_parts[0])

        rest = tokens[first:] + nothing(leads[-1]).astype(BF16)
        rest = lax.all_gather(rest, "wide", axis=1, tiled=True)
        later_pair = [a + nothing(rest).astype(BF16) for a in lead_pair]
        leads.append(project(later_pair, weights[1]))
        lead_parts.append(all_red(leads[1]))
        rest_pair = normed(rest.astype(F32) + nothing(arrived))
        pair = [jnp.concatenate(p, axis=0) for p in zip(lead_pair, rest_pair)]
        arrived_other = swap(arrived)
        every = slice(0, qkv_rows.shape[1])
        near, far = project_rows(*pair, qkv_rows, every, [arrived_other, leads[1]])
        halves, before = [], [near]
        qkv = sum_rows([(near, swap(far))], slice(0, tokens.shape[0]))
        for piece in rest_pieces:
            near, far = project_rows(*rest_pair, w_up, piece, before)
            halves.append((near, swap(far)))
            before = [near]

        def output(have, other, piece, terms, cut, earlier=()):
            last = piece.stop == units
            attention = (attended[cut], attended_other[cut], attn_rows) if last else ()
            return project_hidden(have, other, w_down, piece, terms, attention, last, earlier)

        def chunk_sums(pairs, c, earlier):
            part = slice(cuts[c].start - first, cuts[c].stop - first)
            return sum_rows(pairs, part, [earlier])

        def scatter(kept, got, earlier):
            full = side_by_side(kept, got, core, earlier)
            return full, lax.psum_scatter(full, "wide", scatter_dimension=1, tiled=True)

        terms = output(arrived, arrived_other, pieces[0], (), cuts[0], [halves[-1][0]])
        earlier = [terms[0], halves[-1][1]]
        attended = attend(all_red(qkv), q_gain, k_gain, earlier)
        attended_other = swap(attended)
        second = gelu_sum(lead_parts[1], [attended])
        sums = chunk_sums(halves, 1, second)
        parts = all_red(sums)
        coming = chunk_sums(halves, 2, sums)
        terms = output(second, swap(second), pieces[1], terms, cuts[0], [coming])
        coming = all_red(coming)
        full, got = scatter(terms[0], swap(terms[1]), [])
        scattered = [got]

        hidden = gelu_sum(parts, [full])
        terms = output(hidden, swap(hidden), slice(0, units), (), cuts[1])
        full, got = scatter(terms[0], swap(terms[1]), [scattered[0]])
        scattered.append(got)

        hidden = gelu_sum(coming, [full])
        kept, sent = output(hidden, swap(hidden), slice(0, units), (), cuts[2])
        outs = [tokens[cut].astype(F32) + got.astype(F32) for cut, got in zip(cuts, scattered)]
        outs.append(tokens[cuts[2]].astype(F32) + collect(kept, swap(sent), width))
        return jnp.concatenate(outs, axis=0)

    return body


def solution(mesh):
    return jax.shard_map(
        make_body(mesh),
        mesh=mesh,
        in_specs=(
            P(("grp", "tok"), ("red", "wide")),
            P(("red", "wide")),
            P("wide", None),
            P("wide", None),
            P(("red", "tok"), "wide", None),
            P(("red", "tok"), "wide"),
            P("wide", None, ("red", "tok")),
            P("wide", ("red", "tok")),
        ),
        out_specs=P(("grp", "tok"), ("red", "wide")),
        check_vma=False,
    )
```

```python
import functools
import math

import jax
import jax.numpy as jnp
from jax import lax
from jax.experimental import pallas as pl
from jax.experimental.pallas import tpu as pltpu
from jax.sharding import PartitionSpec as P

D = 6144
PATCHES = 256
EPS = 1e-06
SHARES = (8, 5, 3)
LEAD_PIECES = (1, 1)
REST_PIECES = (2, 1)
AHEAD = 4
GAIN_ROWS = 8
BF16, F32 = jnp.bfloat16, jnp.float32
PARAMS = pltpu.CompilerParams(vmem_limit_bytes=48 * 2**20)
SMALL = pltpu.CompilerParams(vmem_limit_bytes=8 * 2**20)
MIDDLE = pltpu.CompilerParams(vmem_limit_bytes=16 * 2**20)
SOON = pl.CostEstimate(flops=0, bytes_accessed=0, transcendentals=0)


def normalize(values, mean, meansq, gain):
    return (values - mean) * lax.rsqrt(meansq - mean * mean + EPS) * gain.astype(F32)


def head_norm(values, gain):
    mean = jnp.mean(values, axis=-1, keepdims=True)
    meansq = jnp.mean(values * values, axis=-1, keepdims=True)
    return normalize(values, mean, meansq, gain)


def nothing(x):
    corner = x[(0,) * x.ndim].astype(jnp.int32)
    return lax.shift_right_logical(corner & 1, 1).astype(F32)


def slices(size, shares, grain):
    ends = [sum(shares[: i + 1]) * size // sum(shares) for i in range(len(shares))]
    ends = [end // grain * grain for end in ends]
    return [slice(a, b) for a, b in zip([0] + ends[:-1], ends)]


def steps_of(piece):
    size = math.gcd(piece.stop - piece.start, piece.start)
    block = next(b for b in (512, 384, 256, 128) if size % b == 0)
    return block, (piece.stop - piece.start) // block, piece.start // block


def corner_of(x):
    shape = (min(16, x.shape[0]), min(128, x.shape[1]))
    return pl.BlockSpec(shape, lambda *_: (0, 0))


def call(kernel, earlier, operands, specs, params=None, **options):
    def body(*refs):
        n = len(operands)
        kernel(refs[:n], refs[n + len(earlier) :])

    return pl.pallas_call(
        body,
        in_specs=list(specs) + [corner_of(a) for a in earlier],
        compiler_params=params or PARAMS,
        cost_estimate=SOON,
        **options,
    )(*operands, *earlier)


def gelu_sum(parts, earlier=()):
    rows, units = parts[0].shape
    block, steps, _ = steps_of(slice(0, units))
    spec = pl.BlockSpec((rows, block), lambda j: (0, j))

    def kernel(ins, outs):
        up = ins[0][...].astype(F32)
        for part in ins[1:]:
            up = up + part[...].astype(F32)
        outs[0][...] = (0.5 * up * (1.0 + lax.erf(up * 0.5**0.5))).astype(BF16)

    return call(
        kernel,
        earlier,
        parts,
        [spec] * len(parts),
        params=SMALL,
        grid=(steps,),
        out_specs=spec,
        out_shape=jax.ShapeDtypeStruct((rows, units), BF16),
    )


def sum_rows(pairs, cut, earlier=()):
    widths = [near.shape[1] for near, _ in pairs]
    shape = (cut.stop - cut.start, sum(widths))

    def kernel(ins, outs):
        start = 0
        for at, width in enumerate(widths):
            total = ins[2 * at][cut].astype(F32) + ins[2 * at + 1][cut].astype(F32)
            outs[0][:, start : start + width] = total.astype(BF16)
            start += width

    operands = [part for pair in pairs for part in pair]
    return call(
        kernel,
        earlier,
        operands,
        [pl.BlockSpec(part.shape, lambda *_: (0, 0)) for part in operands],
        params=MIDDLE,
        grid=(1,),
        out_specs=pl.BlockSpec(shape, lambda *_: (0, 0)),
        out_shape=jax.ShapeDtypeStruct(shape, BF16),
    )


def side_by_side(kept, got, core, earlier=()):
    rows, columns = kept.shape
    spec = pl.BlockSpec(kept.shape, lambda *_: (0, 0))

    def kernel(ins, outs):
        first = ins[2][0] == 0
        outs[0][:, :columns] = jnp.where(first, ins[0][...], ins[1][...])
        outs[0][:, columns:] = jnp.where(first, ins[1][...], ins[0][...])

    return call(
        kernel,
        earlier,
        (kept, got, core.reshape(1)),
        [spec, spec, pl.BlockSpec(memory_space=pltpu.SMEM)],
        params=SMALL,
        grid=(1,),
        out_specs=pl.BlockSpec((rows, 2 * columns), lambda *_: (0, 0)),
        out_shape=jax.ShapeDtypeStruct((rows, 2 * columns), kept.dtype),
    )


def attend(parts, q_gain, k_gain, earlier=()):
    rows, width = parts[0].shape[0], q_gain.shape[1]
    n = len(parts)

    def kernel(ins, outs):
        def columns(at):
            here = slice(at * width, (at + 1) * width)
            return sum(part[:, here].astype(F32) for part in ins[:n])

        query = head_norm(columns(0), ins[n][...]).astype(BF16)
        key = head_norm(columns(1), ins[n + 1][...]).astype(BF16)
        value = columns(2).astype(BF16).astype(F32)
        for at in range(0, rows, PATCHES):
            image = slice(at, at + PATCHES)
            scores = lax.dot_general(
                query[image], key[image], (((1,), (1,)), ((), ())), preferred_element_type=F32
            )
            scores = scores * width ** (-0.5)
            weights = jnp.exp(scores - jnp.max(scores, axis=-1, keepdims=True))
            total = jnp.sum(weights, axis=-1, keepdims=True)
            acc = jnp.dot(
                weights,
                value[image],
                precision=lax.Precision.HIGHEST,
                preferred_element_type=F32,
            )
            outs[0][image] = (acc / total).astype(BF16)

    whole = [pl.BlockSpec(a.shape, lambda *_: (0, 0)) for a in (*parts, q_gain, k_gain)]
    return call(
        kernel,
        earlier,
        (*parts, q_gain, k_gain),
        whole,
        params=SMALL,
        grid=(1,),
        out_specs=pl.BlockSpec((rows, width), lambda *_: (0, 0)),
        out_shape=jax.ShapeDtypeStruct((rows, width), BF16),
    )


def project_rows(own, other, weight, piece, earlier=()):
    rows, depth = own.shape
    columns = piece.stop - piece.start
    block, steps, _ = steps_of(piece)
    whole = pl.BlockSpec((rows, depth), lambda *_: (0, 0))
    out = pl.BlockSpec((rows, columns), lambda *_: (0, 0))

    def kernel(ins, refs):
        near, far, both, landed, sems = refs

        def bring(at):
            start = pl.multiple_of(piece.start + at * block, block)
            source = ins[2].at[:, pl.ds(start, block)]
            return pltpu.make_async_copy(source, landed.at[at], sems.at[at])

        for at in range(min(AHEAD, steps)):
            bring(at).start()
        both[:rows] = ins[0][...]
        both[rows:] = ins[1][...]

        @pl.loop(0, steps)
        def _(at):
            bring(at).wait()

            @pl.when(at + AHEAD < steps)
            def _():
                bring(at + AHEAD).start()

            part = jnp.dot(both[...], landed[at], preferred_element_type=F32).astype(BF16)
            here = pl.ds(pl.multiple_of(at * block, block), block)
            near[:, here] = part[:rows]
            far[:, here] = part[rows:]

    return call(
        kernel,
        earlier,
        (own, other, weight),
        [whole, whole, pl.BlockSpec(memory_space=pltpu.HBM)],
        grid=(1,),
        out_specs=[out] * 2,
        out_shape=[jax.ShapeDtypeStruct((rows, columns), BF16)] * 2,
        scratch_shapes=[
            pltpu.VMEM((2 * rows, depth), BF16),
            pltpu.VMEM((steps, depth, block), BF16),
            pltpu.SemaphoreType.DMA((steps,)),
        ],
    )


def project_hidden(own, other, weight, piece, added, attention, last, earlier=()):
    rows, units = own.shape
    columns = weight.shape[1]
    block, steps, _ = steps_of(piece)
    whole = pl.BlockSpec((rows, columns), lambda *_: (0, 0))
    part = pl.BlockSpec((rows, units), lambda *_: (0, 0))
    specs = [part, part, pl.BlockSpec(memory_space=pltpu.HBM)]
    specs += [whole] * len(added)
    specs += [pl.BlockSpec(a.shape, lambda *_: (0, 0)) for a in attention]

    def kernel(ins, refs):
        outs, (both, total, landed, sems) = refs[:2], refs[2:]

        def bring(at):
            start = pl.multiple_of(piece.start + at * block, block)
            source = ins[2].at[pl.ds(start, block), :]
            return pltpu.make_async_copy(source, landed.at[at], sems.at[at])

        for at in range(min(AHEAD, steps)):
            bring(at).start()
        halves = (slice(0, rows), slice(rows, 2 * rows))
        for at, half in enumerate(halves):
            both[half] = ins[at][...]
            first = jnp.zeros((rows, columns), F32)
            if added:
                first = ins[3 + at][...]
            if attention:
                first = first + jnp.dot(
                    ins[-3 + at][...], ins[-1][...], preferred_element_type=F32
                )
            total[half] = first

        @pl.loop(0, steps)
        def _(at):
            bring(at).wait()

            @pl.when(at + AHEAD < steps)
            def _():
                bring(at + AHEAD).start()

            here = pl.ds(pl.multiple_of(at * block, block), block)
            total[...] += jnp.dot(both[:, here], landed[at], preferred_element_type=F32)

        for out, half in zip(outs, halves):
            out[...] = total[half].astype(out.dtype)

    return call(
        kernel,
        earlier,
        (own, other, weight, *added, *attention),
        specs,
        grid=(1,),
        out_specs=[whole] * 2,
        out_shape=[jax.ShapeDtypeStruct((rows, columns), BF16 if last else F32)] * 2,
        scratch_shapes=[
            pltpu.VMEM((2 * rows, units), BF16),
            pltpu.VMEM((2 * rows, columns), F32),
            pltpu.VMEM((steps, block, columns), BF16),
            pltpu.SemaphoreType.DMA((steps,)),
        ],
    )


def make_body(mesh):
    n_red, n_wide = mesh.shape["red"], mesh.shape["wide"]
    half_wide = n_wide // 2

    def swap(x):
        return lax.ppermute(x, "tok", [(0, 1), (1, 0)])

    def all_red(x):
        parts = [x]
        for shift in range(1, n_red):
            pairs = [(i, (i + shift) % n_red) for i in range(n_red)]
            parts.append(lax.ppermute(x, "red", pairs))
        return parts

    def sum_red(x):
        return sum(a.astype(F32) for a in all_red(x))

    def collect(kept, got, width):
        core, chip = lax.axis_index("tok"), lax.axis_index("wide")
        terms = jnp.concatenate([kept, got], axis=1)

        def block(at):
            start = ((at // half_wide) ^ core) * half_wide + at % half_wide
            return lax.dynamic_slice_in_dim(terms, start * width, width, axis=1)

        total = block(chip).astype(F32)
        for k in range(n_wide - 1, 0, -1):
            pairs = [(i, i ^ k) for i in range(n_wide)]
            total = total + lax.ppermute(block(chip ^ k), "wide", pairs).astype(F32)
        return total

    def body(tokens, ln_gain, q_gain, k_gain, w_qkv, w_up, w_attn, w_down):
        core = lax.axis_index("tok")
        width = tokens.shape[1]
        qkv_rows = w_qkv.reshape(w_qkv.shape[0], w_qkv.shape[1] * w_qkv.shape[2])
        attn_rows = w_attn.reshape(w_attn.shape[0] * w_attn.shape[1], w_attn.shape[2])
        depth, units = w_up.shape
        cuts = slices(tokens.shape[0], SHARES, 16)
        pieces = slices(units, LEAD_PIECES, 128)
        rest_pieces = slices(units, REST_PIECES, 128)

        first = cuts[0].stop
        gain_rows = jnp.broadcast_to(ln_gain[None], (GAIN_ROWS, width))
        lead = jnp.concatenate([gain_rows, tokens[:first]], axis=0)
        lead = lax.all_gather(lead, "wide", axis=1, tiled=True)
        gain = lead[:1]

        def normed(floats, start=0.0):
            sums = jnp.stack([jnp.sum(floats, axis=1), jnp.sum(floats * floats, axis=1)])
            sums = sum_red(sums)[:, :, None] / D + start
            values = normalize(floats, sums[0], sums[1], gain).astype(BF16)
            mine = lax.dynamic_slice_in_dim(values, core * depth, depth, axis=1)
            theirs = lax.dynamic_slice_in_dim(values, (1 - core) * depth, depth, axis=1)
            return mine, swap(theirs)

        def project(pair, weight):
            both = jnp.concatenate(pair, axis=0)
            half = both.shape[0] // 2
            part = jnp.dot(both, weight, preferred_element_type=F32)
            sent = part[half:].astype(BF16)
            return (part[:half] + swap(sent).astype(F32)).astype(BF16), sent

        weights = [w_up[:, piece] for piece in pieces]
        lead_pair = normed(lead[GAIN_ROWS:].astype(F32))
        leads = [project(lead_pair, weights[0])[0]]
        lead_parts = [all_red(leads[0])]

        rest = tokens[first:] + nothing(leads[-1]).astype(BF16)
        rest = lax.all_gather(rest, "wide", axis=1, tiled=True)
        later_pair = [a + nothing(rest).astype(BF16) for a in lead_pair]
        lead, sent = project(later_pair, weights[1])
        leads.append(lead)
        lead_parts.append(all_red(lead))
        arrived = gelu_sum(lead_parts[0], [sent])
        rest_pair = normed(rest.astype(F32) + nothing(arrived), nothing(leads[1]))
        pair = [jnp.concatenate(p, axis=0) for p in zip(lead_pair, rest_pair)]
        arrived_other = swap(arrived)
        every = slice(0, qkv_rows.shape[1])
        near, far = project_rows(*pair, qkv_rows, every, [arrived_other, leads[1]])
        halves, before = [], [near]
        qkv = sum_rows([(near, swap(far))], slice(0, tokens.shape[0]))
        for piece in rest_pieces:
            near, far = project_rows(*rest_pair, w_up, piece, before)
            halves.append((near, swap(far)))
            before = [near, qkv]

        def output(have, other, piece, terms, cut, earlier=()):
            last = piece.stop == units
            attention = (attended[cut], attended_other[cut], attn_rows) if last else ()
            return project_hidden(have, other, w_down, piece, terms, attention, last, earlier)

        def chunk_sums(pairs, c, earlier):
            part = slice(cuts[c].start - first, cuts[c].stop - first)
            return sum_rows(pairs, part, [earlier])

        def scatter(kept, got, earlier):
            full = side_by_side(kept, got, core, earlier)
            return full, lax.psum_scatter(full, "wide", scatter_dimension=1, tiled=True)

        terms = output(arrived, arrived_other, pieces[0], (), cuts[0], [halves[-1][0]])
        earlier = [terms[0], halves[-1][1]]
        attended = attend(all_red(qkv), q_gain, k_gain, earlier)
        attended_other = swap(attended)
        second = gelu_sum(lead_parts[1], [attended])
        sums = chunk_sums(halves, 1, second)
        parts = all_red(sums)
        coming = chunk_sums(halves, 2, sums)
        terms = output(second, swap(second), pieces[1], terms, cuts[0], [coming])
        coming = all_red(coming)
        full, got = scatter(terms[0], swap(terms[1]), [])
        scattered = [got]

        hidden = gelu_sum(parts, [full])
        terms = output(hidden, swap(hidden), slice(0, units), (), cuts[1])
        full, got = scatter(terms[0], swap(terms[1]), [scattered[0]])
        scattered.append(got)

        hidden = gelu_sum(coming, [full])
        kept, sent = output(hidden, swap(hidden), slice(0, units), (), cuts[2])
        outs = [tokens[cut].astype(F32) + got.astype(F32) for cut, got in zip(cuts, scattered)]
        outs.append(tokens[cuts[2]].astype(F32) + collect(kept, swap(sent), width))
        return jnp.concatenate(outs, axis=0)

    return body


def solution(mesh):
    return jax.shard_map(
        make_body(mesh),
        mesh=mesh,
        in_specs=(
            P(("grp", "tok"), ("red", "wide")),
            P(("red", "wide")),
            P("wide", None),
            P("wide", None),
            P(("red", "tok"), "wide", None),
            P(("red", "tok"), "wide"),
            P("wide", None, ("red", "tok")),
            P("wide", ("red", "tok")),
        ),
        out_specs=P(("grp", "tok"), ("red", "wide")),
        check_vma=False,
    )
```

```python
import functools
import math

import jax
import jax.numpy as jnp
from jax import lax
from jax.experimental import pallas as pl
from jax.experimental.pallas import tpu as pltpu
from jax.sharding import PartitionSpec as P

D = 6144
PATCHES = 256
EPS = 1e-06
SHARES = (8, 5, 3)
LEAD_PIECES = (1, 1)
REST_PIECES = (2, 1)
AHEAD = 4
GAIN_ROWS = 8
BF16, F32 = jnp.bfloat16, jnp.float32
PARAMS = pltpu.CompilerParams(vmem_limit_bytes=48 * 2**20)
SMALL = pltpu.CompilerParams(vmem_limit_bytes=8 * 2**20)
MIDDLE = pltpu.CompilerParams(vmem_limit_bytes=16 * 2**20)
SOON = pl.CostEstimate(flops=0, bytes_accessed=0, transcendentals=0)


def normalize(values, mean, meansq, gain):
    return (values - mean) * lax.rsqrt(meansq - mean * mean + EPS) * gain.astype(F32)


def head_norm(values, gain):
    mean = jnp.mean(values, axis=-1, keepdims=True)
    meansq = jnp.mean(values * values, axis=-1, keepdims=True)
    return normalize(values, mean, meansq, gain)


def nothing(x):
    corner = x[(0,) * x.ndim].astype(jnp.int32)
    return lax.shift_right_logical(corner & 1, 1).astype(F32)


def slices(size, shares, grain):
    ends = [sum(shares[: i + 1]) * size // sum(shares) for i in range(len(shares))]
    ends = [end // grain * grain for end in ends]
    return [slice(a, b) for a, b in zip([0] + ends[:-1], ends)]


def steps_of(piece):
    size = math.gcd(piece.stop - piece.start, piece.start)
    block = next(b for b in (512, 384, 256, 128) if size % b == 0)
    return block, (piece.stop - piece.start) // block, piece.start // block


def corner_of(x):
    shape = (min(16, x.shape[0]), min(128, x.shape[1]))
    return pl.BlockSpec(shape, lambda *_: (0, 0))


def call(kernel, earlier, operands, specs, params=None, **options):
    def body(*refs):
        n = len(operands)
        kernel(refs[:n], refs[n + len(earlier) :])

    return pl.pallas_call(
        body,
        in_specs=list(specs) + [corner_of(a) for a in earlier],
        compiler_params=params or PARAMS,
        cost_estimate=SOON,
        **options,
    )(*operands, *earlier)


def gelu_sum(parts, earlier=()):
    rows, units = parts[0].shape
    block, steps, _ = steps_of(slice(0, units))
    spec = pl.BlockSpec((rows, block), lambda j: (0, j))

    def kernel(ins, outs):
        up = ins[0][...].astype(F32)
        for part in ins[1:]:
            up = up + part[...].astype(F32)
        outs[0][...] = (0.5 * up * (1.0 + lax.erf(up * 0.5**0.5))).astype(BF16)

    return call(
        kernel,
        earlier,
        parts,
        [spec] * len(parts),
        params=SMALL,
        grid=(steps,),
        out_specs=spec,
        out_shape=jax.ShapeDtypeStruct((rows, units), BF16),
    )


def sum_rows(pairs, cut, earlier=()):
    widths = [near.shape[1] for near, _ in pairs]
    shape = (cut.stop - cut.start, sum(widths))

    def kernel(ins, outs):
        start = 0
        for at, width in enumerate(widths):
            total = ins[2 * at][cut].astype(F32) + ins[2 * at + 1][cut].astype(F32)
            outs[0][:, start : start + width] = total.astype(BF16)
            start += width

    operands = [part for pair in pairs for part in pair]
    return call(
        kernel,
        earlier,
        operands,
        [pl.BlockSpec(part.shape, lambda *_: (0, 0)) for part in operands],
        params=MIDDLE,
        grid=(1,),
        out_specs=pl.BlockSpec(shape, lambda *_: (0, 0)),
        out_shape=jax.ShapeDtypeStruct(shape, BF16),
    )


def side_by_side(kept, got, core, earlier=()):
    rows, columns = kept.shape
    spec = pl.BlockSpec(kept.shape, lambda *_: (0, 0))

    def kernel(ins, outs):
        first = ins[2][0] == 0
        outs[0][:, :columns] = jnp.where(first, ins[0][...], ins[1][...])
        outs[0][:, columns:] = jnp.where(first, ins[1][...], ins[0][...])

    return call(
        kernel,
        earlier,
        (kept, got, core.reshape(1)),
        [spec, spec, pl.BlockSpec(memory_space=pltpu.SMEM)],
        params=SMALL,
        grid=(1,),
        out_specs=pl.BlockSpec((rows, 2 * columns), lambda *_: (0, 0)),
        out_shape=jax.ShapeDtypeStruct((rows, 2 * columns), kept.dtype),
    )


def attend(parts, q_gain, k_gain, earlier=()):
    rows, width = parts[0].shape[0], q_gain.shape[1]
    n = len(parts)

    def kernel(ins, outs):
        def columns(at):
            here = slice(at * width, (at + 1) * width)
            return sum(part[:, here].astype(F32) for part in ins[:n])

        query = head_norm(columns(0), ins[n][...]).astype(BF16)
        key = head_norm(columns(1), ins[n + 1][...]).astype(BF16)
        value = columns(2).astype(BF16).astype(F32)
        for at in range(0, rows, PATCHES):
            image = slice(at, at + PATCHES)
            scores = lax.dot_general(
                query[image], key[image], (((1,), (1,)), ((), ())), preferred_element_type=F32
            )
            scores = scores * width ** (-0.5)
            weights = jnp.exp(scores - jnp.max(scores, axis=-1, keepdims=True))
            total = jnp.sum(weights, axis=-1, keepdims=True)
            acc = jnp.dot(
                weights,
                value[image],
                precision=lax.Precision.HIGHEST,
                preferred_element_type=F32,
            )
            outs[0][image] = (acc / total).astype(BF16)

    whole = [pl.BlockSpec(a.shape, lambda *_: (0, 0)) for a in (*parts, q_gain, k_gain)]
    return call(
        kernel,
        earlier,
        (*parts, q_gain, k_gain),
        whole,
        params=SMALL,
        grid=(1,),
        out_specs=pl.BlockSpec((rows, width), lambda *_: (0, 0)),
        out_shape=jax.ShapeDtypeStruct((rows, width), BF16),
    )


def project_rows(own, other, weight, piece, earlier=()):
    rows, depth = own.shape
    columns = piece.stop - piece.start
    block, steps, _ = steps_of(piece)
    whole = pl.BlockSpec((rows, depth), lambda *_: (0, 0))
    out = pl.BlockSpec((rows, columns), lambda *_: (0, 0))

    def kernel(ins, refs):
        near, far, both, landed, sems = refs

        def bring(at):
            start = pl.multiple_of(piece.start + at * block, block)
            source = ins[2].at[:, pl.ds(start, block)]
            return pltpu.make_async_copy(source, landed.at[at], sems.at[at])

        for at in range(min(AHEAD, steps)):
            bring(at).start()
        both[:rows] = ins[0][...]
        both[rows:] = ins[1][...]

        @pl.loop(0, steps)
        def _(at):
            bring(at).wait()

            @pl.when(at + AHEAD < steps)
            def _():
                bring(at + AHEAD).start()

            part = jnp.dot(both[...], landed[at], preferred_element_type=F32).astype(BF16)
            here = pl.ds(pl.multiple_of(at * block, block), block)
            near[:, here] = part[:rows]
            far[:, here] = part[rows:]

    return call(
        kernel,
        earlier,
        (own, other, weight),
        [whole, whole, pl.BlockSpec(memory_space=pltpu.HBM)],
        grid=(1,),
        out_specs=[out] * 2,
        out_shape=[jax.ShapeDtypeStruct((rows, columns), BF16)] * 2,
        scratch_shapes=[
            pltpu.VMEM((2 * rows, depth), BF16),
            pltpu.VMEM((steps, depth, block), BF16),
            pltpu.SemaphoreType.DMA((steps,)),
        ],
    )


def project_hidden(own, other, weight, piece, added, attention, last, earlier=()):
    rows, units = own.shape
    columns = weight.shape[1]
    block, steps, _ = steps_of(piece)
    whole = pl.BlockSpec((rows, columns), lambda *_: (0, 0))
    part = pl.BlockSpec((rows, units), lambda *_: (0, 0))
    specs = [part, part, pl.BlockSpec(memory_space=pltpu.HBM)]
    specs += [whole] * len(added)
    specs += [pl.BlockSpec(a.shape, lambda *_: (0, 0)) for a in attention]

    def kernel(ins, refs):
        outs, (both, total, landed, sems) = refs[:2], refs[2:]

        def bring(at):
            start = pl.multiple_of(piece.start + at * block, block)
            source = ins[2].at[pl.ds(start, block), :]
            return pltpu.make_async_copy(source, landed.at[at], sems.at[at])

        for at in range(min(AHEAD, steps)):
            bring(at).start()
        halves = (slice(0, rows), slice(rows, 2 * rows))
        for at, half in enumerate(halves):
            both[half] = ins[at][...]
            first = jnp.zeros((rows, columns), F32)
            if added:
                first = ins[3 + at][...]
            if attention:
                first = first + jnp.dot(
                    ins[-3 + at][...], ins[-1][...], preferred_element_type=F32
                )
            total[half] = first

        @pl.loop(0, steps)
        def _(at):
            bring(at).wait()

            @pl.when(at + AHEAD < steps)
            def _():
                bring(at + AHEAD).start()

            here = pl.ds(pl.multiple_of(at * block, block), block)
            total[...] += jnp.dot(both[:, here], landed[at], preferred_element_type=F32)

        for out, half in zip(outs, halves):
            out[...] = total[half].astype(out.dtype)

    return call(
        kernel,
        earlier,
        (own, other, weight, *added, *attention),
        specs,
        grid=(1,),
        out_specs=[whole] * 2,
        out_shape=[jax.ShapeDtypeStruct((rows, columns), BF16 if last else F32)] * 2,
        scratch_shapes=[
            pltpu.VMEM((2 * rows, units), BF16),
            pltpu.VMEM((2 * rows, columns), F32),
            pltpu.VMEM((steps, block, columns), BF16),
            pltpu.SemaphoreType.DMA((steps,)),
        ],
    )


def make_body(mesh):
    n_red, n_wide = mesh.shape["red"], mesh.shape["wide"]
    half_wide = n_wide // 2

    def swap(x):
        return lax.ppermute(x, "tok", [(0, 1), (1, 0)])

    def all_red(x):
        parts = [x]
        for shift in range(1, n_red):
            pairs = [(i, (i + shift) % n_red) for i in range(n_red)]
            parts.append(lax.ppermute(x, "red", pairs))
        return parts

    def sum_red(x):
        return sum(a.astype(F32) for a in all_red(x))

    def collect(kept, got, width):
        core, chip = lax.axis_index("tok"), lax.axis_index("wide")
        terms = jnp.concatenate([kept, got], axis=1)

        def block(at):
            start = ((at // half_wide) ^ core) * half_wide + at % half_wide
            return lax.dynamic_slice_in_dim(terms, start * width, width, axis=1)

        total = block(chip).astype(F32)
        for k in range(n_wide - 1, 0, -1):
            pairs = [(i, i ^ k) for i in range(n_wide)]
            total = total + lax.ppermute(block(chip ^ k), "wide", pairs).astype(F32)
        return total

    def body(tokens, ln_gain, q_gain, k_gain, w_qkv, w_up, w_attn, w_down):
        core = lax.axis_index("tok")
        width = tokens.shape[1]
        qkv_rows = w_qkv.reshape(w_qkv.shape[0], w_qkv.shape[1] * w_qkv.shape[2])
        attn_rows = w_attn.reshape(w_attn.shape[0] * w_attn.shape[1], w_attn.shape[2])
        depth, units = w_up.shape
        cuts = slices(tokens.shape[0], SHARES, 16)
        pieces = slices(units, LEAD_PIECES, 128)
        rest_pieces = slices(units, REST_PIECES, 128)

        first = cuts[0].stop
        gain_rows = jnp.broadcast_to(ln_gain[None], (GAIN_ROWS, width))
        lead = jnp.concatenate([gain_rows, tokens[:first]], axis=0)
        lead = lax.all_gather(lead, "wide", axis=1, tiled=True)
        gain = lead[:1]

        def row_sums(raw):
            floats = raw.astype(F32)
            return jnp.stack([jnp.sum(floats, axis=1), jnp.sum(floats * floats, axis=1)])

        def normed(raw, sums, start=0.0):
            sums = sum_red(sums)[:, :, None] / D + start
            values = normalize(raw.astype(F32), sums[0], sums[1], gain).astype(BF16)
            mine = lax.dynamic_slice_in_dim(values, core * depth, depth, axis=1)
            theirs = lax.dynamic_slice_in_dim(values, (1 - core) * depth, depth, axis=1)
            return mine, swap(theirs)

        def project(pair, weight):
            both = jnp.concatenate(pair, axis=0)
            half = both.shape[0] // 2
            part = jnp.dot(both, weight, preferred_element_type=F32)
            far = swap(part[half:].astype(BF16)).astype(F32)
            return (part[:half] + far).astype(BF16)

        weights = [w_up[:, piece] for piece in pieces]
        lead_pair = normed(lead[GAIN_ROWS:], row_sums(lead[GAIN_ROWS:]))
        leads = [project(lead_pair, weights[0])]
        lead_parts = [all_red(leads[0])]
        arrived = gelu_sum(lead_parts[0])

        rest = tokens[first:] + nothing(leads[-1]).astype(BF16)
        rest = lax.all_gather(rest, "wide", axis=1, tiled=True)
        sums = row_sums(rest)
        later_pair = [a + nothing(sums).astype(BF16) for a in lead_pair]
        leads.append(project(later_pair, weights[1]))
        lead_parts.append(all_red(leads[1]))
        rest_pair = normed(rest, sums, nothing(arrived))
        pair = [jnp.concatenate(p, axis=0) for p in zip(lead_pair, rest_pair)]
        arrived_other = swap(arrived)
        every = slice(0, qkv_rows.shape[1])
        near, far = project_rows(*pair, qkv_rows, every, [arrived_other, leads[1]])
        halves, before = [], [near]
        qkv = sum_rows([(near, swap(far))], slice(0, tokens.shape[0]))
        for piece in rest_pieces:
            near, far = project_rows(*rest_pair, w_up, piece, before)
            halves.append((near, swap(far)))
            before = [near]

        def output(have, other, piece, terms, cut, earlier=()):
            last = piece.stop == units
            attention = (attended[cut], attended_other[cut], attn_rows) if last else ()
            return project_hidden(have, other, w_down, piece, terms, attention, last, earlier)

        def chunk_sums(pairs, c, earlier):
            part = slice(cuts[c].start - first, cuts[c].stop - first)
            return sum_rows(pairs, part, [earlier])

        def scatter(kept, got, earlier):
            full = side_by_side(kept, got, core, earlier)
            return full, lax.psum_scatter(full, "wide", scatter_dimension=1, tiled=True)

        terms = output(arrived, arrived_other, pieces[0], (), cuts[0], [halves[-1][0]])
        earlier = [terms[0], halves[-1][1]]
        attended = attend(all_red(qkv), q_gain, k_gain, earlier)
        attended_other = swap(attended)
        second = gelu_sum(lead_parts[1], [attended])
        sums = chunk_sums(halves, 1, second)
        parts = all_red(sums)
        coming = chunk_sums(halves, 2, sums)
        terms = output(second, swap(second), pieces[1], terms, cuts[0], [coming])
        coming = all_red(coming)
        full, got = scatter(terms[0], swap(terms[1]), [])
        scattered = [got]

        hidden = gelu_sum(parts, [full])
        terms = output(hidden, swap(hidden), slice(0, units), (), cuts[1])
        full, got = scatter(terms[0], swap(terms[1]), [scattered[0]])
        scattered.append(got)

        hidden = gelu_sum(coming, [full])
        kept, sent = output(hidden, swap(hidden), slice(0, units), (), cuts[2])
        outs = [tokens[cut].astype(F32) + got.astype(F32) for cut, got in zip(cuts, scattered)]
        outs.append(tokens[cuts[2]].astype(F32) + collect(kept, swap(sent), width))
        return jnp.concatenate(outs, axis=0)

    return body


def solution(mesh):
    return jax.shard_map(
        make_body(mesh),
        mesh=mesh,
        in_specs=(
            P(("grp", "tok"), ("red", "wide")),
            P(("red", "wide")),
            P("wide", None),
            P("wide", None),
            P(("red", "tok"), "wide", None),
            P(("red", "tok"), "wide"),
            P("wide", None, ("red", "tok")),
            P("wide", ("red", "tok")),
        ),
        out_specs=P(("grp", "tok"), ("red", "wide")),
        check_vma=False,
    )
```

```python
import functools
import math

import jax
import jax.numpy as jnp
from jax import lax
from jax.experimental import pallas as pl
from jax.experimental.pallas import tpu as pltpu
from jax.sharding import PartitionSpec as P

D = 6144
PATCHES = 256
EPS = 1e-06
SHARES = (8, 3, 5)
LEAD_PIECES = (1, 1)
REST_PIECES = (2, 1)
AHEAD = 4
GAIN_ROWS = 8
BF16, F32 = jnp.bfloat16, jnp.float32
PARAMS = pltpu.CompilerParams(vmem_limit_bytes=48 * 2**20)
SMALL = pltpu.CompilerParams(vmem_limit_bytes=8 * 2**20)
MIDDLE = pltpu.CompilerParams(vmem_limit_bytes=16 * 2**20)
SOON = pl.CostEstimate(flops=0, bytes_accessed=0, transcendentals=0)


def normalize(values, mean, meansq, gain):
    return (values - mean) * lax.rsqrt(meansq - mean * mean + EPS) * gain.astype(F32)


def head_norm(values, gain):
    mean = jnp.mean(values, axis=-1, keepdims=True)
    meansq = jnp.mean(values * values, axis=-1, keepdims=True)
    return normalize(values, mean, meansq, gain)


def nothing(x):
    corner = x[(0,) * x.ndim].astype(jnp.int32)
    return lax.shift_right_logical(corner & 1, 1).astype(F32)


def slices(size, shares, grain):
    ends = [sum(shares[: i + 1]) * size // sum(shares) for i in range(len(shares))]
    ends = [end // grain * grain for end in ends]
    return [slice(a, b) for a, b in zip([0] + ends[:-1], ends)]


def steps_of(piece):
    size = math.gcd(piece.stop - piece.start, piece.start)
    block = next(b for b in (512, 384, 256, 128) if size % b == 0)
    return block, (piece.stop - piece.start) // block, piece.start // block


def corner_of(x):
    shape = (min(16, x.shape[0]), min(128, x.shape[1]))
    return pl.BlockSpec(shape, lambda *_: (0, 0))


def call(kernel, earlier, operands, specs, params=None, **options):
    def body(*refs):
        n = len(operands)
        kernel(refs[:n], refs[n + len(earlier) :])

    return pl.pallas_call(
        body,
        in_specs=list(specs) + [corner_of(a) for a in earlier],
        compiler_params=params or PARAMS,
        cost_estimate=SOON,
        **options,
    )(*operands, *earlier)


def gelu_sum(parts, earlier=()):
    rows, units = parts[0].shape
    block, steps, _ = steps_of(slice(0, units))
    spec = pl.BlockSpec((rows, block), lambda j: (0, j))

    def kernel(ins, outs):
        up = ins[0][...].astype(F32)
        for part in ins[1:]:
            up = up + part[...].astype(F32)
        outs[0][...] = (0.5 * up * (1.0 + lax.erf(up * 0.5**0.5))).astype(BF16)

    return call(
        kernel,
        earlier,
        parts,
        [spec] * len(parts),
        params=SMALL,
        grid=(steps,),
        out_specs=spec,
        out_shape=jax.ShapeDtypeStruct((rows, units), BF16),
    )


def sum_rows(pairs, cut, earlier=()):
    widths = [near.shape[1] for near, _ in pairs]
    shape = (cut.stop - cut.start, sum(widths))

    def kernel(ins, outs):
        start = 0
        for at, width in enumerate(widths):
            total = ins[2 * at][cut].astype(F32) + ins[2 * at + 1][cut].astype(F32)
            outs[0][:, start : start + width] = total.astype(BF16)
            start += width

    operands = [part for pair in pairs for part in pair]
    return call(
        kernel,
        earlier,
        operands,
        [pl.BlockSpec(part.shape, lambda *_: (0, 0)) for part in operands],
        params=MIDDLE,
        grid=(1,),
        out_specs=pl.BlockSpec(shape, lambda *_: (0, 0)),
        out_shape=jax.ShapeDtypeStruct(shape, BF16),
    )


def side_by_side(kept, got, core, earlier=()):
    rows, columns = kept.shape
    spec = pl.BlockSpec(kept.shape, lambda *_: (0, 0))

    def kernel(ins, outs):
        first = ins[2][0] == 0
        outs[0][:, :columns] = jnp.where(first, ins[0][...], ins[1][...])
        outs[0][:, columns:] = jnp.where(first, ins[1][...], ins[0][...])

    return call(
        kernel,
        earlier,
        (kept, got, core.reshape(1)),
        [spec, spec, pl.BlockSpec(memory_space=pltpu.SMEM)],
        params=SMALL,
        grid=(1,),
        out_specs=pl.BlockSpec((rows, 2 * columns), lambda *_: (0, 0)),
        out_shape=jax.ShapeDtypeStruct((rows, 2 * columns), kept.dtype),
    )


def attend(parts, q_gain, k_gain, earlier=()):
    rows, width = parts[0].shape[0], q_gain.shape[1]
    n = len(parts)

    def kernel(ins, outs):
        def columns(at):
            here = slice(at * width, (at + 1) * width)
            return sum(part[:, here].astype(F32) for part in ins[:n])

        query = head_norm(columns(0), ins[n][...]).astype(BF16)
        key = head_norm(columns(1), ins[n + 1][...]).astype(BF16)
        value = columns(2).astype(BF16).astype(F32)
        for at in range(0, rows, PATCHES):
            image = slice(at, at + PATCHES)
            scores = lax.dot_general(
                query[image], key[image], (((1,), (1,)), ((), ())), preferred_element_type=F32
            )
            scores = scores * width ** (-0.5)
            weights = jnp.exp(scores - jnp.max(scores, axis=-1, keepdims=True))
            total = jnp.sum(weights, axis=-1, keepdims=True)
            acc = jnp.dot(
                weights,
                value[image],
                precision=lax.Precision.HIGHEST,
                preferred_element_type=F32,
            )
            outs[0][image] = (acc / total).astype(BF16)

    whole = [pl.BlockSpec(a.shape, lambda *_: (0, 0)) for a in (*parts, q_gain, k_gain)]
    return call(
        kernel,
        earlier,
        (*parts, q_gain, k_gain),
        whole,
        params=SMALL,
        grid=(1,),
        out_specs=pl.BlockSpec((rows, width), lambda *_: (0, 0)),
        out_shape=jax.ShapeDtypeStruct((rows, width), BF16),
    )


def project_rows(own, other, weight, piece, earlier=()):
    rows, depth = own.shape
    columns = piece.stop - piece.start
    block, steps, _ = steps_of(piece)
    whole = pl.BlockSpec((rows, depth), lambda *_: (0, 0))
    out = pl.BlockSpec((rows, columns), lambda *_: (0, 0))

    def kernel(ins, refs):
        near, far, both, landed, sems = refs

        def bring(at):
            start = pl.multiple_of(piece.start + at * block, block)
            source = ins[2].at[:, pl.ds(start, block)]
            return pltpu.make_async_copy(source, landed.at[at], sems.at[at])

        for at in range(min(AHEAD, steps)):
            bring(at).start()
        both[:rows] = ins[0][...]
        both[rows:] = ins[1][...]

        @pl.loop(0, steps)
        def _(at):
            bring(at).wait()

            @pl.when(at + AHEAD < steps)
            def _():
                bring(at + AHEAD).start()

            part = jnp.dot(both[...], landed[at], preferred_element_type=F32).astype(BF16)
            here = pl.ds(pl.multiple_of(at * block, block), block)
            near[:, here] = part[:rows]
            far[:, here] = part[rows:]

    return call(
        kernel,
        earlier,
        (own, other, weight),
        [whole, whole, pl.BlockSpec(memory_space=pltpu.HBM)],
        grid=(1,),
        out_specs=[out] * 2,
        out_shape=[jax.ShapeDtypeStruct((rows, columns), BF16)] * 2,
        scratch_shapes=[
            pltpu.VMEM((2 * rows, depth), BF16),
            pltpu.VMEM((steps, depth, block), BF16),
            pltpu.SemaphoreType.DMA((steps,)),
        ],
    )


def project_hidden(own, other, weight, piece, added, attention, last, earlier=()):
    rows, units = own.shape
    columns = weight.shape[1]
    block, steps, _ = steps_of(piece)
    whole = pl.BlockSpec((rows, columns), lambda *_: (0, 0))
    part = pl.BlockSpec((rows, units), lambda *_: (0, 0))
    specs = [part, part, pl.BlockSpec(memory_space=pltpu.HBM)]
    specs += [whole] * len(added)
    specs += [pl.BlockSpec(a.shape, lambda *_: (0, 0)) for a in attention]

    def kernel(ins, refs):
        outs, (both, total, landed, sems) = refs[:2], refs[2:]

        def bring(at):
            start = pl.multiple_of(piece.start + at * block, block)
            source = ins[2].at[pl.ds(start, block), :]
            return pltpu.make_async_copy(source, landed.at[at], sems.at[at])

        for at in range(min(AHEAD, steps)):
            bring(at).start()
        halves = (slice(0, rows), slice(rows, 2 * rows))
        for at, half in enumerate(halves):
            both[half] = ins[at][...]
            first = jnp.zeros((rows, columns), F32)
            if added:
                first = ins[3 + at][...]
            if attention:
                first = first + jnp.dot(
                    ins[-3 + at][...], ins[-1][...], preferred_element_type=F32
                )
            total[half] = first

        @pl.loop(0, steps)
        def _(at):
            bring(at).wait()

            @pl.when(at + AHEAD < steps)
            def _():
                bring(at + AHEAD).start()

            here = pl.ds(pl.multiple_of(at * block, block), block)
            total[...] += jnp.dot(both[:, here], landed[at], preferred_element_type=F32)

        for out, half in zip(outs, halves):
            out[...] = total[half].astype(out.dtype)

    return call(
        kernel,
        earlier,
        (own, other, weight, *added, *attention),
        specs,
        grid=(1,),
        out_specs=[whole] * 2,
        out_shape=[jax.ShapeDtypeStruct((rows, columns), BF16 if last else F32)] * 2,
        scratch_shapes=[
            pltpu.VMEM((2 * rows, units), BF16),
            pltpu.VMEM((2 * rows, columns), F32),
            pltpu.VMEM((steps, block, columns), BF16),
            pltpu.SemaphoreType.DMA((steps,)),
        ],
    )


def make_body(mesh):
    n_red, n_wide = mesh.shape["red"], mesh.shape["wide"]
    half_wide = n_wide // 2

    def swap(x):
        return lax.ppermute(x, "tok", [(0, 1), (1, 0)])

    def all_red(x):
        parts = [x]
        for shift in range(1, n_red):
            pairs = [(i, (i + shift) % n_red) for i in range(n_red)]
            parts.append(lax.ppermute(x, "red", pairs))
        return parts

    def sum_red(x):
        return sum(a.astype(F32) for a in all_red(x))

    def collect(kept, got, width):
        core, chip = lax.axis_index("tok"), lax.axis_index("wide")
        terms = jnp.concatenate([kept, got], axis=1)

        def block(at):
            start = ((at // half_wide) ^ core) * half_wide + at % half_wide
            return lax.dynamic_slice_in_dim(terms, start * width, width, axis=1)

        total = block(chip).astype(F32)
        for k in range(n_wide - 1, 0, -1):
            pairs = [(i, i ^ k) for i in range(n_wide)]
            total = total + lax.ppermute(block(chip ^ k), "wide", pairs).astype(F32)
        return total

    def body(tokens, ln_gain, q_gain, k_gain, w_qkv, w_up, w_attn, w_down):
        core = lax.axis_index("tok")
        width = tokens.shape[1]
        qkv_rows = w_qkv.reshape(w_qkv.shape[0], w_qkv.shape[1] * w_qkv.shape[2])
        attn_rows = w_attn.reshape(w_attn.shape[0] * w_attn.shape[1], w_attn.shape[2])
        depth, units = w_up.shape
        cuts = slices(tokens.shape[0], SHARES, 16)
        pieces = slices(units, LEAD_PIECES, 128)
        rest_pieces = slices(units, REST_PIECES, 128)

        first = cuts[0].stop
        gain_rows = jnp.broadcast_to(ln_gain[None], (GAIN_ROWS, width))
        lead = jnp.concatenate([gain_rows, tokens[:first]], axis=0)
        lead = lax.all_gather(lead, "wide", axis=1, tiled=True)
        gain = lead[:1]

        def row_sums(raw):
            floats = raw.astype(F32)
            return jnp.stack([jnp.sum(floats, axis=1), jnp.sum(floats * floats, axis=1)])

        def normed(raw, sums, start=0.0):
            sums = sum_red(sums)[:, :, None] / D + start
            values = normalize(raw.astype(F32), sums[0], sums[1], gain).astype(BF16)
            mine = lax.dynamic_slice_in_dim(values, core * depth, depth, axis=1)
            theirs = lax.dynamic_slice_in_dim(values, (1 - core) * depth, depth, axis=1)
            return mine, swap(theirs)

        def project(pair, weight):
            both = jnp.concatenate(pair, axis=0)
            half = both.shape[0] // 2
            part = jnp.dot(both, weight, preferred_element_type=F32)
            far = swap(part[half:].astype(BF16)).astype(F32)
            return (part[:half] + far).astype(BF16)

        weights = [w_up[:, piece] for piece in pieces]
        lead_pair = normed(lead[GAIN_ROWS:], row_sums(lead[GAIN_ROWS:]))
        leads = [project(lead_pair, weights[0])]
        lead_parts = [all_red(leads[0])]
        arrived = gelu_sum(lead_parts[0])

        rest = tokens[first:] + nothing(leads[-1]).astype(BF16)
        rest = lax.all_gather(rest, "wide", axis=1, tiled=True)
        sums = row_sums(rest)
        later_pair = [a + nothing(sums).astype(BF16) for a in lead_pair]
        leads.append(project(later_pair, weights[1]))
        lead_parts.append(all_red(leads[1]))
        rest_pair = normed(rest, sums, nothing(arrived))
        pair = [jnp.concatenate(p, axis=0) for p in zip(lead_pair, rest_pair)]
        arrived_other = swap(arrived)
        every = slice(0, qkv_rows.shape[1])
        near, far = project_rows(*pair, qkv_rows, every, [arrived_other, leads[1]])
        halves, before = [], [near]
        qkv = sum_rows([(near, swap(far))], slice(0, tokens.shape[0]))
        for piece in rest_pieces:
            near, far = project_rows(*rest_pair, w_up, piece, before)
            halves.append((near, swap(far)))
            before = [near]

        def output(have, other, piece, terms, cut, earlier=()):
            last = piece.stop == units
            attention = (attended[cut], attended_other[cut], attn_rows) if last else ()
            return project_hidden(have, other, w_down, piece, terms, attention, last, earlier)

        def chunk_sums(pairs, c, earlier):
            part = slice(cuts[c].start - first, cuts[c].stop - first)
            return sum_rows(pairs, part, [earlier])

        def scatter(kept, got, earlier):
            full = side_by_side(kept, got, core, earlier)
            return full, lax.psum_scatter(full, "wide", scatter_dimension=1, tiled=True)

        terms = output(arrived, arrived_other, pieces[0], (), cuts[0], [halves[-1][0]])
        earlier = [terms[0], halves[-1][1]]
        attended = attend(all_red(qkv), q_gain, k_gain, earlier)
        attended_other = swap(attended)
        second = gelu_sum(lead_parts[1], [attended])
        sums = chunk_sums(halves, 1, second)
        parts = all_red(sums)
        coming = chunk_sums(halves, 2, sums)
        terms = output(second, swap(second), pieces[1], terms, cuts[0], [coming])
        coming = all_red(coming)
        full, got = scatter(terms[0], swap(terms[1]), [])
        scattered = [got]

        hidden = gelu_sum(parts, [full])
        terms = output(hidden, swap(hidden), slice(0, units), (), cuts[1])
        full, got = scatter(terms[0], swap(terms[1]), [scattered[0]])
        scattered.append(got)

        hidden = gelu_sum(coming, [full])
        kept, sent = output(hidden, swap(hidden), slice(0, units), (), cuts[2])
        outs = [tokens[cut].astype(F32) + got.astype(F32) for cut, got in zip(cuts, scattered)]
        outs.append(tokens[cuts[2]].astype(F32) + collect(kept, swap(sent), width))
        return jnp.concatenate(outs, axis=0)

    return body


def solution(mesh):
    return jax.shard_map(
        make_body(mesh),
        mesh=mesh,
        in_specs=(
            P(("grp", "tok"), ("red", "wide")),
            P(("red", "wide")),
            P("wide", None),
            P("wide", None),
            P(("red", "tok"), "wide", None),
            P(("red", "tok"), "wide"),
            P("wide", None, ("red", "tok")),
            P("wide", ("red", "tok")),
        ),
        out_specs=P(("grp", "tok"), ("red", "wide")),
        check_vma=False,
    )
```

```python
import functools
import math

import jax
import jax.numpy as jnp
from jax import lax
from jax.experimental import pallas as pl
from jax.experimental.pallas import tpu as pltpu
from jax.sharding import PartitionSpec as P

D = 6144
PATCHES = 256
EPS = 1e-06
SHARES = (9, 5, 2)
LEAD_PIECES = (1, 1)
REST_PIECES = (2, 1)
AHEAD = 4
GAIN_ROWS = 8
BF16, F32 = jnp.bfloat16, jnp.float32
PARAMS = pltpu.CompilerParams(vmem_limit_bytes=48 * 2**20)
SMALL = pltpu.CompilerParams(vmem_limit_bytes=8 * 2**20)
MIDDLE = pltpu.CompilerParams(vmem_limit_bytes=16 * 2**20)
SOON = pl.CostEstimate(flops=0, bytes_accessed=0, transcendentals=0)


def normalize(values, mean, meansq, gain):
    return (values - mean) * lax.rsqrt(meansq - mean * mean + EPS) * gain.astype(F32)


def head_norm(values, gain):
    mean = jnp.mean(values, axis=-1, keepdims=True)
    meansq = jnp.mean(values * values, axis=-1, keepdims=True)
    return normalize(values, mean, meansq, gain)


def nothing(x):
    corner = x[(0,) * x.ndim].astype(jnp.int32)
    return lax.shift_right_logical(corner & 1, 1).astype(F32)


def slices(size, shares, grain):
    ends = [sum(shares[: i + 1]) * size // sum(shares) for i in range(len(shares))]
    ends = [end // grain * grain for end in ends]
    return [slice(a, b) for a, b in zip([0] + ends[:-1], ends)]


def steps_of(piece):
    size = math.gcd(piece.stop - piece.start, piece.start)
    block = next(b for b in (512, 384, 256, 128) if size % b == 0)
    return block, (piece.stop - piece.start) // block, piece.start // block


def corner_of(x):
    shape = (min(16, x.shape[0]), min(128, x.shape[1]))
    return pl.BlockSpec(shape, lambda *_: (0, 0))


def call(kernel, earlier, operands, specs, params=None, **options):
    def body(*refs):
        n = len(operands)
        kernel(refs[:n], refs[n + len(earlier) :])

    return pl.pallas_call(
        body,
        in_specs=list(specs) + [corner_of(a) for a in earlier],
        compiler_params=params or PARAMS,
        cost_estimate=SOON,
        **options,
    )(*operands, *earlier)


def gelu_sum(parts, earlier=()):
    rows, units = parts[0].shape
    block, steps, _ = steps_of(slice(0, units))
    spec = pl.BlockSpec((rows, block), lambda j: (0, j))

    def kernel(ins, outs):
        up = ins[0][...].astype(F32)
        for part in ins[1:]:
            up = up + part[...].astype(F32)
        outs[0][...] = (0.5 * up * (1.0 + lax.erf(up * 0.5**0.5))).astype(BF16)

    return call(
        kernel,
        earlier,
        parts,
        [spec] * len(parts),
        params=SMALL,
        grid=(steps,),
        out_specs=spec,
        out_shape=jax.ShapeDtypeStruct((rows, units), BF16),
    )


def sum_rows(pairs, cut, earlier=()):
    widths = [near.shape[1] for near, _ in pairs]
    shape = (cut.stop - cut.start, sum(widths))

    def kernel(ins, outs):
        start = 0
        for at, width in enumerate(widths):
            total = ins[2 * at][cut].astype(F32) + ins[2 * at + 1][cut].astype(F32)
            outs[0][:, start : start + width] = total.astype(BF16)
            start += width

    operands = [part for pair in pairs for part in pair]
    return call(
        kernel,
        earlier,
        operands,
        [pl.BlockSpec(part.shape, lambda *_: (0, 0)) for part in operands],
        params=MIDDLE,
        grid=(1,),
        out_specs=pl.BlockSpec(shape, lambda *_: (0, 0)),
        out_shape=jax.ShapeDtypeStruct(shape, BF16),
    )


def side_by_side(kept, got, core, earlier=()):
    rows, columns = kept.shape
    spec = pl.BlockSpec(kept.shape, lambda *_: (0, 0))

    def kernel(ins, outs):
        first = ins[2][0] == 0
        outs[0][:, :columns] = jnp.where(first, ins[0][...], ins[1][...])
        outs[0][:, columns:] = jnp.where(first, ins[1][...], ins[0][...])

    return call(
        kernel,
        earlier,
        (kept, got, core.reshape(1)),
        [spec, spec, pl.BlockSpec(memory_space=pltpu.SMEM)],
        params=SMALL,
        grid=(1,),
        out_specs=pl.BlockSpec((rows, 2 * columns), lambda *_: (0, 0)),
        out_shape=jax.ShapeDtypeStruct((rows, 2 * columns), kept.dtype),
    )


def attend(parts, q_gain, k_gain, earlier=()):
    rows, width = parts[0].shape[0], q_gain.shape[1]
    n = len(parts)

    def kernel(ins, outs):
        def columns(at):
            here = slice(at * width, (at + 1) * width)
            return sum(part[:, here].astype(F32) for part in ins[:n])

        query = head_norm(columns(0), ins[n][...]).astype(BF16)
        key = head_norm(columns(1), ins[n + 1][...]).astype(BF16)
        value = columns(2).astype(BF16).astype(F32)
        for at in range(0, rows, PATCHES):
            image = slice(at, at + PATCHES)
            scores = lax.dot_general(
                query[image], key[image], (((1,), (1,)), ((), ())), preferred_element_type=F32
            )
            scores = scores * width ** (-0.5)
            weights = jnp.exp(scores - jnp.max(scores, axis=-1, keepdims=True))
            total = jnp.sum(weights, axis=-1, keepdims=True)
            acc = jnp.dot(
                weights,
                value[image],
                precision=lax.Precision.HIGHEST,
                preferred_element_type=F32,
            )
            outs[0][image] = (acc / total).astype(BF16)

    whole = [pl.BlockSpec(a.shape, lambda *_: (0, 0)) for a in (*parts, q_gain, k_gain)]
    return call(
        kernel,
        earlier,
        (*parts, q_gain, k_gain),
        whole,
        params=SMALL,
        grid=(1,),
        out_specs=pl.BlockSpec((rows, width), lambda *_: (0, 0)),
        out_shape=jax.ShapeDtypeStruct((rows, width), BF16),
    )


def project_rows(own, other, weight, piece, earlier=()):
    rows, depth = own.shape
    columns = piece.stop - piece.start
    block, steps, _ = steps_of(piece)
    whole = pl.BlockSpec((rows, depth), lambda *_: (0, 0))
    out = pl.BlockSpec((rows, columns), lambda *_: (0, 0))

    def kernel(ins, refs):
        near, far, both, landed, sems = refs

        def bring(at):
            start = pl.multiple_of(piece.start + at * block, block)
            source = ins[2].at[:, pl.ds(start, block)]
            return pltpu.make_async_copy(source, landed.at[at], sems.at[at])

        for at in range(min(AHEAD, steps)):
            bring(at).start()
        both[:rows] = ins[0][...]
        both[rows:] = ins[1][...]

        @pl.loop(0, steps)
        def _(at):
            bring(at).wait()

            @pl.when(at + AHEAD < steps)
            def _():
                bring(at + AHEAD).start()

            part = jnp.dot(both[...], landed[at], preferred_element_type=F32).astype(BF16)
            here = pl.ds(pl.multiple_of(at * block, block), block)
            near[:, here] = part[:rows]
            far[:, here] = part[rows:]

    return call(
        kernel,
        earlier,
        (own, other, weight),
        [whole, whole, pl.BlockSpec(memory_space=pltpu.HBM)],
        grid=(1,),
        out_specs=[out] * 2,
        out_shape=[jax.ShapeDtypeStruct((rows, columns), BF16)] * 2,
        scratch_shapes=[
            pltpu.VMEM((2 * rows, depth), BF16),
            pltpu.VMEM((steps, depth, block), BF16),
            pltpu.SemaphoreType.DMA((steps,)),
        ],
    )


def project_hidden(own, other, weight, piece, added, attention, last, earlier=()):
    rows, units = own.shape
    columns = weight.shape[1]
    block, steps, _ = steps_of(piece)
    whole = pl.BlockSpec((rows, columns), lambda *_: (0, 0))
    part = pl.BlockSpec((rows, units), lambda *_: (0, 0))
    specs = [part, part, pl.BlockSpec(memory_space=pltpu.HBM)]
    specs += [whole] * len(added)
    specs += [pl.BlockSpec(a.shape, lambda *_: (0, 0)) for a in attention]

    def kernel(ins, refs):
        outs, (both, total, landed, sems) = refs[:2], refs[2:]

        def bring(at):
            start = pl.multiple_of(piece.start + at * block, block)
            source = ins[2].at[pl.ds(start, block), :]
            return pltpu.make_async_copy(source, landed.at[at], sems.at[at])

        for at in range(min(AHEAD, steps)):
            bring(at).start()
        halves = (slice(0, rows), slice(rows, 2 * rows))
        for at, half in enumerate(halves):
            both[half] = ins[at][...]
            first = jnp.zeros((rows, columns), F32)
            if added:
                first = ins[3 + at][...]
            if attention:
                first = first + jnp.dot(
                    ins[-3 + at][...], ins[-1][...], preferred_element_type=F32
                )
            total[half] = first

        @pl.loop(0, steps)
        def _(at):
            bring(at).wait()

            @pl.when(at + AHEAD < steps)
            def _():
                bring(at + AHEAD).start()

            here = pl.ds(pl.multiple_of(at * block, block), block)
            total[...] += jnp.dot(both[:, here], landed[at], preferred_element_type=F32)

        for out, half in zip(outs, halves):
            out[...] = total[half].astype(out.dtype)

    return call(
        kernel,
        earlier,
        (own, other, weight, *added, *attention),
        specs,
        grid=(1,),
        out_specs=[whole] * 2,
        out_shape=[jax.ShapeDtypeStruct((rows, columns), BF16 if last else F32)] * 2,
        scratch_shapes=[
            pltpu.VMEM((2 * rows, units), BF16),
            pltpu.VMEM((2 * rows, columns), F32),
            pltpu.VMEM((steps, block, columns), BF16),
            pltpu.SemaphoreType.DMA((steps,)),
        ],
    )


def make_body(mesh):
    n_red, n_wide = mesh.shape["red"], mesh.shape["wide"]
    half_wide = n_wide // 2

    def swap(x):
        return lax.ppermute(x, "tok", [(0, 1), (1, 0)])

    def all_red(x):
        parts = [x]
        for shift in range(1, n_red):
            pairs = [(i, (i + shift) % n_red) for i in range(n_red)]
            parts.append(lax.ppermute(x, "red", pairs))
        return parts

    def sum_red(x):
        return sum(a.astype(F32) for a in all_red(x))

    def collect(kept, got, width):
        core, chip = lax.axis_index("tok"), lax.axis_index("wide")
        terms = jnp.concatenate([kept, got], axis=1)

        def block(at):
            start = ((at // half_wide) ^ core) * half_wide + at % half_wide
            return lax.dynamic_slice_in_dim(terms, start * width, width, axis=1)

        total = block(chip).astype(F32)
        for k in range(n_wide - 1, 0, -1):
            pairs = [(i, i ^ k) for i in range(n_wide)]
            total = total + lax.ppermute(block(chip ^ k), "wide", pairs).astype(F32)
        return total

    def body(tokens, ln_gain, q_gain, k_gain, w_qkv, w_up, w_attn, w_down):
        core = lax.axis_index("tok")
        width = tokens.shape[1]
        qkv_rows = w_qkv.reshape(w_qkv.shape[0], w_qkv.shape[1] * w_qkv.shape[2])
        attn_rows = w_attn.reshape(w_attn.shape[0] * w_attn.shape[1], w_attn.shape[2])
        depth, units = w_up.shape
        cuts = slices(tokens.shape[0], SHARES, 16)
        pieces = slices(units, LEAD_PIECES, 128)
        rest_pieces = slices(units, REST_PIECES, 128)

        first = cuts[0].stop
        gain_rows = jnp.broadcast_to(ln_gain[None], (GAIN_ROWS, width))
        lead = jnp.concatenate([gain_rows, tokens[:first]], axis=0)
        lead = lax.all_gather(lead, "wide", axis=1, tiled=True)
        gain = lead[:1]

        def row_sums(raw):
            floats = raw.astype(F32)
            return jnp.stack([jnp.sum(floats, axis=1), jnp.sum(floats * floats, axis=1)])

        def normed(raw, sums, start=0.0):
            sums = sum_red(sums)[:, :, None] / D + start
            values = normalize(raw.astype(F32), sums[0], sums[1], gain).astype(BF16)
            mine = lax.dynamic_slice_in_dim(values, core * depth, depth, axis=1)
            theirs = lax.dynamic_slice_in_dim(values, (1 - core) * depth, depth, axis=1)
            return mine, swap(theirs)

        def project(pair, weight):
            both = jnp.concatenate(pair, axis=0)
            half = both.shape[0] // 2
            part = jnp.dot(both, weight, preferred_element_type=F32)
            far = swap(part[half:].astype(BF16)).astype(F32)
            return (part[:half] + far).astype(BF16)

        weights = [w_up[:, piece] for piece in pieces]
        lead_pair = normed(lead[GAIN_ROWS:], row_sums(lead[GAIN_ROWS:]))
        leads = [project(lead_pair, weights[0])]
        lead_parts = [all_red(leads[0])]
        arrived = gelu_sum(lead_parts[0])

        rest = tokens[first:] + nothing(leads[-1]).astype(BF16)
        rest = lax.all_gather(rest, "wide", axis=1, tiled=True)
        sums = row_sums(rest)
        later_pair = [a + nothing(sums).astype(BF16) for a in lead_pair]
        leads.append(project(later_pair, weights[1]))
        lead_parts.append(all_red(leads[1]))
        rest_pair = normed(rest, sums, nothing(arrived))
        pair = [jnp.concatenate(p, axis=0) for p in zip(lead_pair, rest_pair)]
        arrived_other = swap(arrived)
        every = slice(0, qkv_rows.shape[1])
        near, far = project_rows(*pair, qkv_rows, every, [arrived_other, leads[1]])
        halves, before = [], [near]
        qkv = sum_rows([(near, swap(far))], slice(0, tokens.shape[0]))
        for piece in rest_pieces:
            near, far = project_rows(*rest_pair, w_up, piece, before)
            halves.append((near, swap(far)))
            before = [near]

        def output(have, other, piece, terms, cut, earlier=()):
            last = piece.stop == units
            attention = (attended[cut], attended_other[cut], attn_rows) if last else ()
            return project_hidden(have, other, w_down, piece, terms, attention, last, earlier)

        def chunk_sums(pairs, c, earlier):
            part = slice(cuts[c].start - first, cuts[c].stop - first)
            return sum_rows(pairs, part, [earlier])

        def scatter(kept, got, earlier):
            full = side_by_side(kept, got, core, earlier)
            return full, lax.psum_scatter(full, "wide", scatter_dimension=1, tiled=True)

        terms = output(arrived, arrived_other, pieces[0], (), cuts[0], [halves[-1][0]])
        earlier = [terms[0], halves[-1][1]]
        attended = attend(all_red(qkv), q_gain, k_gain, earlier)
        attended_other = swap(attended)
        second = gelu_sum(lead_parts[1], [attended])
        sums = chunk_sums(halves, 1, second)
        parts = all_red(sums)
        coming = chunk_sums(halves, 2, sums)
        terms = output(second, swap(second), pieces[1], terms, cuts[0], [coming])
        coming = all_red(coming)
        full, got = scatter(terms[0], swap(terms[1]), [])
        scattered = [got]

        hidden = gelu_sum(parts, [full])
        terms = output(hidden, swap(hidden), slice(0, units), (), cuts[1])
        full, got = scatter(terms[0], swap(terms[1]), [scattered[0]])
        scattered.append(got)

        hidden = gelu_sum(coming, [full])
        kept, sent = output(hidden, swap(hidden), slice(0, units), (), cuts[2])
        outs = [tokens[cut].astype(F32) + got.astype(F32) for cut, got in zip(cuts, scattered)]
        outs.append(tokens[cuts[2]].astype(F32) + collect(kept, swap(sent), width))
        return jnp.concatenate(outs, axis=0)

    return body


def solution(mesh):
    return jax.shard_map(
        make_body(mesh),
        mesh=mesh,
        in_specs=(
            P(("grp", "tok"), ("red", "wide")),
            P(("red", "wide")),
            P("wide", None),
            P("wide", None),
            P(("red", "tok"), "wide", None),
            P(("red", "tok"), "wide"),
            P("wide", None, ("red", "tok")),
            P("wide", ("red", "tok")),
        ),
        out_specs=P(("grp", "tok"), ("red", "wide")),
        check_vma=False,
    )
```

```python
import functools
import math

import jax
import jax.numpy as jnp
from jax import lax
from jax.experimental import pallas as pl
from jax.experimental.pallas import tpu as pltpu
from jax.sharding import PartitionSpec as P

D = 6144
PATCHES = 256
EPS = 1e-06
SHARES = (9, 5, 2)
LEAD_PIECES = (1, 1)
REST_PIECES = (2, 1)
AHEAD = 4
GAIN_ROWS = 8
BF16, F32 = jnp.bfloat16, jnp.float32
PARAMS = pltpu.CompilerParams(vmem_limit_bytes=48 * 2**20)
SMALL = pltpu.CompilerParams(vmem_limit_bytes=8 * 2**20)
MIDDLE = pltpu.CompilerParams(vmem_limit_bytes=16 * 2**20)
SOON = pl.CostEstimate(flops=0, bytes_accessed=0, transcendentals=0)


def normalize(values, mean, meansq, gain):
    return (values - mean) * lax.rsqrt(meansq - mean * mean + EPS) * gain.astype(F32)


def head_norm(values, gain):
    mean = jnp.mean(values, axis=-1, keepdims=True)
    meansq = jnp.mean(values * values, axis=-1, keepdims=True)
    return normalize(values, mean, meansq, gain)


def nothing(x):
    corner = x[(0,) * x.ndim].astype(jnp.int32)
    return lax.shift_right_logical(corner & 1, 1).astype(F32)


def slices(size, shares, grain):
    ends = [sum(shares[: i + 1]) * size // sum(shares) for i in range(len(shares))]
    ends = [end // grain * grain for end in ends]
    return [slice(a, b) for a, b in zip([0] + ends[:-1], ends)]


def steps_of(piece):
    size = math.gcd(piece.stop - piece.start, piece.start)
    block = next(b for b in (512, 384, 256, 128) if size % b == 0)
    return block, (piece.stop - piece.start) // block, piece.start // block


def corner_of(x):
    shape = (min(16, x.shape[0]), min(128, x.shape[1]))
    return pl.BlockSpec(shape, lambda *_: (0, 0))


def call(kernel, earlier, operands, specs, params=None, **options):
    def body(*refs):
        n = len(operands)
        kernel(refs[:n], refs[n + len(earlier) :])

    return pl.pallas_call(
        body,
        in_specs=list(specs) + [corner_of(a) for a in earlier],
        compiler_params=params or PARAMS,
        cost_estimate=SOON,
        **options,
    )(*operands, *earlier)


def gelu_sum(parts, earlier=()):
    rows, units = parts[0].shape
    block, steps, _ = steps_of(slice(0, units))
    spec = pl.BlockSpec((rows, block), lambda j: (0, j))

    def kernel(ins, outs):
        up = ins[0][...].astype(F32)
        for part in ins[1:]:
            up = up + part[...].astype(F32)
        outs[0][...] = (0.5 * up * (1.0 + lax.erf(up * 0.5**0.5))).astype(BF16)

    return call(
        kernel,
        earlier,
        parts,
        [spec] * len(parts),
        params=SMALL,
        grid=(steps,),
        out_specs=spec,
        out_shape=jax.ShapeDtypeStruct((rows, units), BF16),
    )


def sum_rows(pairs, cut, earlier=()):
    widths = [near.shape[1] for near, _ in pairs]
    shape = (cut.stop - cut.start, sum(widths))

    def kernel(ins, outs):
        start = 0
        for at, width in enumerate(widths):
            total = ins[2 * at][cut].astype(F32) + ins[2 * at + 1][cut].astype(F32)
            outs[0][:, start : start + width] = total.astype(BF16)
            start += width

    operands = [part for pair in pairs for part in pair]
    return call(
        kernel,
        earlier,
        operands,
        [pl.BlockSpec(part.shape, lambda *_: (0, 0)) for part in operands],
        params=MIDDLE,
        grid=(1,),
        out_specs=pl.BlockSpec(shape, lambda *_: (0, 0)),
        out_shape=jax.ShapeDtypeStruct(shape, BF16),
    )


def side_by_side(kept, got, core, earlier=()):
    rows, columns = kept.shape
    spec = pl.BlockSpec(kept.shape, lambda *_: (0, 0))

    def kernel(ins, outs):
        first = ins[2][0] == 0
        outs[0][:, :columns] = jnp.where(first, ins[0][...], ins[1][...])
        outs[0][:, columns:] = jnp.where(first, ins[1][...], ins[0][...])

    return call(
        kernel,
        earlier,
        (kept, got, core.reshape(1)),
        [spec, spec, pl.BlockSpec(memory_space=pltpu.SMEM)],
        params=SMALL,
        grid=(1,),
        out_specs=pl.BlockSpec((rows, 2 * columns), lambda *_: (0, 0)),
        out_shape=jax.ShapeDtypeStruct((rows, 2 * columns), kept.dtype),
    )


def attend(parts, q_gain, k_gain, earlier=()):
    rows, width = parts[0].shape[0], q_gain.shape[1]
    n = len(parts)

    def kernel(ins, outs):
        def columns(at):
            here = slice(at * width, (at + 1) * width)
            return sum(part[:, here].astype(F32) for part in ins[:n])

        query = head_norm(columns(0), ins[n][...]).astype(BF16)
        key = head_norm(columns(1), ins[n + 1][...]).astype(BF16)
        value = columns(2).astype(BF16).astype(F32)
        for at in range(0, rows, PATCHES):
            image = slice(at, at + PATCHES)
            scores = lax.dot_general(
                query[image], key[image], (((1,), (1,)), ((), ())), preferred_element_type=F32
            )
            scores = scores * width ** (-0.5)
            weights = jnp.exp(scores - jnp.max(scores, axis=-1, keepdims=True))
            total = jnp.sum(weights, axis=-1, keepdims=True)
            acc = jnp.dot(
                weights,
                value[image],
                precision=lax.Precision.HIGHEST,
                preferred_element_type=F32,
            )
            outs[0][image] = (acc / total).astype(BF16)

    whole = [pl.BlockSpec(a.shape, lambda *_: (0, 0)) for a in (*parts, q_gain, k_gain)]
    return call(
        kernel,
        earlier,
        (*parts, q_gain, k_gain),
        whole,
        params=SMALL,
        grid=(1,),
        out_specs=pl.BlockSpec((rows, width), lambda *_: (0, 0)),
        out_shape=jax.ShapeDtypeStruct((rows, width), BF16),
    )


def project_rows(own, other, weight, piece, earlier=()):
    rows, depth = own.shape
    columns = piece.stop - piece.start
    block, steps, _ = steps_of(piece)
    whole = pl.BlockSpec((rows, depth), lambda *_: (0, 0))
    out = pl.BlockSpec((rows, columns), lambda *_: (0, 0))

    def kernel(ins, refs):
        near, far, both, landed, sems = refs

        def bring(at):
            start = pl.multiple_of(piece.start + at * block, block)
            source = ins[2].at[:, pl.ds(start, block)]
            return pltpu.make_async_copy(source, landed.at[at], sems.at[at])

        for at in range(min(AHEAD, steps)):
            bring(at).start()
        both[:rows] = ins[0][...]
        both[rows:] = ins[1][...]

        @pl.loop(0, steps)
        def _(at):
            bring(at).wait()

            @pl.when(at + AHEAD < steps)
            def _():
                bring(at + AHEAD).start()

            part = jnp.dot(both[...], landed[at], preferred_element_type=F32).astype(BF16)
            here = pl.ds(pl.multiple_of(at * block, block), block)
            near[:, here] = part[:rows]
            far[:, here] = part[rows:]

    return call(
        kernel,
        earlier,
        (own, other, weight),
        [whole, whole, pl.BlockSpec(memory_space=pltpu.HBM)],
        grid=(1,),
        out_specs=[out] * 2,
        out_shape=[jax.ShapeDtypeStruct((rows, columns), BF16)] * 2,
        scratch_shapes=[
            pltpu.VMEM((2 * rows, depth), BF16),
            pltpu.VMEM((steps, depth, block), BF16),
            pltpu.SemaphoreType.DMA((steps,)),
        ],
    )


def project_hidden(own, other, weight, piece, added, attention, last, earlier=()):
    rows, units = own.shape
    columns = weight.shape[1]
    block, steps, _ = steps_of(piece)
    whole = pl.BlockSpec((rows, columns), lambda *_: (0, 0))
    part = pl.BlockSpec((rows, units), lambda *_: (0, 0))
    specs = [part, part, pl.BlockSpec(memory_space=pltpu.HBM)]
    specs += [whole] * len(added)
    specs += [pl.BlockSpec(a.shape, lambda *_: (0, 0)) for a in attention]

    def kernel(ins, refs):
        outs, (both, total, landed, sems) = refs[:2], refs[2:]

        def bring(at):
            start = pl.multiple_of(piece.start + at * block, block)
            source = ins[2].at[pl.ds(start, block), :]
            return pltpu.make_async_copy(source, landed.at[at], sems.at[at])

        for at in range(min(AHEAD, steps)):
            bring(at).start()
        halves = (slice(0, rows), slice(rows, 2 * rows))
        for at, half in enumerate(halves):
            both[half] = ins[at][...]
            first = jnp.zeros((rows, columns), F32)
            if added:
                first = ins[3 + at][...]
            if attention:
                first = first + jnp.dot(
                    ins[-3 + at][...], ins[-1][...], preferred_element_type=F32
                )
            total[half] = first

        @pl.loop(0, steps)
        def _(at):
            bring(at).wait()

            @pl.when(at + AHEAD < steps)
            def _():
                bring(at + AHEAD).start()

            here = pl.ds(pl.multiple_of(at * block, block), block)
            total[...] += jnp.dot(both[:, here], landed[at], preferred_element_type=F32)

        for out, half in zip(outs, halves):
            out[...] = total[half].astype(out.dtype)

    return call(
        kernel,
        earlier,
        (own, other, weight, *added, *attention),
        specs,
        grid=(1,),
        out_specs=[whole] * 2,
        out_shape=[jax.ShapeDtypeStruct((rows, columns), BF16 if last else F32)] * 2,
        scratch_shapes=[
            pltpu.VMEM((2 * rows, units), BF16),
            pltpu.VMEM((2 * rows, columns), F32),
            pltpu.VMEM((steps, block, columns), BF16),
            pltpu.SemaphoreType.DMA((steps,)),
        ],
    )


def make_body(mesh):
    n_red, n_wide = mesh.shape["red"], mesh.shape["wide"]
    half_wide = n_wide // 2

    def swap(x):
        return lax.ppermute(x, "tok", [(0, 1), (1, 0)])

    def all_red(x):
        parts = [x]
        for shift in range(1, n_red):
            pairs = [(i, (i + shift) % n_red) for i in range(n_red)]
            parts.append(lax.ppermute(x, "red", pairs))
        return parts

    def sum_red(x):
        return sum(a.astype(F32) for a in all_red(x))

    def collect(kept, got, width):
        core, chip = lax.axis_index("tok"), lax.axis_index("wide")
        terms = jnp.concatenate([kept, got], axis=1)

        def block(at):
            start = ((at // half_wide) ^ core) * half_wide + at % half_wide
            return lax.dynamic_slice_in_dim(terms, start * width, width, axis=1)

        total = block(chip).astype(F32)
        for k in range(n_wide - 1, 0, -1):
            pairs = [(i, i ^ k) for i in range(n_wide)]
            total = total + lax.ppermute(block(chip ^ k), "wide", pairs).astype(F32)
        return total

    def body(tokens, ln_gain, q_gain, k_gain, w_qkv, w_up, w_attn, w_down):
        core = lax.axis_index("tok")
        width = tokens.shape[1]
        qkv_rows = w_qkv.reshape(w_qkv.shape[0], w_qkv.shape[1] * w_qkv.shape[2])
        attn_rows = w_attn.reshape(w_attn.shape[0] * w_attn.shape[1], w_attn.shape[2])
        depth, units = w_up.shape
        cuts = slices(tokens.shape[0], SHARES, 16)
        pieces = slices(units, LEAD_PIECES, 128)
        rest_pieces = slices(units, REST_PIECES, 128)

        first = cuts[0].stop
        gain_rows = jnp.broadcast_to(ln_gain[None], (GAIN_ROWS, width))
        lead = jnp.concatenate([gain_rows, tokens[:first]], axis=0)
        lead = lax.all_gather(lead, "wide", axis=1, tiled=True)
        gain = lead[:1]

        def row_sums(raw):
            floats = raw.astype(F32)
            return jnp.stack([jnp.sum(floats, axis=1), jnp.sum(floats * floats, axis=1)])

        def normed(raw, sums, start=0.0):
            sums = sum_red(sums)[:, :, None] / D + start
            values = normalize(raw.astype(F32), sums[0], sums[1], gain).astype(BF16)
            mine = lax.dynamic_slice_in_dim(values, core * depth, depth, axis=1)
            theirs = lax.dynamic_slice_in_dim(values, (1 - core) * depth, depth, axis=1)
            return mine, swap(theirs)

        def project(pair, weight):
            both = jnp.concatenate(pair, axis=0)
            half = both.shape[0] // 2
            part = jnp.dot(both, weight, preferred_element_type=F32)
            far = swap(part[half:].astype(BF16)).astype(F32)
            return (part[:half] + far).astype(BF16)

        weights = [w_up[:, piece] for piece in pieces]
        lead_pair = normed(lead[GAIN_ROWS:], row_sums(lead[GAIN_ROWS:]))
        leads = [project(lead_pair, weights[0])]
        lead_parts = [all_red(leads[0])]
        arrived = gelu_sum(lead_parts[0])

        rest = tokens[first:] + nothing(leads[-1]).astype(BF16)
        rest = lax.all_gather(rest, "wide", axis=1, tiled=True)
        sums = row_sums(rest)
        later_pair = [a + nothing(sums).astype(BF16) for a in lead_pair]
        leads.append(project(later_pair, weights[1]))
        lead_parts.append(all_red(leads[1]))
        rest_pair = normed(rest, sums, nothing(arrived))
        pair = [jnp.concatenate(p, axis=0) for p in zip(lead_pair, rest_pair)]
        arrived_other = swap(arrived)
        every = slice(0, qkv_rows.shape[1])
        near, far = project_rows(*pair, qkv_rows, every, [arrived_other, leads[1]])
        halves, before = [], [near]
        qkv = sum_rows([(near, swap(far))], slice(0, tokens.shape[0]))
        for piece in rest_pieces:
            near, far = project_rows(*rest_pair, w_up, piece, before)
            halves.append((near, swap(far)))
            before = [near]

        def output(have, other, piece, terms, cut, earlier=()):
            last = piece.stop == units
            attention = (attended[cut], attended_other[cut], attn_rows) if last else ()
            return project_hidden(have, other, w_down, piece, terms, attention, last, earlier)

        def chunk_sums(pairs, c, earlier):
            part = slice(cuts[c].start - first, cuts[c].stop - first)
            return sum_rows(pairs, part, [earlier])

        def scatter(kept, got, earlier):
            full = side_by_side(kept, got, core, earlier)
            return full, lax.psum_scatter(full, "wide", scatter_dimension=1, tiled=True)

        terms = output(arrived, arrived_other, pieces[0], (), cuts[0], [halves[-1][0]])
        earlier = [terms[0], *(far for _, far in halves)]
        attended = attend(all_red(qkv), q_gain, k_gain, earlier)
        attended_other = swap(attended)
        second = gelu_sum(lead_parts[1], [attended])
        sums = chunk_sums(halves, 1, second)
        parts = all_red(sums)
        coming = chunk_sums(halves, 2, sums)
        terms = output(second, swap(second), pieces[1], terms, cuts[0], [coming])
        coming = all_red(coming)
        full, got = scatter(terms[0], swap(terms[1]), [])
        scattered = [got]

        hidden = gelu_sum(parts, [full])
        terms = output(hidden, swap(hidden), slice(0, units), (), cuts[1])
        full, got = scatter(terms[0], swap(terms[1]), [scattered[0]])
        scattered.append(got)

        hidden = gelu_sum(coming, [full])
        kept, sent = output(hidden, swap(hidden), slice(0, units), (), cuts[2])
        outs = [got.astype(F32) for got in scattered]
        outs.append(collect(kept, swap(sent), width))
        return tokens.astype(F32) + jnp.concatenate(outs, axis=0)

    return body


def solution(mesh):
    return jax.shard_map(
        make_body(mesh),
        mesh=mesh,
        in_specs=(
            P(("grp", "tok"), ("red", "wide")),
            P(("red", "wide")),
            P("wide", None),
            P("wide", None),
            P(("red", "tok"), "wide", None),
            P(("red", "tok"), "wide"),
            P("wide", None, ("red", "tok")),
            P("wide", ("red", "tok")),
        ),
        out_specs=P(("grp", "tok"), ("red", "wide")),
        check_vma=False,
    )
```

```python
import functools
import math

import jax
import jax.numpy as jnp
from jax import lax
from jax.experimental import pallas as pl
from jax.experimental.pallas import tpu as pltpu
from jax.sharding import PartitionSpec as P

D = 6144
PATCHES = 256
EPS = 1e-06
SHARES = (8, 5, 3)
LEAD_PIECES = (1, 1)
REST_PIECES = (2, 1)
AHEAD = 6
GAIN_ROWS = 8
BF16, F32 = jnp.bfloat16, jnp.float32
PARAMS = pltpu.CompilerParams(vmem_limit_bytes=48 * 2**20)
SMALL = pltpu.CompilerParams(vmem_limit_bytes=8 * 2**20)
MIDDLE = pltpu.CompilerParams(vmem_limit_bytes=16 * 2**20)
SOON = pl.CostEstimate(flops=0, bytes_accessed=0, transcendentals=0)


def normalize(values, mean, meansq, gain):
    return (values - mean) * lax.rsqrt(meansq - mean * mean + EPS) * gain.astype(F32)


def head_norm(values, gain):
    mean = jnp.mean(values, axis=-1, keepdims=True)
    meansq = jnp.mean(values * values, axis=-1, keepdims=True)
    return normalize(values, mean, meansq, gain)


def nothing(x):
    corner = x[(0,) * x.ndim].astype(jnp.int32)
    return lax.shift_right_logical(corner & 1, 1).astype(F32)


def slices(size, shares, grain):
    ends = [sum(shares[: i + 1]) * size // sum(shares) for i in range(len(shares))]
    ends = [end // grain * grain for end in ends]
    return [slice(a, b) for a, b in zip([0] + ends[:-1], ends)]


def steps_of(piece):
    size = math.gcd(piece.stop - piece.start, piece.start)
    block = next(b for b in (512, 384, 256, 128) if size % b == 0)
    return block, (piece.stop - piece.start) // block, piece.start // block


def corner_of(x):
    shape = (min(16, x.shape[0]), min(128, x.shape[1]))
    return pl.BlockSpec(shape, lambda *_: (0, 0))


def call(kernel, earlier, operands, specs, params=None, **options):
    def body(*refs):
        n = len(operands)
        kernel(refs[:n], refs[n + len(earlier) :])

    return pl.pallas_call(
        body,
        in_specs=list(specs) + [corner_of(a) for a in earlier],
        compiler_params=params or PARAMS,
        cost_estimate=SOON,
        **options,
    )(*operands, *earlier)


def gelu_sum(parts, earlier=()):
    rows, units = parts[0].shape
    block, steps, _ = steps_of(slice(0, units))
    spec = pl.BlockSpec((rows, block), lambda j: (0, j))

    def kernel(ins, outs):
        up = ins[0][...].astype(F32)
        for part in ins[1:]:
            up = up + part[...].astype(F32)
        outs[0][...] = (0.5 * up * (1.0 + lax.erf(up * 0.5**0.5))).astype(BF16)

    return call(
        kernel,
        earlier,
        parts,
        [spec] * len(parts),
        params=SMALL,
        grid=(steps,),
        out_specs=spec,
        out_shape=jax.ShapeDtypeStruct((rows, units), BF16),
    )


def sum_rows(pairs, cut, earlier=()):
    widths = [near.shape[1] for near, _ in pairs]
    shape = (cut.stop - cut.start, sum(widths))

    def kernel(ins, outs):
        start = 0
        for at, width in enumerate(widths):
            total = ins[2 * at][cut].astype(F32) + ins[2 * at + 1][cut].astype(F32)
            outs[0][:, start : start + width] = total.astype(BF16)
            start += width

    operands = [part for pair in pairs for part in pair]
    return call(
        kernel,
        earlier,
        operands,
        [pl.BlockSpec(part.shape, lambda *_: (0, 0)) for part in operands],
        params=MIDDLE,
        grid=(1,),
        out_specs=pl.BlockSpec(shape, lambda *_: (0, 0)),
        out_shape=jax.ShapeDtypeStruct(shape, BF16),
    )


def side_by_side(kept, got, core, earlier=()):
    rows, columns = kept.shape
    spec = pl.BlockSpec(kept.shape, lambda *_: (0, 0))

    def kernel(ins, outs):
        first = ins[2][0] == 0
        outs[0][:, :columns] = jnp.where(first, ins[0][...], ins[1][...])
        outs[0][:, columns:] = jnp.where(first, ins[1][...], ins[0][...])

    return call(
        kernel,
        earlier,
        (kept, got, core.reshape(1)),
        [spec, spec, pl.BlockSpec(memory_space=pltpu.SMEM)],
        params=SMALL,
        grid=(1,),
        out_specs=pl.BlockSpec((rows, 2 * columns), lambda *_: (0, 0)),
        out_shape=jax.ShapeDtypeStruct((rows, 2 * columns), kept.dtype),
    )


def attend(parts, q_gain, k_gain, earlier=()):
    rows, width = parts[0].shape[0], q_gain.shape[1]
    n = len(parts)

    def kernel(ins, outs):
        def columns(at):
            here = slice(at * width, (at + 1) * width)
            return sum(part[:, here].astype(F32) for part in ins[:n])

        query = head_norm(columns(0), ins[n][...]).astype(BF16)
        key = head_norm(columns(1), ins[n + 1][...]).astype(BF16)
        value = columns(2).astype(BF16).astype(F32)
        for at in range(0, rows, PATCHES):
            image = slice(at, at + PATCHES)
            scores = lax.dot_general(
                query[image], key[image], (((1,), (1,)), ((), ())), preferred_element_type=F32
            )
            scores = scores * width ** (-0.5)
            weights = jnp.exp(scores - jnp.max(scores, axis=-1, keepdims=True))
            total = jnp.sum(weights, axis=-1, keepdims=True)
            acc = jnp.dot(
                weights,
                value[image],
                precision=lax.Precision.HIGHEST,
                preferred_element_type=F32,
            )
            outs[0][image] = (acc / total).astype(BF16)

    whole = [pl.BlockSpec(a.shape, lambda *_: (0, 0)) for a in (*parts, q_gain, k_gain)]
    return call(
        kernel,
        earlier,
        (*parts, q_gain, k_gain),
        whole,
        params=SMALL,
        grid=(1,),
        out_specs=pl.BlockSpec((rows, width), lambda *_: (0, 0)),
        out_shape=jax.ShapeDtypeStruct((rows, width), BF16),
    )


def project_rows(own, other, weight, piece, earlier=()):
    rows, depth = own.shape
    columns = piece.stop - piece.start
    block, steps, _ = steps_of(piece)
    whole = pl.BlockSpec((rows, depth), lambda *_: (0, 0))
    out = pl.BlockSpec((rows, columns), lambda *_: (0, 0))

    def kernel(ins, refs):
        near, far, both, landed, sems = refs

        def bring(at):
            start = pl.multiple_of(piece.start + at * block, block)
            source = ins[2].at[:, pl.ds(start, block)]
            return pltpu.make_async_copy(source, landed.at[at], sems.at[at])

        for at in range(min(AHEAD, steps)):
            bring(at).start()
        both[:rows] = ins[0][...]
        both[rows:] = ins[1][...]

        @pl.loop(0, steps)
        def _(at):
            bring(at).wait()

            @pl.when(at + AHEAD < steps)
            def _():
                bring(at + AHEAD).start()

            part = jnp.dot(both[...], landed[at], preferred_element_type=F32).astype(BF16)
            here = pl.ds(pl.multiple_of(at * block, block), block)
            near[:, here] = part[:rows]
            far[:, here] = part[rows:]

    return call(
        kernel,
        earlier,
        (own, other, weight),
        [whole, whole, pl.BlockSpec(memory_space=pltpu.HBM)],
        grid=(1,),
        out_specs=[out] * 2,
        out_shape=[jax.ShapeDtypeStruct((rows, columns), BF16)] * 2,
        scratch_shapes=[
            pltpu.VMEM((2 * rows, depth), BF16),
            pltpu.VMEM((steps, depth, block), BF16),
            pltpu.SemaphoreType.DMA((steps,)),
        ],
    )


def project_hidden(own, other, weight, piece, added, attention, last, earlier=()):
    rows, units = own.shape
    columns = weight.shape[1]
    block, steps, _ = steps_of(piece)
    whole = pl.BlockSpec((rows, columns), lambda *_: (0, 0))
    part = pl.BlockSpec((rows, units), lambda *_: (0, 0))
    specs = [part, part, pl.BlockSpec(memory_space=pltpu.HBM)]
    specs += [whole] * len(added)
    specs += [pl.BlockSpec(a.shape, lambda *_: (0, 0)) for a in attention]

    def kernel(ins, refs):
        outs, (both, total, landed, sems) = refs[:2], refs[2:]

        def bring(at):
            start = pl.multiple_of(piece.start + at * block, block)
            source = ins[2].at[pl.ds(start, block), :]
            return pltpu.make_async_copy(source, landed.at[at], sems.at[at])

        for at in range(min(AHEAD, steps)):
            bring(at).start()
        halves = (slice(0, rows), slice(rows, 2 * rows))
        for at, half in enumerate(halves):
            both[half] = ins[at][...]
            first = jnp.zeros((rows, columns), F32)
            if added:
                first = ins[3 + at][...]
            if attention:
                first = first + jnp.dot(
                    ins[-3 + at][...], ins[-1][...], preferred_element_type=F32
                )
            total[half] = first

        @pl.loop(0, steps)
        def _(at):
            bring(at).wait()

            @pl.when(at + AHEAD < steps)
            def _():
                bring(at + AHEAD).start()

            here = pl.ds(pl.multiple_of(at * block, block), block)
            total[...] += jnp.dot(both[:, here], landed[at], preferred_element_type=F32)

        for out, half in zip(outs, halves):
            out[...] = total[half].astype(out.dtype)

    return call(
        kernel,
        earlier,
        (own, other, weight, *added, *attention),
        specs,
        grid=(1,),
        out_specs=[whole] * 2,
        out_shape=[jax.ShapeDtypeStruct((rows, columns), BF16 if last else F32)] * 2,
        scratch_shapes=[
            pltpu.VMEM((2 * rows, units), BF16),
            pltpu.VMEM((2 * rows, columns), F32),
            pltpu.VMEM((steps, block, columns), BF16),
            pltpu.SemaphoreType.DMA((steps,)),
        ],
    )


def make_body(mesh):
    n_red, n_wide = mesh.shape["red"], mesh.shape["wide"]
    half_wide = n_wide // 2

    def swap(x):
        return lax.ppermute(x, "tok", [(0, 1), (1, 0)])

    def all_red(x):
        parts = [x]
        for shift in range(1, n_red):
            pairs = [(i, (i + shift) % n_red) for i in range(n_red)]
            parts.append(lax.ppermute(x, "red", pairs))
        return parts

    def sum_red(x):
        return sum(a.astype(F32) for a in all_red(x))

    def collect(kept, got, width):
        core, chip = lax.axis_index("tok"), lax.axis_index("wide")
        terms = jnp.concatenate([kept, got], axis=1)

        def block(at):
            start = ((at // half_wide) ^ core) * half_wide + at % half_wide
            return lax.dynamic_slice_in_dim(terms, start * width, width, axis=1)

        total = block(chip).astype(F32)
        for k in range(n_wide - 1, 0, -1):
            pairs = [(i, i ^ k) for i in range(n_wide)]
            total = total + lax.ppermute(block(chip ^ k), "wide", pairs).astype(F32)
        return total

    def body(tokens, ln_gain, q_gain, k_gain, w_qkv, w_up, w_attn, w_down):
        core = lax.axis_index("tok")
        width = tokens.shape[1]
        qkv_rows = w_qkv.reshape(w_qkv.shape[0], w_qkv.shape[1] * w_qkv.shape[2])
        attn_rows = w_attn.reshape(w_attn.shape[0] * w_attn.shape[1], w_attn.shape[2])
        depth, units = w_up.shape
        cuts = slices(tokens.shape[0], SHARES, 16)
        pieces = slices(units, LEAD_PIECES, 128)
        rest_pieces = slices(units, REST_PIECES, 128)

        first = cuts[0].stop
        gain_rows = jnp.broadcast_to(ln_gain[None], (GAIN_ROWS, width))
        lead = jnp.concatenate([gain_rows, tokens[:first]], axis=0)
        lead = lax.all_gather(lead, "wide", axis=1, tiled=True)
        gain = lead[:1]

        def row_sums(raw):
            floats = raw.astype(F32)
            return jnp.stack([jnp.sum(floats, axis=1), jnp.sum(floats * floats, axis=1)])

        def normed(raw, sums, start=0.0):
            sums = sum_red(sums)[:, :, None] / D + start
            values = normalize(raw.astype(F32), sums[0], sums[1], gain).astype(BF16)
            mine = lax.dynamic_slice_in_dim(values, core * depth, depth, axis=1)
            theirs = lax.dynamic_slice_in_dim(values, (1 - core) * depth, depth, axis=1)
            return mine, swap(theirs)

        def project(pair, weight):
            both = jnp.concatenate(pair, axis=0)
            half = both.shape[0] // 2
            part = jnp.dot(both, weight, preferred_element_type=F32)
            far = swap(part[half:].astype(BF16)).astype(F32)
            return (part[:half] + far).astype(BF16)

        weights = [w_up[:, piece] for piece in pieces]
        lead_pair = normed(lead[GAIN_ROWS:], row_sums(lead[GAIN_ROWS:]))
        leads = [project(lead_pair, weights[0])]
        lead_parts = [all_red(leads[0])]
        arrived = gelu_sum(lead_parts[0])

        rest = tokens[first:] + nothing(leads[-1]).astype(BF16)
        rest = lax.all_gather(rest, "wide", axis=1, tiled=True)
        sums = row_sums(rest)
        later_pair = [a + nothing(sums).astype(BF16) for a in lead_pair]
        leads.append(project(later_pair, weights[1]))
        lead_parts.append(all_red(leads[1]))
        rest_pair = normed(rest, sums, nothing(arrived))
        pair = [jnp.concatenate(p, axis=0) for p in zip(lead_pair, rest_pair)]
        arrived_other = swap(arrived)
        every = slice(0, qkv_rows.shape[1])
        near, far = project_rows(*pair, qkv_rows, every, [arrived_other, leads[1]])
        halves, before = [], [near]
        qkv = sum_rows([(near, swap(far))], slice(0, tokens.shape[0]))
        for piece in rest_pieces:
            near, far = project_rows(*rest_pair, w_up, piece, before)
            halves.append((near, swap(far)))
            before = [near]

        def output(have, other, piece, terms, cut, earlier=()):
            last = piece.stop == units
            attention = (attended[cut], attended_other[cut], attn_rows) if last else ()
            return project_hidden(have, other, w_down, piece, terms, attention, last, earlier)

        def chunk_sums(pairs, c, earlier):
            part = slice(cuts[c].start - first, cuts[c].stop - first)
            return sum_rows(pairs, part, [earlier])

        def scatter(kept, got, earlier):
            full = side_by_side(kept, got, core, earlier)
            return full, lax.psum_scatter(full, "wide", scatter_dimension=1, tiled=True)

        terms = output(arrived, arrived_other, pieces[0], (), cuts[0], [halves[-1][0]])
        earlier = [terms[0], halves[-1][1]]
        attended = attend(all_red(qkv), q_gain, k_gain, earlier)
        attended_other = swap(attended)
        second = gelu_sum(lead_parts[1], [attended])
        sums = chunk_sums(halves, 1, second)
        parts = all_red(sums)
        coming = chunk_sums(halves, 2, sums)
        terms = output(second, swap(second), pieces[1], terms, cuts[0], [coming])
        coming = all_red(coming)
        full, got = scatter(terms[0], swap(terms[1]), [])
        scattered = [got]

        hidden = gelu_sum(parts, [full])
        terms = output(hidden, swap(hidden), slice(0, units), (), cuts[1])
        full, got = scatter(terms[0], swap(terms[1]), [scattered[0]])
        scattered.append(got)

        hidden = gelu_sum(coming, [full])
        kept, sent = output(hidden, swap(hidden), slice(0, units), (), cuts[2])
        outs = [tokens[cut].astype(F32) + got.astype(F32) for cut, got in zip(cuts, scattered)]
        outs.append(tokens[cuts[2]].astype(F32) + collect(kept, swap(sent), width))
        return jnp.concatenate(outs, axis=0)

    return body


def solution(mesh):
    return jax.shard_map(
        make_body(mesh),
        mesh=mesh,
        in_specs=(
            P(("grp", "tok"), ("red", "wide")),
            P(("red", "wide")),
            P("wide", None),
            P("wide", None),
            P(("red", "tok"), "wide", None),
            P(("red", "tok"), "wide"),
            P("wide", None, ("red", "tok")),
            P("wide", ("red", "tok")),
        ),
        out_specs=P(("grp", "tok"), ("red", "wide")),
        check_vma=False,
    )
```

```python
import functools
import math

import jax
import jax.numpy as jnp
from jax import lax
from jax.experimental import pallas as pl
from jax.experimental.pallas import tpu as pltpu
from jax.sharding import PartitionSpec as P

D = 6144
PATCHES = 256
EPS = 1e-06
SHARES = (8, 5, 3)
LEAD_PIECES = (1, 1)
REST_PIECES = (2, 1)
AHEAD = 6
GAIN_ROWS = 8
BF16, F32 = jnp.bfloat16, jnp.float32
PARAMS = pltpu.CompilerParams(vmem_limit_bytes=48 * 2**20)
SMALL = pltpu.CompilerParams(vmem_limit_bytes=8 * 2**20)
MIDDLE = pltpu.CompilerParams(vmem_limit_bytes=16 * 2**20)
SOON = pl.CostEstimate(flops=0, bytes_accessed=0, transcendentals=0)


def normalize(values, mean, meansq, gain):
    return (values - mean) * lax.rsqrt(meansq - mean * mean + EPS) * gain.astype(F32)


def head_norm(values, gain):
    mean = jnp.mean(values, axis=-1, keepdims=True)
    meansq = jnp.mean(values * values, axis=-1, keepdims=True)
    return normalize(values, mean, meansq, gain)


def nothing(x):
    corner = x[(0,) * x.ndim].astype(jnp.int32)
    return lax.shift_right_logical(corner & 1, 1).astype(F32)


def slices(size, shares, grain):
    ends = [sum(shares[: i + 1]) * size // sum(shares) for i in range(len(shares))]
    ends = [end // grain * grain for end in ends]
    return [slice(a, b) for a, b in zip([0] + ends[:-1], ends)]


def steps_of(piece, blocks=(512, 384, 256, 128)):
    size = math.gcd(piece.stop - piece.start, piece.start)
    block = next(b for b in blocks if size % b == 0)
    return block, (piece.stop - piece.start) // block, piece.start // block


def corner_of(x):
    shape = (min(16, x.shape[0]), min(128, x.shape[1]))
    return pl.BlockSpec(shape, lambda *_: (0, 0))


def call(kernel, earlier, operands, specs, params=None, **options):
    def body(*refs):
        n = len(operands)
        kernel(refs[:n], refs[n + len(earlier) :])

    return pl.pallas_call(
        body,
        in_specs=list(specs) + [corner_of(a) for a in earlier],
        compiler_params=params or PARAMS,
        cost_estimate=SOON,
        **options,
    )(*operands, *earlier)


def gelu_sum(parts, earlier=()):
    rows, units = parts[0].shape
    block, steps, _ = steps_of(slice(0, units), (1024, 768, 512, 384, 256, 128))
    spec = pl.BlockSpec((rows, block), lambda j: (0, j))

    def kernel(ins, outs):
        up = ins[0][...].astype(F32)
        for part in ins[1:]:
            up = up + part[...].astype(F32)
        outs[0][...] = (0.5 * up * (1.0 + lax.erf(up * 0.5**0.5))).astype(BF16)

    return call(
        kernel,
        earlier,
        parts,
        [spec] * len(parts),
        params=SMALL,
        grid=(steps,),
        out_specs=spec,
        out_shape=jax.ShapeDtypeStruct((rows, units), BF16),
    )


def sum_rows(pairs, cut, earlier=()):
    widths = [near.shape[1] for near, _ in pairs]
    shape = (cut.stop - cut.start, sum(widths))

    def kernel(ins, outs):
        start = 0
        for at, width in enumerate(widths):
            total = ins[2 * at][cut].astype(F32) + ins[2 * at + 1][cut].astype(F32)
            outs[0][:, start : start + width] = total.astype(BF16)
            start += width

    operands = [part for pair in pairs for part in pair]
    return call(
        kernel,
        earlier,
        operands,
        [pl.BlockSpec(part.shape, lambda *_: (0, 0)) for part in operands],
        params=MIDDLE,
        grid=(1,),
        out_specs=pl.BlockSpec(shape, lambda *_: (0, 0)),
        out_shape=jax.ShapeDtypeStruct(shape, BF16),
    )


def side_by_side(kept, got, core, earlier=()):
    rows, columns = kept.shape
    spec = pl.BlockSpec(kept.shape, lambda *_: (0, 0))

    def kernel(ins, outs):
        first = ins[2][0] == 0
        outs[0][:, :columns] = jnp.where(first, ins[0][...], ins[1][...])
        outs[0][:, columns:] = jnp.where(first, ins[1][...], ins[0][...])

    return call(
        kernel,
        earlier,
        (kept, got, core.reshape(1)),
        [spec, spec, pl.BlockSpec(memory_space=pltpu.SMEM)],
        params=SMALL,
        grid=(1,),
        out_specs=pl.BlockSpec((rows, 2 * columns), lambda *_: (0, 0)),
        out_shape=jax.ShapeDtypeStruct((rows, 2 * columns), kept.dtype),
    )


def attend(parts, q_gain, k_gain, earlier=()):
    rows, width = parts[0].shape[0], q_gain.shape[1]
    n = len(parts)

    def kernel(ins, outs):
        def columns(at):
            here = slice(at * width, (at + 1) * width)
            return sum(part[:, here].astype(F32) for part in ins[:n])

        query = head_norm(columns(0), ins[n][...]).astype(BF16)
        key = head_norm(columns(1), ins[n + 1][...]).astype(BF16)
        value = columns(2).astype(BF16).astype(F32)
        for at in range(0, rows, PATCHES):
            image = slice(at, at + PATCHES)
            scores = lax.dot_general(
                query[image], key[image], (((1,), (1,)), ((), ())), preferred_element_type=F32
            )
            scores = scores * width ** (-0.5)
            weights = jnp.exp(scores - jnp.max(scores, axis=-1, keepdims=True))
            total = jnp.sum(weights, axis=-1, keepdims=True)
            acc = jnp.dot(
                weights,
                value[image],
                precision=lax.Precision.HIGHEST,
                preferred_element_type=F32,
            )
            outs[0][image] = (acc / total).astype(BF16)

    whole = [pl.BlockSpec(a.shape, lambda *_: (0, 0)) for a in (*parts, q_gain, k_gain)]
    return call(
        kernel,
        earlier,
        (*parts, q_gain, k_gain),
        whole,
        params=SMALL,
        grid=(1,),
        out_specs=pl.BlockSpec((rows, width), lambda *_: (0, 0)),
        out_shape=jax.ShapeDtypeStruct((rows, width), BF16),
    )


def project_rows(own, other, weight, piece, earlier=()):
    rows, depth = own.shape
    columns = piece.stop - piece.start
    block, steps, _ = steps_of(piece)
    whole = pl.BlockSpec((rows, depth), lambda *_: (0, 0))
    out = pl.BlockSpec((rows, columns), lambda *_: (0, 0))

    def kernel(ins, refs):
        near, far, both, landed, sems = refs

        def bring(at):
            start = pl.multiple_of(piece.start + at * block, block)
            source = ins[2].at[:, pl.ds(start, block)]
            return pltpu.make_async_copy(source, landed.at[at], sems.at[at])

        for at in range(min(AHEAD, steps)):
            bring(at).start()
        both[:rows] = ins[0][...]
        both[rows:] = ins[1][...]

        @pl.loop(0, steps)
        def _(at):
            bring(at).wait()

            @pl.when(at + AHEAD < steps)
            def _():
                bring(at + AHEAD).start()

            part = jnp.dot(both[...], landed[at], preferred_element_type=F32).astype(BF16)
            here = pl.ds(pl.multiple_of(at * block, block), block)
            near[:, here] = part[:rows]
            far[:, here] = part[rows:]

    return call(
        kernel,
        earlier,
        (own, other, weight),
        [whole, whole, pl.BlockSpec(memory_space=pltpu.HBM)],
        grid=(1,),
        out_specs=[out] * 2,
        out_shape=[jax.ShapeDtypeStruct((rows, columns), BF16)] * 2,
        scratch_shapes=[
            pltpu.VMEM((2 * rows, depth), BF16),
            pltpu.VMEM((steps, depth, block), BF16),
            pltpu.SemaphoreType.DMA((steps,)),
        ],
    )


def project_hidden(own, other, weight, piece, added, attention, last, earlier=()):
    rows, units = own.shape
    columns = weight.shape[1]
    block, steps, _ = steps_of(piece)
    whole = pl.BlockSpec((rows, columns), lambda *_: (0, 0))
    part = pl.BlockSpec((rows, units), lambda *_: (0, 0))
    specs = [part, part, pl.BlockSpec(memory_space=pltpu.HBM)]
    specs += [whole] * len(added)
    specs += [pl.BlockSpec(a.shape, lambda *_: (0, 0)) for a in attention]

    def kernel(ins, refs):
        outs, (both, total, landed, sems) = refs[:2], refs[2:]

        def bring(at):
            start = pl.multiple_of(piece.start + at * block, block)
            source = ins[2].at[pl.ds(start, block), :]
            return pltpu.make_async_copy(source, landed.at[at], sems.at[at])

        for at in range(min(AHEAD, steps)):
            bring(at).start()
        halves = (slice(0, rows), slice(rows, 2 * rows))
        for at, half in enumerate(halves):
            both[half] = ins[at][...]
            first = jnp.zeros((rows, columns), F32)
            if added:
                first = ins[3 + at][...]
            if attention:
                first = first + jnp.dot(
                    ins[-3 + at][...], ins[-1][...], preferred_element_type=F32
                )
            total[half] = first

        @pl.loop(0, steps)
        def _(at):
            bring(at).wait()

            @pl.when(at + AHEAD < steps)
            def _():
                bring(at + AHEAD).start()

            here = pl.ds(pl.multiple_of(at * block, block), block)
            total[...] += jnp.dot(both[:, here], landed[at], preferred_element_type=F32)

        for out, half in zip(outs, halves):
            out[...] = total[half].astype(out.dtype)

    return call(
        kernel,
        earlier,
        (own, other, weight, *added, *attention),
        specs,
        grid=(1,),
        out_specs=[whole] * 2,
        out_shape=[jax.ShapeDtypeStruct((rows, columns), BF16 if last else F32)] * 2,
        scratch_shapes=[
            pltpu.VMEM((2 * rows, units), BF16),
            pltpu.VMEM((2 * rows, columns), F32),
            pltpu.VMEM((steps, block, columns), BF16),
            pltpu.SemaphoreType.DMA((steps,)),
        ],
    )


def make_body(mesh):
    n_red, n_wide = mesh.shape["red"], mesh.shape["wide"]
    half_wide = n_wide // 2

    def swap(x):
        return lax.ppermute(x, "tok", [(0, 1), (1, 0)])

    def all_red(x):
        parts = [x]
        for shift in range(1, n_red):
            pairs = [(i, (i + shift) % n_red) for i in range(n_red)]
            parts.append(lax.ppermute(x, "red", pairs))
        return parts

    def sum_red(x):
        return sum(a.astype(F32) for a in all_red(x))

    def collect(kept, got, width):
        core, chip = lax.axis_index("tok"), lax.axis_index("wide")
        terms = jnp.concatenate([kept, got], axis=1)

        def block(at):
            start = ((at // half_wide) ^ core) * half_wide + at % half_wide
            return lax.dynamic_slice_in_dim(terms, start * width, width, axis=1)

        total = block(chip).astype(F32)
        for k in range(n_wide - 1, 0, -1):
            pairs = [(i, i ^ k) for i in range(n_wide)]
            total = total + lax.ppermute(block(chip ^ k), "wide", pairs).astype(F32)
        return total

    def body(tokens, ln_gain, q_gain, k_gain, w_qkv, w_up, w_attn, w_down):
        core = lax.axis_index("tok")
        width = tokens.shape[1]
        qkv_rows = w_qkv.reshape(w_qkv.shape[0], w_qkv.shape[1] * w_qkv.shape[2])
        attn_rows = w_attn.reshape(w_attn.shape[0] * w_attn.shape[1], w_attn.shape[2])
        depth, units = w_up.shape
        cuts = slices(tokens.shape[0], SHARES, 16)
        pieces = slices(units, LEAD_PIECES, 128)
        rest_pieces = slices(units, REST_PIECES, 128)

        first = cuts[0].stop
        gain_rows = jnp.broadcast_to(ln_gain[None], (GAIN_ROWS, width))
        lead = jnp.concatenate([gain_rows, tokens[:first]], axis=0)
        lead = lax.all_gather(lead, "wide", axis=1, tiled=True)
        gain = lead[:1]

        def row_sums(raw):
            floats = raw.astype(F32)
            return jnp.stack([jnp.sum(floats, axis=1), jnp.sum(floats * floats, axis=1)])

        def normed(raw, sums, start=0.0):
            sums = sum_red(sums)[:, :, None] / D + start
            values = normalize(raw.astype(F32), sums[0], sums[1], gain).astype(BF16)
            mine = lax.dynamic_slice_in_dim(values, core * depth, depth, axis=1)
            theirs = lax.dynamic_slice_in_dim(values, (1 - core) * depth, depth, axis=1)
            return mine, swap(theirs)

        def project(pair, weight):
            both = jnp.concatenate(pair, axis=0)
            half = both.shape[0] // 2
            part = jnp.dot(both, weight, preferred_element_type=F32)
            far = swap(part[half:].astype(BF16)).astype(F32)
            return (part[:half] + far).astype(BF16)

        weights = [w_up[:, piece] for piece in pieces]
        lead_pair = normed(lead[GAIN_ROWS:], row_sums(lead[GAIN_ROWS:]))
        leads = [project(lead_pair, weights[0])]
        lead_parts = [all_red(leads[0])]
        arrived = gelu_sum(lead_parts[0])

        rest = tokens[first:] + nothing(leads[-1]).astype(BF16)
        rest = lax.all_gather(rest, "wide", axis=1, tiled=True)
        sums = row_sums(rest)
        later_pair = [a + nothing(sums).astype(BF16) for a in lead_pair]
        leads.append(project(later_pair, weights[1]))
        lead_parts.append(all_red(leads[1]))
        rest_pair = normed(rest, sums, nothing(arrived))
        pair = [jnp.concatenate(p, axis=0) for p in zip(lead_pair, rest_pair)]
        arrived_other = swap(arrived)
        every = slice(0, qkv_rows.shape[1])
        near, far = project_rows(*pair, qkv_rows, every, [arrived_other, leads[1]])
        halves, before = [], [near]
        qkv = sum_rows([(near, swap(far))], slice(0, tokens.shape[0]))
        for piece in rest_pieces:
            near, far = project_rows(*rest_pair, w_up, piece, before)
            halves.append((near, swap(far)))
            before = [near]

        def output(have, other, piece, terms, cut, earlier=()):
            last = piece.stop == units
            attention = (attended[cut], attended_other[cut], attn_rows) if last else ()
            return project_hidden(have, other, w_down, piece, terms, attention, last, earlier)

        def chunk_sums(pairs, c, earlier):
            part = slice(cuts[c].start - first, cuts[c].stop - first)
            return sum_rows(pairs, part, [earlier])

        def scatter(kept, got, earlier):
            full = side_by_side(kept, got, core, earlier)
            return full, lax.psum_scatter(full, "wide", scatter_dimension=1, tiled=True)

        terms = output(arrived, arrived_other, pieces[0], (), cuts[0], [halves[-1][0]])
        earlier = [terms[0], halves[-1][1]]
        attended = attend(all_red(qkv), q_gain, k_gain, earlier)
        attended_other = swap(attended)
        second = gelu_sum(lead_parts[1], [attended])
        sums = chunk_sums(halves, 1, second)
        parts = all_red(sums)
        coming = chunk_sums(halves, 2, sums)
        terms = output(second, swap(second), pieces[1], terms, cuts[0], [coming])
        coming = all_red(coming)
        full, got = scatter(terms[0], swap(terms[1]), [])
        scattered = [got]

        hidden = gelu_sum(parts, [full])
        terms = output(hidden, swap(hidden), slice(0, units), (), cuts[1])
        full, got = scatter(terms[0], swap(terms[1]), [scattered[0]])
        scattered.append(got)

        hidden = gelu_sum(coming, [full])
        kept, sent = output(hidden, swap(hidden), slice(0, units), (), cuts[2])
        outs = [tokens[cut].astype(F32) + got.astype(F32) for cut, got in zip(cuts, scattered)]
        outs.append(tokens[cuts[2]].astype(F32) + collect(kept, swap(sent), width))
        return jnp.concatenate(outs, axis=0)

    return body


def solution(mesh):
    return jax.shard_map(
        make_body(mesh),
        mesh=mesh,
        in_specs=(
            P(("grp", "tok"), ("red", "wide")),
            P(("red", "wide")),
            P("wide", None),
            P("wide", None),
            P(("red", "tok"), "wide", None),
            P(("red", "tok"), "wide"),
            P("wide", None, ("red", "tok")),
            P("wide", ("red", "tok")),
        ),
        out_specs=P(("grp", "tok"), ("red", "wide")),
        check_vma=False,
    )
```

```python
import functools
import math

import jax
import jax.numpy as jnp
from jax import lax
from jax.experimental import pallas as pl
from jax.experimental.pallas import tpu as pltpu
from jax.sharding import PartitionSpec as P

D = 6144
PATCHES = 256
EPS = 1e-06
SHARES = (8, 5, 3)
LEAD_PIECES = (1, 1)
REST_PIECES = (2, 1)
AHEAD = 6
GAIN_ROWS = 8
BF16, F32 = jnp.bfloat16, jnp.float32
PARAMS = pltpu.CompilerParams(vmem_limit_bytes=48 * 2**20)
SMALL = pltpu.CompilerParams(vmem_limit_bytes=8 * 2**20)
MIDDLE = pltpu.CompilerParams(vmem_limit_bytes=16 * 2**20)
SOON = pl.CostEstimate(flops=0, bytes_accessed=0, transcendentals=0)


def normalize(values, mean, meansq, gain):
    return (values - mean) * lax.rsqrt(meansq - mean * mean + EPS) * gain.astype(F32)


def head_norm(values, gain):
    mean = jnp.mean(values, axis=-1, keepdims=True)
    meansq = jnp.mean(values * values, axis=-1, keepdims=True)
    return normalize(values, mean, meansq, gain)


def nothing(x):
    corner = x[(0,) * x.ndim].astype(jnp.int32)
    return lax.shift_right_logical(corner & 1, 1).astype(F32)


def slices(size, shares, grain):
    ends = [sum(shares[: i + 1]) * size // sum(shares) for i in range(len(shares))]
    ends = [end // grain * grain for end in ends]
    return [slice(a, b) for a, b in zip([0] + ends[:-1], ends)]


def steps_of(piece):
    size = math.gcd(piece.stop - piece.start, piece.start)
    block = next(b for b in (512, 384, 256, 128) if size % b == 0)
    return block, (piece.stop - piece.start) // block, piece.start // block


def corner_of(x):
    shape = (min(16, x.shape[0]), min(128, x.shape[1]))
    return pl.BlockSpec(shape, lambda *_: (0, 0))


def call(kernel, earlier, operands, specs, params=None, **options):
    def body(*refs):
        n = len(operands)
        kernel(refs[:n], refs[n + len(earlier) :])

    return pl.pallas_call(
        body,
        in_specs=list(specs) + [corner_of(a) for a in earlier],
        compiler_params=params or PARAMS,
        cost_estimate=SOON,
        **options,
    )(*operands, *earlier)


def gelu_sum(parts, earlier=()):
    rows, units = parts[0].shape
    block, steps, _ = steps_of(slice(0, units))
    spec = pl.BlockSpec((rows, block), lambda j: (0, j))

    def kernel(ins, outs):
        up = ins[0][...].astype(F32)
        for part in ins[1:]:
            up = up + part[...].astype(F32)
        outs[0][...] = (0.5 * up * (1.0 + lax.erf(up * 0.5**0.5))).astype(BF16)

    return call(
        kernel,
        earlier,
        parts,
        [spec] * len(parts),
        params=SMALL,
        grid=(steps,),
        out_specs=spec,
        out_shape=jax.ShapeDtypeStruct((rows, units), BF16),
    )


def sum_rows(pairs, cut, earlier=()):
    widths = [near.shape[1] for near, _ in pairs]
    shape = (cut.stop - cut.start, sum(widths))

    def kernel(ins, outs):
        start = 0
        for at, width in enumerate(widths):
            total = ins[2 * at][cut].astype(F32) + ins[2 * at + 1][cut].astype(F32)
            outs[0][:, start : start + width] = total.astype(BF16)
            start += width

    operands = [part for pair in pairs for part in pair]
    return call(
        kernel,
        earlier,
        operands,
        [pl.BlockSpec(part.shape, lambda *_: (0, 0)) for part in operands],
        params=MIDDLE,
        grid=(1,),
        out_specs=pl.BlockSpec(shape, lambda *_: (0, 0)),
        out_shape=jax.ShapeDtypeStruct(shape, BF16),
    )


def side_by_side(kept, got, core, earlier=()):
    rows, columns = kept.shape
    spec = pl.BlockSpec(kept.shape, lambda *_: (0, 0))

    def kernel(ins, outs):
        first = ins[2][0] == 0
        outs[0][:, :columns] = jnp.where(first, ins[0][...], ins[1][...])
        outs[0][:, columns:] = jnp.where(first, ins[1][...], ins[0][...])

    return call(
        kernel,
        earlier,
        (kept, got, core.reshape(1)),
        [spec, spec, pl.BlockSpec(memory_space=pltpu.SMEM)],
        params=SMALL,
        grid=(1,),
        out_specs=pl.BlockSpec((rows, 2 * columns), lambda *_: (0, 0)),
        out_shape=jax.ShapeDtypeStruct((rows, 2 * columns), kept.dtype),
    )


def attend(parts, q_gain, k_gain, earlier=()):
    rows, width = parts[0].shape[0], q_gain.shape[1]
    n = len(parts)

    def kernel(ins, outs):
        def columns(at):
            here = slice(at * width, (at + 1) * width)
            return sum(part[:, here].astype(F32) for part in ins[:n])

        query = head_norm(columns(0), ins[n][...]).astype(BF16)
        key = head_norm(columns(1), ins[n + 1][...]).astype(BF16)
        value = columns(2).astype(BF16).astype(F32)
        for at in range(0, rows, PATCHES):
            image = slice(at, at + PATCHES)
            scores = lax.dot_general(
                query[image], key[image], (((1,), (1,)), ((), ())), preferred_element_type=F32
            )
            scores = scores * width ** (-0.5)
            weights = jnp.exp(scores - jnp.max(scores, axis=-1, keepdims=True))
            total = jnp.sum(weights, axis=-1, keepdims=True)
            acc = jnp.dot(
                weights,
                value[image],
                precision=lax.Precision.HIGHEST,
                preferred_element_type=F32,
            )
            outs[0][image] = (acc / total).astype(BF16)

    whole = [pl.BlockSpec(a.shape, lambda *_: (0, 0)) for a in (*parts, q_gain, k_gain)]
    return call(
        kernel,
        earlier,
        (*parts, q_gain, k_gain),
        whole,
        params=SMALL,
        grid=(1,),
        out_specs=pl.BlockSpec((rows, width), lambda *_: (0, 0)),
        out_shape=jax.ShapeDtypeStruct((rows, width), BF16),
    )


def project_rows(own, other, weight, piece, earlier=()):
    rows, depth = own.shape
    columns = piece.stop - piece.start
    block, steps, _ = steps_of(piece)
    whole = pl.BlockSpec((rows, depth), lambda *_: (0, 0))
    out = pl.BlockSpec((rows, columns), lambda *_: (0, 0))

    def kernel(ins, refs):
        near, far, both, landed, sems = refs

        def bring(at):
            start = pl.multiple_of(piece.start + at * block, block)
            source = ins[2].at[:, pl.ds(start, block)]
            return pltpu.make_async_copy(source, landed.at[at], sems.at[at])

        for at in range(min(AHEAD, steps)):
            bring(at).start()
        both[:rows] = ins[0][...]
        both[rows:] = ins[1][...]

        @pl.loop(0, steps)
        def _(at):
            bring(at).wait()

            @pl.when(at + AHEAD < steps)
            def _():
                bring(at + AHEAD).start()

            part = jnp.dot(both[...], landed[at], preferred_element_type=F32).astype(BF16)
            here = pl.ds(pl.multiple_of(at * block, block), block)
            near[:, here] = part[:rows]
            far[:, here] = part[rows:]

    return call(
        kernel,
        earlier,
        (own, other, weight),
        [whole, whole, pl.BlockSpec(memory_space=pltpu.HBM)],
        grid=(1,),
        out_specs=[out] * 2,
        out_shape=[jax.ShapeDtypeStruct((rows, columns), BF16)] * 2,
        scratch_shapes=[
            pltpu.VMEM((2 * rows, depth), BF16),
            pltpu.VMEM((steps, depth, block), BF16),
            pltpu.SemaphoreType.DMA((steps,)),
        ],
    )


def project_hidden(own, other, weight, piece, added, attention, last, earlier=()):
    rows, units = own.shape
    columns = weight.shape[1]
    block, steps, _ = steps_of(piece)
    whole = pl.BlockSpec((rows, columns), lambda *_: (0, 0))
    part = pl.BlockSpec((rows, units), lambda *_: (0, 0))
    specs = [part, part, pl.BlockSpec(memory_space=pltpu.HBM)]
    specs += [whole] * len(added)
    specs += [pl.BlockSpec(a.shape, lambda *_: (0, 0)) for a in attention]

    def kernel(ins, refs):
        outs, (both, total, landed, sems) = refs[:2], refs[2:]

        def bring(at):
            start = pl.multiple_of(piece.start + at * block, block)
            source = ins[2].at[pl.ds(start, block), :]
            return pltpu.make_async_copy(source, landed.at[at], sems.at[at])

        for at in range(min(AHEAD, steps)):
            bring(at).start()
        halves = (slice(0, rows), slice(rows, 2 * rows))
        for at, half in enumerate(halves):
            both[half] = ins[at][...]
            first = jnp.zeros((rows, columns), F32)
            if added:
                first = ins[3 + at][...]
            if attention:
                first = first + jnp.dot(
                    ins[-3 + at][...], ins[-1][...], preferred_element_type=F32
                )
            total[half] = first

        @pl.loop(0, steps)
        def _(at):
            bring(at).wait()

            @pl.when(at + AHEAD < steps)
            def _():
                bring(at + AHEAD).start()

            here = pl.ds(pl.multiple_of(at * block, block), block)
            total[...] += jnp.dot(both[:, here], landed[at], preferred_element_type=F32)

        for out, half in zip(outs, halves):
            out[...] = total[half].astype(out.dtype)

    return call(
        kernel,
        earlier,
        (own, other, weight, *added, *attention),
        specs,
        grid=(1,),
        out_specs=[whole] * 2,
        out_shape=[jax.ShapeDtypeStruct((rows, columns), BF16 if last else F32)] * 2,
        scratch_shapes=[
            pltpu.VMEM((2 * rows, units), BF16),
            pltpu.VMEM((2 * rows, columns), F32),
            pltpu.VMEM((steps, block, columns), BF16),
            pltpu.SemaphoreType.DMA((steps,)),
        ],
    )


def make_body(mesh):
    n_red, n_wide = mesh.shape["red"], mesh.shape["wide"]
    half_wide = n_wide // 2

    def swap(x):
        return lax.ppermute(x, "tok", [(0, 1), (1, 0)])

    def all_red(x):
        parts = [x]
        for shift in range(1, n_red):
            pairs = [(i, (i + shift) % n_red) for i in range(n_red)]
            parts.append(lax.ppermute(x, "red", pairs))
        return parts

    def sum_red(x):
        return sum(a.astype(F32) for a in all_red(x))

    def collect(kept, got, width):
        core, chip = lax.axis_index("tok"), lax.axis_index("wide")
        terms = jnp.concatenate([kept, got], axis=1)

        def block(at):
            start = ((at // half_wide) ^ core) * half_wide + at % half_wide
            return lax.dynamic_slice_in_dim(terms, start * width, width, axis=1)

        total = block(chip).astype(F32)
        for k in range(n_wide - 1, 0, -1):
            pairs = [(i, i ^ k) for i in range(n_wide)]
            total = total + lax.ppermute(block(chip ^ k), "wide", pairs).astype(F32)
        return total

    def body(tokens, ln_gain, q_gain, k_gain, w_qkv, w_up, w_attn, w_down):
        core = lax.axis_index("tok")
        width = tokens.shape[1]
        qkv_rows = w_qkv.reshape(w_qkv.shape[0], w_qkv.shape[1] * w_qkv.shape[2])
        attn_rows = w_attn.reshape(w_attn.shape[0] * w_attn.shape[1], w_attn.shape[2])
        depth, units = w_up.shape
        cuts = slices(tokens.shape[0], SHARES, 16)
        pieces = slices(units, LEAD_PIECES, 128)
        rest_pieces = slices(units, REST_PIECES, 128)

        first = cuts[0].stop
        gain_rows = jnp.broadcast_to(ln_gain[None], (GAIN_ROWS, width))
        lead = jnp.concatenate([gain_rows, tokens[:first]], axis=0)
        lead = lax.all_gather(lead, "wide", axis=1, tiled=True)
        gain = lead[:1]

        def row_sums(raw):
            floats = raw.astype(F32)
            return jnp.stack([jnp.sum(floats, axis=1), jnp.sum(floats * floats, axis=1)])

        def normed(raw, sums, start=0.0):
            sums = sum_red(sums)[:, :, None] / D + start
            values = normalize(raw.astype(F32), sums[0], sums[1], gain).astype(BF16)
            mine = lax.dynamic_slice_in_dim(values, core * depth, depth, axis=1)
            theirs = lax.dynamic_slice_in_dim(values, (1 - core) * depth, depth, axis=1)
            return mine, swap(theirs)

        def project(pair, weight):
            both = jnp.concatenate(pair, axis=0)
            half = both.shape[0] // 2
            part = jnp.dot(both, weight, preferred_element_type=F32)
            far = swap(part[half:].astype(BF16)).astype(F32)
            return (part[:half] + far).astype(BF16)

        weights = [w_up[:, piece] for piece in pieces]
        lead_pair = normed(lead[GAIN_ROWS:], row_sums(lead[GAIN_ROWS:]))
        leads = [project(lead_pair, weights[0])]
        lead_parts = [all_red(leads[0])]
        arrived = gelu_sum(lead_parts[0])

        rest = tokens[first:] + nothing(leads[-1]).astype(BF16)
        rest = lax.all_gather(rest, "wide", axis=1, tiled=True)
        sums = row_sums(rest)
        later_pair = [a + nothing(sums).astype(BF16) for a in lead_pair]
        leads.append(project(later_pair, weights[1]))
        lead_parts.append(all_red(leads[1]))
        rest_pair = normed(rest, sums, nothing(arrived))
        pair = [jnp.concatenate(p, axis=0) for p in zip(lead_pair, rest_pair)]
        arrived_other = swap(arrived)
        every = slice(0, qkv_rows.shape[1])
        near, far = project_rows(*pair, qkv_rows, every, [arrived_other, leads[1]])
        halves, before = [], [near]
        qkv = sum_rows([(near, swap(far))], slice(0, tokens.shape[0]))
        for piece in rest_pieces:
            near, far = project_rows(*rest_pair, w_up, piece, before)
            halves.append((near, swap(far)))
            before = [near]

        def output(have, other, piece, terms, cut, earlier=()):
            last = piece.stop == units
            attention = (attended[cut], attended_other[cut], attn_rows) if last else ()
            return project_hidden(have, other, w_down, piece, terms, attention, last, earlier)

        def chunk_sums(pairs, c, earlier):
            part = slice(cuts[c].start - first, cuts[c].stop - first)
            return sum_rows(pairs, part, [earlier])

        def scatter(kept, got, earlier):
            full = side_by_side(kept, got, core, earlier)
            return full, lax.psum_scatter(full, "wide", scatter_dimension=1, tiled=True)

        terms = output(arrived, arrived_other, pieces[0], (), cuts[0], [halves[-1][0]])
        earlier = [terms[0], halves[-1][1]]
        attended = attend(all_red(qkv), q_gain, k_gain, earlier)
        attended_other = swap(attended)
        second = gelu_sum(lead_parts[1], [attended])
        sums = chunk_sums(halves, 1, second)
        parts = all_red(sums)
        coming = chunk_sums(halves, 2, sums)
        terms = output(second, swap(second), pieces[1], terms, cuts[0], [coming])
        coming = all_red(coming)
        full, got = scatter(terms[0], swap(terms[1]), [])
        scattered = [got]

        hidden = gelu_sum(parts, [full])
        terms = output(hidden, swap(hidden), slice(0, units), (), cuts[1])
        full, got = scatter(terms[0], swap(terms[1]), [])
        scattered.append(got)

        hidden = gelu_sum(coming, [full, scattered[0]])
        kept, sent = output(hidden, swap(hidden), slice(0, units), (), cuts[2])
        outs = [tokens[cut].astype(F32) + got.astype(F32) for cut, got in zip(cuts, scattered)]
        outs.append(tokens[cuts[2]].astype(F32) + collect(kept, swap(sent), width))
        return jnp.concatenate(outs, axis=0)

    return body


def solution(mesh):
    return jax.shard_map(
        make_body(mesh),
        mesh=mesh,
        in_specs=(
            P(("grp", "tok"), ("red", "wide")),
            P(("red", "wide")),
            P("wide", None),
            P("wide", None),
            P(("red", "tok"), "wide", None),
            P(("red", "tok"), "wide"),
            P("wide", None, ("red", "tok")),
            P("wide", ("red", "tok")),
        ),
        out_specs=P(("grp", "tok"), ("red", "wide")),
        check_vma=False,
    )
```
